512 devices in a mesh: lat: 16 (over x_lo, y), lon: 32 (over x_hi, z, core).
Axes of the slice: x: 4 (x_hi: 2, x_lo: 2; x = x_hi * 2 + x_lo), y: 8, z: 8, core: 2. Of those that a mesh axis runs over, the one named last changes fastest.
Arguments:
- latent: bfloat16 [4, 96, 384, 512], P(None, 'lat', 'lon'), may hold values from -21 to 21
- qkv_weight: bfloat16 [512, 1536], P('lon'), may hold values from -0.25 to 0.25
- proj_weight: bfloat16 [512, 512], P('lon'), may hold values from -0.25 to 0.25
- position_bias: bfloat16 [16, 288, 288], replicated, may hold values from -4 to 4
- attn_gain: float32 [512], replicated, may hold values from 0.1 to 1.9
- up_weight: bfloat16 [2048, 512], P('lon'), may hold values from -0.25 to 0.25
- down_weight: bfloat16 [2048, 512], P('lon'), may hold values from -0.125 to 0.125
- mlp_gain: float32 [512], replicated, may hold values from 0.1 to 1.9
Outputs:
- block_out: bfloat16 [4, 96, 384, 512], P(None, 'lat', 'lon')
The draws below stay inside these ranges and needn't reach their ends.
All inputs are finite; a program needn't handle non-finite values.
Results may differ from the reference program's by a relative error of at most 0.0072.
Values may be sent and summed in bfloat16 or wider, within the bound.
No kernel may reach another device: no remote copies, remote signals or barrier semaphores. Data moves between devices by JAX's collectives and lax.ppermute only.
A program may use at most 64 MiB of HBM per device.

```python
import math
import jax
import jax.numpy as jnp
from jax import lax

D = 512
FF = 2048
LEV = 4
WLAT = 6
WLON = 12
HEADS = 16
WN = 288
NLAT = 96
NLON = 384


def draw_latent(key, part):
    key = jax.random.fold_in(key, 7)
    unit_key, scale_key = jax.random.split(key)
    full_shape = (LEV, NLAT, NLON, D)
    unit_draw = jnp.clip(jax.random.normal(unit_key, full_shape, jnp.float32), -4.0, 4.0)
    spread = jax.random.uniform(scale_key, (LEV, NLAT, NLON, 1), jnp.float32, 0.0, math.log(3.0))
    return (unit_draw * jnp.exp(spread)).astype(jnp.bfloat16)


def shard_levels(key, shape, cuts, smallest, top_value):
    level = 1.0
    for axis_at, parts in cuts:
        heights = jax.random.uniform(jax.random.fold_in(jax.random.fold_in(key, 6), axis_at), (parts,), jnp.float32, smallest / len(cuts), top_value / len(cuts))
        level = level * jnp.repeat(jnp.exp(heights), shape[axis_at] // parts).reshape((-1,) + (1,) * (len(shape) - 1 - axis_at))
    return level


def scatter_about(own_key, dims, scale, most, cuts=(), kind=jnp.bfloat16):
    values = scale * jax.random.normal(own_key, dims, jnp.float32)
    if cuts:
        values = values * shard_levels(own_key, dims, cuts, -0.22, 0.18)
    return jnp.clip(values, -most, most).astype(kind)


def setup_inputs(seed: int = 0) -> dict:
    splits = jax.random.split(jax.random.key(seed), 9)
    latent = draw_latent(jax.random.fold_in(splits[8], 71), 0)
    qkv_weight = scatter_about(splits[1], (D, 3 * D), D ** -0.5, 0.25, ((0, 32),))
    proj_weight = scatter_about(splits[2], (D, D), D ** -0.5, 0.25, ((0, 32),))
    position_bias = scatter_about(splits[3], (HEADS, WN, WN), 1.0, 4.0)
    attn_gain = jnp.clip(1.0 + 0.18 * jax.random.normal(splits[4], (D,), jnp.float32), 0.1, 1.9)
    up_weight = scatter_about(splits[5], (FF, D), D ** -0.5, 0.25, ((0, 32),))
    down_weight = scatter_about(splits[6], (FF, D), FF ** -0.5, 0.125, ((0, 32),))
    mlp_gain = jnp.clip(1.0 + 0.18 * jax.random.normal(splits[7], (D,), jnp.float32), 0.1, 1.9)
    return {"latent": latent, "qkv_weight": qkv_weight, "proj_weight": proj_weight, "position_bias": position_bias, "attn_gain": attn_gain, "up_weight": up_weight, "down_weight": down_weight, "mlp_gain": mlp_gain}


epsilon = 1e-05

def layer_norm(values, gain):
    average = lax.optimization_barrier(jnp.mean(values, -1, keepdims=True))
    centered = values - average
    variance = lax.optimization_barrier(jnp.mean(centered * centered, -1, keepdims=True))
    return centered * lax.rsqrt(variance + epsilon) * gain

def attend(cells, labels, qkv_weight, position_bias):
    levels, lat_rows, lon_cols, features = cells.shape
    head_count = position_bias.shape[0]
    head_dim = features // head_count
    lat_bands = lat_rows // WLAT
    strips = lon_cols // WLON
    windows = lat_bands * strips
    window_len = levels * WLAT * WLON
    packed = jnp.dot(cells.reshape(-1, features), qkv_weight, preferred_element_type=jnp.float32).astype(jnp.bfloat16)
    packed = packed.reshape(levels, lat_bands, WLAT, strips, WLON, 3, head_count, head_dim)
    packed = packed.transpose(5, 1, 3, 6, 0, 2, 4, 7).reshape(3, windows, head_count, window_len, head_dim)
    queries = packed[0].astype(jnp.float32)
    key_rows = packed[1].astype(jnp.float32)
    values = packed[2].astype(jnp.float32)
    scores = jnp.einsum('wgqd,wgkd->wgqk', queries, key_rows) * head_dim ** (-0.5)
    scores = scores + position_bias.astype(jnp.float32)[None]
    region_tags = jnp.broadcast_to(labels.reshape(lat_bands, 1, 1, WLAT, 1), (lat_bands, strips, levels, WLAT, WLON)).reshape(windows, window_len)
    same_region = region_tags[:, :, None] == region_tags[:, None, :]
    scores = jnp.where(same_region[:, None], scores, -1e+30)
    row_max = lax.optimization_barrier(jnp.max(scores, -1, keepdims=True))
    weights = jnp.exp(scores - row_max)
    weights = (weights / lax.optimization_barrier(jnp.sum(weights, -1, keepdims=True))).astype(jnp.bfloat16)
    attn_out = jnp.einsum('wgqk,wgkd->wgqd', weights.astype(jnp.float32), values).astype(jnp.bfloat16)
    attn_out = attn_out.reshape(lat_bands, strips, head_count, levels, WLAT, WLON, head_dim).transpose(3, 0, 4, 1, 5, 2, 6)
    return attn_out.reshape(levels * lat_rows * lon_cols, features)

def reference(latent, qkv_weight, proj_weight, position_bias, attn_gain, up_weight, down_weight, mlp_gain):
    half_lat = WLAT // 2
    half_lon = WLON // 2
    rolled = jnp.roll(latent, (half_lat, half_lon), axis=(1, 2))
    band_count = NLAT // WLAT
    stripes = rolled.reshape(LEV, band_count, WLAT, NLON, D).transpose(1, 0, 2, 3, 4)

    def one_band(pair):
        stripe, band_index = pair
        labels = band_index * WLAT + jnp.arange(WLAT, dtype=jnp.int32) < half_lat
        attn_out = attend(stripe, labels, qkv_weight, position_bias)
        projected = jnp.dot(attn_out, proj_weight, preferred_element_type=jnp.float32)
        updated = stripe.reshape(-1, D).astype(jnp.float32) + layer_norm(projected, attn_gain)
        return updated.astype(jnp.bfloat16).reshape(stripe.shape)
    mixed = lax.map(one_band, (stripes, jnp.arange(band_count, dtype=jnp.int32)))
    mixed = mixed.transpose(1, 0, 2, 3, 4).reshape(LEV, NLAT, NLON, D)
    restored = jnp.roll(mixed, (-half_lat, -half_lon), axis=(1, 2))
    groups = restored.reshape(LEV * band_count, WLAT * NLON, D)

    def feed_forward(token_rows):
        raised = lax.dot_general(token_rows, up_weight, (((1,), (1,)), ((), ())), preferred_element_type=jnp.float32)
        hidden = jax.nn.gelu(raised, approximate=False).astype(jnp.bfloat16)
        lowered = jnp.dot(hidden, down_weight, preferred_element_type=jnp.float32)
        return (token_rows.astype(jnp.float32) + layer_norm(lowered, mlp_gain)).astype(jnp.bfloat16)
    block_out = lax.map(feed_forward, groups).reshape(LEV, NLAT, NLON, D)
    return block_out
```

```python
import jax
import jax.numpy as jnp
import numpy as np
from jax import lax
from jax.experimental import pallas as pl
from jax.experimental.pallas import tpu as pltpu
from jax.sharding import Mesh, PartitionSpec as P

WLAT = 6
WLON = 12
LEVELS = 4
HALF_LAT = WLAT // 2
HALF_LON = WLON // 2
QUARTER = LEVELS * HALF_LAT * HALF_LON
WN = 4 * QUARTER
D = 512
CORNER = (HALF_LAT, HALF_LON, LEVELS, D)
HEADS = 16
HEAD_DIM = D // HEADS
FF = 2048
LANES = 128
PER_GROUP = LANES // HEAD_DIM
MASKED = -1e30
EPSILON = 1e-05
F32 = jnp.float32
BF16 = jnp.bfloat16
VMEM_LIMIT = 48 * 1024 * 1024

AXES = ("xl", "y", "xh", "z", "c")
SIZES = (2, 8, 2, 8, 2)
LAT = ("xl", "y")
LON = ("xh", "z", "c")


def place(lat, lon):
    return (lat % 16) * 32 + lon % 32


def shifted(dlat, dlon):
    return [(place(a, o), place(a + dlat, o + dlon)) for a in range(16) for o in range(32)]


def mirrored():
    def at(x, y, z, c):
        return (((x % 2) * 8 + y) * 2 + x // 2) * 16 + z * 2 + c

    return [
        (at(x, y, z, c), at(3 - x, y, z, c))
        for x in range(4)
        for y in range(8)
        for z in range(8)
        for c in range(2)
    ]


def to_quarters():
    hot = np.zeros((WN, LEVELS, WLAT, WLON), np.float32)
    place_of = 0
    for i in range(2):
        for j in range(2):
            for row in range(HALF_LAT):
                for col in range(HALF_LON):
                    for lev in range(LEVELS):
                        hot[place_of, lev, i * HALF_LAT + row, j * HALF_LON + col] = 1
                        place_of += 1
    return hot.reshape(WN, WN)


def normed(values, gain):
    average = jnp.mean(values, -1, keepdims=True)
    centered = values - average
    variance = jnp.mean(centered * centered, -1, keepdims=True)
    return centered * lax.rsqrt(variance + EPSILON) * gain


def dot(a, b):
    return jnp.dot(a, b, preferred_element_type=F32)


def dot_t(a, b):
    return lax.dot_general(a, b, (((1,), (1,)), ((), ())), preferred_element_type=F32)


def stacked(quarter_refs):
    return jnp.concatenate([q[...].astype(F32).reshape(QUARTER, D) for q in quarter_refs], 0)


def project(rows, weight_ref):
    first = weight_ref[:, 0].reshape(D // 2, D)
    second = weight_ref[:, 1].reshape(D // 2, D)
    return dot(rows[:, : D // 2], first) + dot(rows[:, D // 2 :], second)


def bias_kernel(edge_ref, hot_ref, bias_ref, out_ref):
    moved = dot(hot_ref[...], bias_ref[0]).astype(BF16)
    moved = dot_t(moved, hot_ref[...])
    upper_q = lax.broadcasted_iota(jnp.int32, (WN, WN), 0) < WN // 2
    upper_k = lax.broadcasted_iota(jnp.int32, (WN, WN), 1) < WN // 2
    apart = jnp.logical_and(upper_q != upper_k, edge_ref[0] == 1)
    out_ref[0] = jnp.where(apart, MASKED, moved).astype(BF16)


def attention_kernel(
    r0, r1, r2, r3, wq, wk, wv, wp, bias_ref, gain_ref, o0, o1, o2, o3
):
    cells = stacked((r0, r1, r2, r3))
    rows = cells.astype(BF16)
    queries = project(rows, wq).astype(BF16)
    keys = project(rows, wk).astype(BF16)
    values = project(rows, wv).astype(BF16)
    lane_head = lax.broadcasted_iota(jnp.int32, (1, LANES), 1) // HEAD_DIM
    zero = jnp.zeros((), BF16)
    groups = []
    for group in range(HEADS // PER_GROUP):
        lanes = slice(group * LANES, (group + 1) * LANES)
        group_q, group_k, group_v = queries[:, lanes], keys[:, lanes], values[:, lanes]
        total = None
        for j in range(PER_GROUP):
            mine = lane_head == j
            head_q = jnp.where(mine, group_q, zero)
            scores = dot_t(head_q, group_k) * HEAD_DIM ** (-0.5)
            scores = scores + bias_ref[group * PER_GROUP + j].astype(F32)
            weights = jnp.exp(scores - jnp.max(scores, -1, keepdims=True))
            weights = weights * (1.0 / jnp.sum(weights, -1, keepdims=True))
            part = dot(weights.astype(BF16), jnp.where(mine, group_v, zero))
            total = part if total is None else total + part
        groups.append(total.astype(BF16))
    projected = project(jnp.concatenate(groups, 1), wp)
    mixed = cells + normed(projected, gain_ref[...])
    for i, out in enumerate((o0, o1, o2, o3)):
        out[...] = mixed[i * QUARTER : (i + 1) * QUARTER].reshape(CORNER).astype(BF16)


def mlp_kernel(m0, m1, m2, m3, wu, wd, gain_ref, out_ref):
    cells = stacked((m0, m1, m2, m3))
    rows = cells.astype(BF16)
    lowered = None
    step = 4
    units = FF // 16 * step
    for i in range(0, 16, step):
        up = wu[i : i + step].reshape(units, D)
        down = wd[i : i + step].reshape(units, D)
        raised = dot_t(rows, up)
        hidden = 0.5 * raised * (1.0 + lax.erf(raised * (0.5**0.5)))
        part = dot(hidden.astype(BF16), down)
        lowered = part if lowered is None else lowered + part
    updated = cells + normed(lowered, gain_ref[...])
    run = HALF_LON * LEVELS
    for i in range(2):
        for j in range(2):
            for row in range(HALF_LAT):
                start = (i * 2 + j) * QUARTER + row * run
                piece = updated[start : start + run].reshape(HALF_LON, LEVELS, D)
                out_ref[i * HALF_LAT + row, j * HALF_LON : (j + 1) * HALF_LON] = piece.astype(BF16)


def whole(shape):
    return pl.BlockSpec(shape, lambda i: (0,) * len(shape))


def weight_block(rows, at):
    return pl.BlockSpec((16, 2, rows, D), lambda i: (0, 0, at, 0))


def params():
    return pltpu.CompilerParams(vmem_limit_bytes=VMEM_LIMIT)


def arranged_bias(position_bias, edge):
    one_head = pl.BlockSpec((1, WN, WN), lambda h: (h, 0, 0))
    return pl.pallas_call(
        bias_kernel,
        grid=(HEADS,),
        in_specs=[
            pl.BlockSpec(memory_space=pltpu.SMEM),
            pl.BlockSpec((WN, WN), lambda h: (0, 0)),
            one_head,
        ],
        out_specs=one_head,
        out_shape=jax.ShapeDtypeStruct(position_bias.shape, BF16),
        compiler_params=params(),
        name="bias",
    )(edge, jnp.asarray(to_quarters(), BF16), position_bias)


def attention(quarters, gathered, bias, gain):
    quarter = whole(CORNER)
    return pl.pallas_call(
        attention_kernel,
        grid=(1,),
        in_specs=[quarter] * 4
        + [weight_block(16, i) for i in range(4)]
        + [whole((HEADS, WN, WN)), whole((1, D))],
        out_specs=[quarter] * 4,
        out_shape=[jax.ShapeDtypeStruct(CORNER, BF16)] * 4,
        compiler_params=params(),
        name="attention",
    )(*quarters, gathered, gathered, gathered, gathered, bias, gain.reshape(1, D))


def feed_forward(quarters, gathered, gain):
    quarter = whole(CORNER)
    out = (WLAT, WLON, LEVELS, D)
    return pl.pallas_call(
        mlp_kernel,
        grid=(1,),
        in_specs=[quarter] * 4
        + [weight_block(64, i) for i in (1, 2)]
        + [whole((1, D))],
        out_specs=whole(out),
        out_shape=jax.ShapeDtypeStruct(out, BF16),
        compiler_params=params(),
        name="mlp",
    )(*quarters, gathered, gathered, gain.reshape(1, D))


def shards(
    latent, qkv_weight, proj_weight, position_bias, attn_gain, up_weight, down_weight, mlp_gain
):
    own = jnp.concatenate(
        [qkv_weight[:, i * D : (i + 1) * D] for i in range(3)]
        + [proj_weight, up_weight, down_weight],
        0,
    )
    other = lax.ppermute(own, AXES, mirrored())
    low_half = lax.axis_index("xh") == 0
    both = jnp.stack([jnp.where(low_half, own, other), jnp.where(low_half, other, own)])
    gathered = lax.all_gather(both, ("z", "c"), axis=0, tiled=False)

    cells = latent.transpose(1, 2, 0, 3)

    def corner(i, j):
        return cells[i * HALF_LAT : (i + 1) * HALF_LAT, j * HALF_LON : (j + 1) * HALF_LON]

    rolled = [
        lax.ppermute(corner(1, 1), AXES, shifted(1, 1)),
        lax.ppermute(corner(1, 0), AXES, shifted(1, 0)),
        lax.ppermute(corner(0, 1), AXES, shifted(0, 1)),
        corner(0, 0),
    ]
    edge = (lax.axis_index(LAT) == 0).astype(jnp.int32).reshape(1)
    bias = arranged_bias(position_bias, edge)
    mixed = attention(rolled, gathered, bias, attn_gain)
    restored = [
        mixed[3],
        lax.ppermute(mixed[2], AXES, shifted(0, -1)),
        lax.ppermute(mixed[1], AXES, shifted(-1, 0)),
        lax.ppermute(mixed[0], AXES, shifted(-1, -1)),
    ]
    return feed_forward(restored, gathered, mlp_gain).transpose(2, 0, 1, 3)


def solution(mesh):
    mesh = Mesh(mesh.devices.reshape(SIZES), AXES)
    placed = (
        P(None, LAT, LON, None),
        P(LON, None),
        P(LON, None),
        P(),
        P(),
        P(LON, None),
        P(LON, None),
        P(),
    )
    return jax.shard_map(
        shards, mesh=mesh, in_specs=placed, out_specs=P(None, LAT, LON, None), check_vma=False
    )
```

```python
import jax
import jax.numpy as jnp
import numpy as np
from jax import lax
from jax.experimental import pallas as pl
from jax.experimental.pallas import tpu as pltpu
from jax.sharding import Mesh, PartitionSpec as P

WLAT = 6
WLON = 12
LEVELS = 4
HALF_LAT = WLAT // 2
HALF_LON = WLON // 2
QUARTER = LEVELS * HALF_LAT * HALF_LON
WN = 4 * QUARTER
D = 512
CORNER = (HALF_LAT, HALF_LON, LEVELS, D)
HEADS = 16
HEAD_DIM = D // HEADS
FF = 2048
LANES = 128
PER_GROUP = LANES // HEAD_DIM
MASKED = -1e30
EPSILON = 1e-05
F32 = jnp.float32
BF16 = jnp.bfloat16
VMEM_LIMIT = 48 * 1024 * 1024

AXES = ("xl", "y", "xh", "z", "c")
SIZES = (2, 8, 2, 8, 2)
LAT = ("xl", "y")
LON = ("xh", "z", "c")


def place(lat, lon):
    return (lat % 16) * 32 + lon % 32


def shifted(dlat, dlon):
    return [(place(a, o), place(a + dlat, o + dlon)) for a in range(16) for o in range(32)]


def mirrored():
    def at(x, y, z, c):
        return (((x % 2) * 8 + y) * 2 + x // 2) * 16 + z * 2 + c

    return [
        (at(x, y, z, c), at(3 - x, y, z, c))
        for x in range(4)
        for y in range(8)
        for z in range(8)
        for c in range(2)
    ]


def swapped():
    return [(d, d ^ 1) for d in range(512)]


def to_quarters():
    hot = np.zeros((WN, LEVELS, WLAT, WLON), np.float32)
    place_of = 0
    for i in range(2):
        for j in range(2):
            for row in range(HALF_LAT):
                for col in range(HALF_LON):
                    for lev in range(LEVELS):
                        hot[place_of, lev, i * HALF_LAT + row, j * HALF_LON + col] = 1
                        place_of += 1
    return hot.reshape(WN, WN)


def apart():
    upper = np.arange(WN) // WLON % WLAT < HALF_LAT
    return np.where(upper[:, None] != upper[None], MASKED, 0.0).astype(np.float32)


def normed(values, gain):
    average = jnp.mean(values, -1, keepdims=True)
    centered = values - average
    variance = jnp.mean(centered * centered, -1, keepdims=True)
    return centered * lax.rsqrt(variance + EPSILON) * gain


def dot(a, b):
    return jnp.dot(a, b, preferred_element_type=F32)


def dot_t(a, b):
    return lax.dot_general(a, b, (((1,), (1,)), ((), ())), preferred_element_type=F32)


def stacked(quarters):
    return jnp.concatenate([q.astype(F32).reshape(QUARTER, D) for q in quarters], 0)


def corner(cells, i, j):
    return cells[i * HALF_LAT : (i + 1) * HALF_LAT, j * HALF_LON : (j + 1) * HALF_LON]


def pack_kernel(qkv_ref, proj_ref, up_ref, down_ref, out_ref):
    for i in range(3):
        out_ref[i * 16 : (i + 1) * 16] = qkv_ref[:, i * D : (i + 1) * D]
    out_ref[48:112] = up_ref[...]
    out_ref[112:176] = down_ref[...]
    out_ref[176:192] = proj_ref[...]


def attention_kernel(
    spot_ref, r0, r1, r2, r3, mine_ref, other_ref, bias_ref, hot_ref, away_ref, o0, o1, o2, o3
):
    hot = hot_ref[...]
    rows = stacked([r[...] for r in (r0, r1, r2, r3)]).astype(BF16)
    rows = lax.dot_general(hot, rows, (((0,), (0,)), ((), ())), preferred_element_type=F32)
    rows = rows.astype(BF16)
    first_core = spot_ref[0] == 0
    away = jnp.where(spot_ref[1] == 1, away_ref[...], 0.0)

    def projected(which):
        total = None
        for half in range(2):
            mine, other = mine_ref[:, half, which], other_ref[:, half, which]
            even = jnp.where(first_core, mine, other)
            odd = jnp.where(first_core, other, mine)
            weight = jnp.stack([even, odd], 1).reshape(D // 2, D)
            part = dot(rows[:, half * (D // 2) : (half + 1) * (D // 2)], weight)
            total = part if total is None else total + part
        return total.astype(BF16)

    queries, keys, values = projected(0), projected(1), projected(2)
    lane_head = lax.broadcasted_iota(jnp.int32, (1, LANES), 1) // HEAD_DIM
    zero = jnp.zeros((), BF16)
    groups = []
    for group in range(HEADS // PER_GROUP):
        lanes = slice(group * LANES, (group + 1) * LANES)
        group_q, group_k, group_v = queries[:, lanes], keys[:, lanes], values[:, lanes]
        total = None
        for j in range(PER_GROUP):
            mine = lane_head == j
            head_q = jnp.where(mine, group_q, zero)
            scores = dot_t(head_q, group_k) * HEAD_DIM ** (-0.5)
            scores = scores + bias_ref[group * PER_GROUP + j].astype(F32) + away
            weights = jnp.exp(scores - jnp.max(scores, -1, keepdims=True))
            weights = weights * (1.0 / jnp.sum(weights, -1, keepdims=True))
            part = dot(weights.astype(BF16), jnp.where(mine, group_v, zero))
            total = part if total is None else total + part
        groups.append(total.astype(BF16))
    attended = dot(hot, jnp.concatenate(groups, 1))
    for i, out in enumerate((o0, o1, o2, o3)):
        out[...] = attended[i * QUARTER : (i + 1) * QUARTER].reshape(CORNER).astype(BF16)


def token_kernel(m0, m1, m2, m3, cells_ref, wp, wu, wd, attn_gain_ref, mlp_gain_ref, out_ref):
    attended = stacked([m[...] for m in (m0, m1, m2, m3)]).astype(BF16)
    cells = stacked([corner(cells_ref, i, j) for i in range(2) for j in range(2)])
    projected = dot(attended[:, : D // 2], wp[:, 0].reshape(D // 2, D)) + dot(
        attended[:, D // 2 :], wp[:, 1].reshape(D // 2, D)
    )
    rows = (cells + normed(projected, attn_gain_ref[...])).astype(BF16)
    lowered = None
    step = 4
    units = FF // 16 * step
    for i in range(0, 16, step):
        up = wu[i : i + step].reshape(units, D)
        down = wd[i : i + step].reshape(units, D)
        raised = dot_t(rows, up)
        hidden = 0.5 * raised * (1.0 + lax.erf(raised * (0.5**0.5)))
        part = dot(hidden.astype(BF16), down)
        lowered = part if lowered is None else lowered + part
    updated = rows.astype(F32) + normed(lowered, mlp_gain_ref[...])
    run = HALF_LON * LEVELS
    for i in range(2):
        for j in range(2):
            for row in range(HALF_LAT):
                start = (i * 2 + j) * QUARTER + row * run
                piece = updated[start : start + run].reshape(HALF_LON, LEVELS, D)
                out_ref[i * HALF_LAT + row, j * HALF_LON : (j + 1) * HALF_LON] = piece.astype(BF16)


def whole(shape):
    return pl.BlockSpec(shape, lambda i: (0,) * len(shape))


def weight_block(rows, at):
    return pl.BlockSpec((16, 2, rows, D), lambda i: (0, 0, at, 0))


def scalars():
    return pl.BlockSpec(memory_space=pltpu.SMEM)


def params():
    return pltpu.CompilerParams(vmem_limit_bytes=VMEM_LIMIT)


def packed(qkv_weight, proj_weight, up_weight, down_weight):
    weights = (qkv_weight, proj_weight, up_weight, down_weight)
    return pl.pallas_call(
        pack_kernel,
        grid=(1,),
        in_specs=[whole(w.shape) for w in weights],
        out_specs=whole((192, D)),
        out_shape=jax.ShapeDtypeStruct((192, D), BF16),
        compiler_params=params(),
        name="pack",
    )(*weights)


def attention(spot, quarters, mine, other, bias):
    quarter = whole(CORNER)
    weight = whole(mine.shape)
    return pl.pallas_call(
        attention_kernel,
        grid=(1,),
        in_specs=[scalars()]
        + [quarter] * 4
        + [weight] * 2
        + [whole(bias.shape), whole((WN, WN)), whole((WN, WN))],
        out_specs=[quarter] * 4,
        out_shape=[jax.ShapeDtypeStruct(CORNER, BF16)] * 4,
        compiler_params=params(),
        name="attention",
    )(spot, *quarters, mine, other, bias, jnp.asarray(to_quarters(), BF16), jnp.asarray(apart()))


def tokens(quarters, cells, gathered, attn_gain, mlp_gain):
    quarter = whole(CORNER)
    out = (WLAT, WLON, LEVELS, D)
    return pl.pallas_call(
        token_kernel,
        grid=(1,),
        in_specs=[quarter] * 4
        + [whole(out), weight_block(16, 8), weight_block(64, 0), weight_block(64, 1)]
        + [whole((1, D))] * 2,
        out_specs=whole(out),
        out_shape=jax.ShapeDtypeStruct(out, BF16),
        compiler_params=params(),
        name="tokens",
    )(*quarters, cells, gathered, gathered, gathered, attn_gain.reshape(1, D), mlp_gain.reshape(1, D))


def shards(
    latent, qkv_weight, proj_weight, position_bias, attn_gain, up_weight, down_weight, mlp_gain
):
    own = packed(qkv_weight, proj_weight, up_weight, down_weight)
    other = lax.ppermute(own, AXES, mirrored())
    low_half = lax.axis_index("xh") == 0

    def halves(start, stop):
        ours, theirs = own[start:stop], other[start:stop]
        return jnp.stack([jnp.where(low_half, ours, theirs), jnp.where(low_half, theirs, ours)])

    gathered = lax.all_gather(halves(48, 192), ("z", "c"), axis=0, tiled=False)
    mine = lax.all_gather(halves(0, 48), "z", axis=0, tiled=False)
    theirs = lax.ppermute(mine, AXES, swapped())
    by_shard = (8, 2, 3, 16, D)

    cells = latent.transpose(1, 2, 0, 3)
    rolled = [
        lax.ppermute(corner(cells, 1, 1), AXES, shifted(1, 1)),
        lax.ppermute(corner(cells, 1, 0), AXES, shifted(1, 0)),
        lax.ppermute(corner(cells, 0, 1), AXES, shifted(0, 1)),
        corner(cells, 0, 0),
    ]
    spot = jnp.stack([lax.axis_index("c"), (lax.axis_index(LAT) == 0).astype(jnp.int32)])
    attended = attention(
        spot, rolled, mine.reshape(by_shard), theirs.reshape(by_shard), position_bias
    )
    restored = [
        attended[3],
        lax.ppermute(attended[2], AXES, shifted(0, -1)),
        lax.ppermute(attended[1], AXES, shifted(-1, 0)),
        lax.ppermute(attended[0], AXES, shifted(-1, -1)),
    ]
    return tokens(restored, cells, gathered, attn_gain, mlp_gain).transpose(2, 0, 1, 3)


def solution(mesh):
    mesh = Mesh(mesh.devices.reshape(SIZES), AXES)
    placed = (
        P(None, LAT, LON, None),
        P(LON, None),
        P(LON, None),
        P(),
        P(),
        P(LON, None),
        P(LON, None),
        P(),
    )
    return jax.shard_map(
        shards, mesh=mesh, in_specs=placed, out_specs=P(None, LAT, LON, None), check_vma=False
    )
```

```python
import jax
import jax.numpy as jnp
import numpy as np
from jax import lax
from jax.experimental import pallas as pl
from jax.experimental.pallas import tpu as pltpu
from jax.sharding import Mesh, PartitionSpec as P

WLAT = 6
WLON = 12
LEVELS = 4
HALF_LAT = WLAT // 2
HALF_LON = WLON // 2
QUARTER = LEVELS * HALF_LAT * HALF_LON
WN = 4 * QUARTER
D = 512
CORNER = (HALF_LAT, HALF_LON, LEVELS, D)
HEADS = 16
HEAD_DIM = D // HEADS
FF = 2048
LANES = 128
PER_GROUP = LANES // HEAD_DIM
GROUPS = HEADS // PER_GROUP
PIECES = 4
MASKED = -1e30
EPSILON = 1e-05
F32 = jnp.float32
BF16 = jnp.bfloat16
VMEM_LIMIT = 60 * 1024 * 1024

AXES = ("xl", "y", "xh", "z", "c")
SIZES = (2, 8, 2, 8, 2)
LAT = ("xl", "y")
LON = ("xh", "z", "c")


def place(lat, lon):
    return (lat % 16) * 32 + lon % 32


def shifted(dlat, dlon):
    return [(place(a, o), place(a + dlat, o + dlon)) for a in range(16) for o in range(32)]


def mirrored():
    def at(x, y, z, c):
        return (((x % 2) * 8 + y) * 2 + x // 2) * 16 + z * 2 + c

    return [
        (at(x, y, z, c), at(3 - x, y, z, c))
        for x in range(4)
        for y in range(8)
        for z in range(8)
        for c in range(2)
    ]


def to_quarters():
    hot = np.zeros((WN, LEVELS, WLAT, WLON), np.float32)
    place_of = 0
    for i in range(2):
        for j in range(2):
            for row in range(HALF_LAT):
                for col in range(HALF_LON):
                    for lev in range(LEVELS):
                        hot[place_of, lev, i * HALF_LAT + row, j * HALF_LON + col] = 1
                        place_of += 1
    return hot.reshape(WN, WN)


def tags():
    upper = (np.arange(WN) // WLON % WLAT < HALF_LAT).astype(np.float32)
    columns = np.zeros((2, WN, LANES), np.float32)
    columns[0, :, 0], columns[0, :, 1] = upper, 1 - upper
    columns[1, :, 0], columns[1, :, 1] = MASKED * (1 - upper), MASKED * upper
    return columns


def normed(values, gain):
    average = jnp.mean(values, -1, keepdims=True)
    centered = values - average
    variance = jnp.mean(centered * centered, -1, keepdims=True)
    return centered * lax.rsqrt(variance + EPSILON) * gain


def dot(a, b):
    return jnp.dot(a, b, preferred_element_type=F32)


def dot_t(a, b):
    return lax.dot_general(a, b, (((1,), (1,)), ((), ())), preferred_element_type=F32)


def stacked(quarters):
    return jnp.concatenate([q.astype(F32).reshape(QUARTER, D) for q in quarters], 0)


def corner(cells, i, j):
    return cells[i * HALF_LAT : (i + 1) * HALF_LAT, j * HALF_LON : (j + 1) * HALF_LON]


def pack_kernel(up_ref, down_ref, proj_ref, out_ref, sems):
    copies = [
        pltpu.make_async_copy(source, out_ref.at[start : start + source.shape[0]], sems.at[i])
        for i, (source, start) in enumerate(((up_ref, 0), (down_ref, 64), (proj_ref, 128)))
    ]
    for copy in copies:
        copy.start()
    for copy in copies:
        copy.wait()


def attention_kernel(
    spot_ref, r0, r1, r2, r3, mine_ref, other_ref, hot_ref, tags_ref, bias_hbm,
    o0, o1, o2, o3, bias_ref, sems,
):
    fetches = [
        pltpu.make_async_copy(
            bias_hbm.at[g * PER_GROUP : (g + 1) * PER_GROUP],
            bias_ref.at[g * PER_GROUP : (g + 1) * PER_GROUP],
            sems.at[g],
        )
        for g in range(GROUPS)
    ]
    for fetch in fetches:
        fetch.start()
    hot = hot_ref[...]
    rows = stacked([r[...] for r in (r0, r1, r2, r3)]).astype(BF16)
    rows = lax.dot_general(hot, rows, (((0,), (0,)), ((), ())), preferred_element_type=F32)
    rows = rows.astype(BF16)
    low_half = spot_ref[0] == 0

    def projected(which):
        columns = slice(which * D, (which + 1) * D)
        mine = mine_ref[:, :, columns].reshape(D // 2, D)
        other = jnp.stack([other_ref[0, :, :, columns], other_ref[1, :, :, columns]], 1)
        other = other.reshape(D // 2, D)
        low = dot(rows[:, : D // 2], jnp.where(low_half, mine, other))
        return (low + dot(rows[:, D // 2 :], jnp.where(low_half, other, mine))).astype(BF16)

    queries, keys, values = projected(0), projected(1), projected(2)
    lane_head = lax.broadcasted_iota(jnp.int32, (1, LANES), 1) // HEAD_DIM
    zero = jnp.zeros((), BF16)
    ones = jnp.ones((WN, LANES), BF16)
    query_tags = jnp.where(spot_ref[1] == 1, tags_ref[0], zero)
    key_tags = tags_ref[1]
    groups = []
    for group in range(GROUPS):
        fetches[group].wait()
        lanes = slice(group * LANES, (group + 1) * LANES)
        group_q, group_v = queries[:, lanes], values[:, lanes]
        group_k = jnp.concatenate([keys[:, lanes], key_tags], 1)
        total = None
        for j in range(PER_GROUP):
            mine = lane_head == j
            head_q = jnp.concatenate([jnp.where(mine, group_q, zero), query_tags], 1)
            scores = dot_t(head_q, group_k) * HEAD_DIM ** (-0.5)
            scores = scores + bias_ref[group * PER_GROUP + j].astype(F32)
            weights = jnp.exp(scores - jnp.max(scores, -1, keepdims=True)).astype(BF16)
            head_v = jnp.concatenate([jnp.where(mine, group_v, zero), ones], 1)
            product = dot(weights, head_v)
            part = product[:, :LANES] / product[:, LANES:]
            total = part if total is None else total + part
        groups.append(total.astype(BF16))
    attended = dot(hot, jnp.concatenate(groups, 1))
    for i, out in enumerate((o0, o1, o2, o3)):
        out[...] = attended[i * QUARTER : (i + 1) * QUARTER].reshape(CORNER).astype(BF16)


def token_kernel(
    m0, m1, m2, m3, cells_ref, attn_gain_ref, mlp_gain_ref, weights_hbm, out_ref, wp, wu, wd, sems
):
    fetch_proj = pltpu.make_async_copy(weights_hbm.at[:, :, 128:144], wp, sems.at[0])
    fetch_proj.start()
    fetches = []
    step = 16 // PIECES
    for i in range(PIECES):
        shards_of = slice(i * step, (i + 1) * step)
        fetches.append(
            [
                pltpu.make_async_copy(
                    weights_hbm.at[shards_of, :, 64 * k : 64 * (k + 1)],
                    target.at[shards_of],
                    sems.at[1 + 2 * i + k],
                )
                for k, target in enumerate((wu, wd))
            ]
        )
        for fetch in fetches[-1]:
            fetch.start()
    attended = stacked([m[...] for m in (m0, m1, m2, m3)]).astype(BF16)
    cells = stacked([corner(cells_ref, i, j) for i in range(2) for j in range(2)])
    fetch_proj.wait()
    projected = dot(attended[:, : D // 2], wp[:, 0].reshape(D // 2, D)) + dot(
        attended[:, D // 2 :], wp[:, 1].reshape(D // 2, D)
    )
    rows = (cells + normed(projected, attn_gain_ref[...])).astype(BF16)
    lowered = None
    units = FF // PIECES
    for i in range(PIECES):
        for fetch in fetches[i]:
            fetch.wait()
        up = wu[i * step : (i + 1) * step].reshape(units, D)
        down = wd[i * step : (i + 1) * step].reshape(units, D)
        raised = dot_t(rows, up)
        hidden = 0.5 * raised * (1.0 + lax.erf(raised * (0.5**0.5)))
        part = dot(hidden.astype(BF16), down)
        lowered = part if lowered is None else lowered + part
    updated = rows.astype(F32) + normed(lowered, mlp_gain_ref[...])
    run = HALF_LON * LEVELS
    for i in range(2):
        for j in range(2):
            for row in range(HALF_LAT):
                start = (i * 2 + j) * QUARTER + row * run
                piece = updated[start : start + run].reshape(HALF_LON, LEVELS, D)
                out_ref[i * HALF_LAT + row, j * HALF_LON : (j + 1) * HALF_LON] = piece.astype(BF16)


def whole(shape):
    return pl.BlockSpec(shape, lambda i: (0,) * len(shape))


def scalars():
    return pl.BlockSpec(memory_space=pltpu.SMEM)


def fetched():
    return pl.BlockSpec(memory_space=pl.ANY)


def params():
    return pltpu.CompilerParams(vmem_limit_bytes=VMEM_LIMIT)


def packed(up_weight, down_weight, proj_weight):
    return pl.pallas_call(
        pack_kernel,
        grid=(1,),
        in_specs=[fetched()] * 3,
        out_specs=whole((144, D)),
        out_shape=jax.ShapeDtypeStruct((144, D), BF16),
        scratch_shapes=[pltpu.SemaphoreType.DMA((3,))],
        compiler_params=params(),
        name="pack",
    )(up_weight, down_weight, proj_weight)


def attention(spot, quarters, mine, other, bias):
    quarter = whole(CORNER)
    constants = (jnp.asarray(to_quarters(), BF16), jnp.asarray(tags(), BF16))
    return pl.pallas_call(
        attention_kernel,
        grid=(1,),
        in_specs=[scalars()]
        + [quarter] * 4
        + [whole(a.shape) for a in (mine, other, *constants)]
        + [fetched()],
        out_specs=[quarter] * 4,
        out_shape=[jax.ShapeDtypeStruct(CORNER, BF16)] * 4,
        scratch_shapes=[pltpu.VMEM(bias.shape, BF16), pltpu.SemaphoreType.DMA((GROUPS,))],
        compiler_params=params(),
        name="attention",
    )(spot, *quarters, mine, other, *constants, bias)


def tokens(quarters, cells, gathered, attn_gain, mlp_gain):
    out = (WLAT, WLON, LEVELS, D)
    return pl.pallas_call(
        token_kernel,
        grid=(1,),
        in_specs=[whole(CORNER)] * 4 + [whole(out)] + [whole((1, D))] * 2 + [fetched()],
        out_specs=whole(out),
        out_shape=jax.ShapeDtypeStruct(out, BF16),
        scratch_shapes=[pltpu.VMEM((16, 2, rows, D), BF16) for rows in (16, 64, 64)]
        + [pltpu.SemaphoreType.DMA((1 + 2 * PIECES,))],
        compiler_params=params(),
        name="tokens",
    )(*quarters, cells, attn_gain.reshape(1, D), mlp_gain.reshape(1, D), gathered)


def shards(
    latent, qkv_weight, proj_weight, position_bias, attn_gain, up_weight, down_weight, mlp_gain
):
    own = packed(up_weight, down_weight, proj_weight)
    other = lax.ppermute(own, AXES, mirrored())
    low_half = lax.axis_index("xh") == 0
    both = jnp.stack([jnp.where(low_half, own, other), jnp.where(low_half, other, own)])
    gathered = lax.all_gather(both, ("z", "c"), axis=0, tiled=False)

    cells = latent.transpose(1, 2, 0, 3)
    rolled = [
        lax.ppermute(corner(cells, 1, 1), AXES, shifted(1, 1)),
        lax.ppermute(corner(cells, 1, 0), AXES, shifted(1, 0)),
        lax.ppermute(corner(cells, 0, 1), AXES, shifted(0, 1)),
        corner(cells, 0, 0),
    ]
    qkv_weight, _, rolled = lax.optimization_barrier((qkv_weight, both, rolled))
    mine = lax.all_gather(qkv_weight, ("z", "c"), axis=0, tiled=False)
    core = lax.axis_index("c")
    sent = lax.dynamic_index_in_dim(mine.reshape(8, 2, 16, 3 * D), core, 1, keepdims=False)
    theirs = lax.all_gather(lax.ppermute(sent, AXES, mirrored()), "c", axis=0, tiled=False)

    spot = jnp.stack([lax.axis_index("xh"), (lax.axis_index(LAT) == 0).astype(jnp.int32)])
    attended = attention(spot, rolled, mine, theirs, position_bias)
    restored = [
        attended[3],
        lax.ppermute(attended[2], AXES, shifted(0, -1)),
        lax.ppermute(attended[1], AXES, shifted(-1, 0)),
        lax.ppermute(attended[0], AXES, shifted(-1, -1)),
    ]
    return tokens(restored, cells, gathered, attn_gain, mlp_gain).transpose(2, 0, 1, 3)


def solution(mesh):
    mesh = Mesh(mesh.devices.reshape(SIZES), AXES)
    placed = (
        P(None, LAT, LON, None),
        P(LON, None),
        P(LON, None),
        P(),
        P(),
        P(LON, None),
        P(LON, None),
        P(),
    )
    return jax.shard_map(
        shards, mesh=mesh, in_specs=placed, out_specs=P(None, LAT, LON, None), check_vma=False
    )
```

```python
import jax
import jax.numpy as jnp
import numpy as np
from jax import lax
from jax.experimental import pallas as pl
from jax.experimental.pallas import tpu as pltpu
from jax.sharding import Mesh, PartitionSpec as P

WLAT = 6
WLON = 12
LEVELS = 4
HALF_LAT = WLAT // 2
HALF_LON = WLON // 2
QUARTER = LEVELS * HALF_LAT * HALF_LON
WN = 4 * QUARTER
D = 512
CORNER = (HALF_LAT, HALF_LON, LEVELS, D)
HEADS = 16
HEAD_DIM = D // HEADS
FF = 2048
LANES = 128
PER_GROUP = LANES // HEAD_DIM
GROUPS = HEADS // PER_GROUP
PIECES = 4
MASKED = -1e30
EPSILON = 1e-05
F32 = jnp.float32
BF16 = jnp.bfloat16
VMEM_LIMIT = 60 * 1024 * 1024
STAGE_LIMIT = 48 * 1024 * 1024
TOKENS_LIMIT = 40 * 1024 * 1024

AXES = ("xl", "y", "xh", "z", "c")
SIZES = (2, 8, 2, 8, 2)
LAT = ("xl", "y")
LON = ("xh", "z", "c")


def place(lat, lon):
    return (lat % 16) * 32 + lon % 32


def shifted(dlat, dlon):
    return [(place(a, o), place(a + dlat, o + dlon)) for a in range(16) for o in range(32)]


def mirrored():
    def at(x, y, z, c):
        return (((x % 2) * 8 + y) * 2 + x // 2) * 16 + z * 2 + c

    return [
        (at(x, y, z, c), at(3 - x, y, z, c))
        for x in range(4)
        for y in range(8)
        for z in range(8)
        for c in range(2)
    ]


def to_quarters():
    hot = np.zeros((WN, LEVELS, WLAT, WLON), np.float32)
    place_of = 0
    for i in range(2):
        for j in range(2):
            for row in range(HALF_LAT):
                for col in range(HALF_LON):
                    for lev in range(LEVELS):
                        hot[place_of, lev, i * HALF_LAT + row, j * HALF_LON + col] = 1
                        place_of += 1
    return hot.reshape(WN, WN)


def tags():
    upper = (np.arange(WN) // WLON % WLAT < HALF_LAT).astype(np.float32)
    columns = np.zeros((2, WN, LANES), np.float32)
    columns[0, :, 0], columns[0, :, 1] = upper, 1 - upper
    columns[1, :, 0], columns[1, :, 1] = MASKED * (1 - upper), MASKED * upper
    return columns


def normed(values, gain):
    average = jnp.mean(values, -1, keepdims=True)
    centered = values - average
    variance = jnp.mean(centered * centered, -1, keepdims=True)
    return centered * lax.rsqrt(variance + EPSILON) * gain


def dot(a, b):
    return jnp.dot(a, b, preferred_element_type=F32)


def dot_t(a, b):
    return lax.dot_general(a, b, (((1,), (1,)), ((), ())), preferred_element_type=F32)


def stacked(quarters):
    return jnp.concatenate([q.astype(F32).reshape(QUARTER, D) for q in quarters], 0)


def corner(cells, i, j):
    return cells[i * HALF_LAT : (i + 1) * HALF_LAT, j * HALF_LON : (j + 1) * HALF_LON]


def pack_kernel(up_ref, down_ref, proj_ref, out_ref, sems):
    copies = [
        pltpu.make_async_copy(source, out_ref.at[start : start + source.shape[0]], sems.at[i])
        for i, (source, start) in enumerate(((up_ref, 0), (down_ref, 64), (proj_ref, 128)))
    ]
    for copy in copies:
        copy.start()
    for copy in copies:
        copy.wait()


def attention_kernel(
    spot_ref, r0, r1, r2, r3, mine_ref, other_ref, hot_ref, tags_ref, bias_hbm,
    o0, o1, o2, o3, bias_ref, sems,
):
    fetches = [
        pltpu.make_async_copy(
            bias_hbm.at[g * PER_GROUP : (g + 1) * PER_GROUP],
            bias_ref.at[g * PER_GROUP : (g + 1) * PER_GROUP],
            sems.at[g],
        )
        for g in range(GROUPS)
    ]
    for fetch in fetches:
        fetch.start()
    hot = hot_ref[...]
    rows = stacked([r[...] for r in (r0, r1, r2, r3)]).astype(BF16)
    rows = lax.dot_general(hot, rows, (((0,), (0,)), ((), ())), preferred_element_type=F32)
    rows = rows.astype(BF16)
    low_half = spot_ref[0] == 0

    def projected(which):
        columns = slice(which * D, (which + 1) * D)
        mine = mine_ref[:, :, columns].reshape(D // 2, D)
        other = jnp.stack([other_ref[0, :, :, columns], other_ref[1, :, :, columns]], 1)
        other = other.reshape(D // 2, D)
        low = dot(rows[:, : D // 2], jnp.where(low_half, mine, other))
        return (low + dot(rows[:, D // 2 :], jnp.where(low_half, other, mine))).astype(BF16)

    queries, keys, values = projected(0), projected(1), projected(2)
    lane_head = lax.broadcasted_iota(jnp.int32, (1, LANES), 1) // HEAD_DIM
    zero = jnp.zeros((), BF16)
    ones = jnp.ones((WN, LANES), BF16)
    query_tags = jnp.where(spot_ref[1] == 1, tags_ref[0], zero)
    key_tags = tags_ref[1]
    groups = []
    for group in range(GROUPS):
        fetches[group].wait()
        lanes = slice(group * LANES, (group + 1) * LANES)
        group_q, group_v = queries[:, lanes], values[:, lanes]
        group_k = jnp.concatenate([keys[:, lanes], key_tags], 1)
        total = None
        for j in range(PER_GROUP):
            mine = lane_head == j
            head_q = jnp.concatenate([jnp.where(mine, group_q, zero), query_tags], 1)
            scores = dot_t(head_q, group_k) * HEAD_DIM ** (-0.5)
            scores = scores + bias_ref[group * PER_GROUP + j].astype(F32)
            weights = jnp.exp(scores - jnp.max(scores, -1, keepdims=True)).astype(BF16)
            head_v = jnp.concatenate([jnp.where(mine, group_v, zero), ones], 1)
            product = dot(weights, head_v)
            part = product[:, :LANES] / product[:, LANES:]
            total = part if total is None else total + part
        groups.append(total.astype(BF16))
    attended = dot(hot, jnp.concatenate(groups, 1))
    for i, out in enumerate((o0, o1, o2, o3)):
        out[...] = attended[i * QUARTER : (i + 1) * QUARTER].reshape(CORNER).astype(BF16)


def stage_kernel(gathered_ref, wp_ref, wu_ref, wd_ref, sems):
    copies = [
        pltpu.make_async_copy(gathered_ref.at[:, :, start:stop], target, sems.at[i])
        for i, (start, stop, target) in enumerate(
            ((128, 144, wp_ref), (0, 64, wu_ref), (64, 128, wd_ref))
        )
    ]
    for copy in copies:
        copy.start()
    for copy in copies:
        copy.wait()


def token_kernel(
    spot_ref, m0, m1, m2, m3, cells_ref, wp, wu, wd, attn_gain_ref, mlp_gain_ref, out_ref
):
    attended = stacked([m[...] for m in (m0, m1, m2, m3)]).astype(BF16)
    cells = stacked([corner(cells_ref, i, j) for i in range(2) for j in range(2)])
    low_half = spot_ref[0] == 0
    low, high = attended[:, : D // 2], attended[:, D // 2 :]
    ours, theirs = jnp.where(low_half, low, high), jnp.where(low_half, high, low)
    projected = dot(ours, wp[:, 0].reshape(D // 2, D)) + dot(theirs, wp[:, 1].reshape(D // 2, D))
    rows = (cells + normed(projected, attn_gain_ref[...])).astype(BF16)
    lowered = None
    step = 16 // PIECES
    units = FF // PIECES
    for i in range(0, 16, step):
        up = wu[i : i + step].reshape(units, D)
        down = wd[i : i + step].reshape(units, D)
        raised = dot_t(rows, up)
        hidden = 0.5 * raised * (1.0 + lax.erf(raised * (0.5**0.5)))
        part = dot(hidden.astype(BF16), down)
        lowered = part if lowered is None else lowered + part
    updated = rows.astype(F32) + normed(lowered, mlp_gain_ref[...])
    run = HALF_LON * LEVELS
    for i in range(2):
        for j in range(2):
            for row in range(HALF_LAT):
                start = (i * 2 + j) * QUARTER + row * run
                piece = updated[start : start + run].reshape(HALF_LON, LEVELS, D)
                out_ref[i * HALF_LAT + row, j * HALF_LON : (j + 1) * HALF_LON] = piece.astype(BF16)


def whole(shape):
    return pl.BlockSpec(shape, lambda i: (0,) * len(shape))


def scalars():
    return pl.BlockSpec(memory_space=pltpu.SMEM)


def fetched():
    return pl.BlockSpec(memory_space=pl.ANY)


def params():
    return pltpu.CompilerParams(vmem_limit_bytes=VMEM_LIMIT)


def packed(up_weight, down_weight, proj_weight):
    return pl.pallas_call(
        pack_kernel,
        grid=(1,),
        in_specs=[fetched()] * 3,
        out_specs=whole((144, D)),
        out_shape=jax.ShapeDtypeStruct((144, D), BF16),
        scratch_shapes=[pltpu.SemaphoreType.DMA((3,))],
        compiler_params=params(),
        name="pack",
    )(up_weight, down_weight, proj_weight)


def attention(spot, quarters, mine, other, bias):
    quarter = whole(CORNER)
    constants = (jnp.asarray(to_quarters(), BF16), jnp.asarray(tags(), BF16))
    return pl.pallas_call(
        attention_kernel,
        grid=(1,),
        in_specs=[scalars()]
        + [quarter] * 4
        + [whole(a.shape) for a in (mine, other, *constants)]
        + [fetched()],
        out_specs=[quarter] * 4,
        out_shape=[jax.ShapeDtypeStruct(CORNER, BF16)] * 4,
        scratch_shapes=[pltpu.VMEM(bias.shape, BF16), pltpu.SemaphoreType.DMA((GROUPS,))],
        compiler_params=params(),
        name="attention",
    )(spot, *quarters, mine, other, *constants, bias)


def staged(gathered):
    sizes = [(16, 2, rows, D) for rows in (16, 64, 64)]
    return pl.pallas_call(
        stage_kernel,
        in_specs=[fetched()],
        out_specs=[pl.BlockSpec(memory_space=pltpu.VMEM)] * 3,
        out_shape=[jax.ShapeDtypeStruct(size, BF16) for size in sizes],
        scratch_shapes=[pltpu.SemaphoreType.DMA((3,))],
        compiler_params=pltpu.CompilerParams(vmem_limit_bytes=STAGE_LIMIT),
        cost_estimate=pl.CostEstimate(flops=0, bytes_accessed=2 * 144 * 32 * D * 2, transcendentals=0),
        name="stage",
    )(gathered)


def tokens(spot, quarters, cells, weights, attn_gain, mlp_gain):
    out = (WLAT, WLON, LEVELS, D)
    return pl.pallas_call(
        token_kernel,
        grid=(1,),
        in_specs=[scalars()]
        + [whole(CORNER)] * 4
        + [whole(a.shape) for a in (cells, *weights)]
        + [whole((1, D))] * 2,
        out_specs=whole(out),
        out_shape=jax.ShapeDtypeStruct(out, BF16),
        compiler_params=pltpu.CompilerParams(vmem_limit_bytes=TOKENS_LIMIT),
        name="tokens",
    )(
        spot, *quarters, cells, *weights,
        attn_gain.reshape(1, D), mlp_gain.reshape(1, D),
    )


def shards(
    latent, qkv_weight, proj_weight, position_bias, attn_gain, up_weight, down_weight, mlp_gain
):
    own = packed(up_weight, down_weight, proj_weight)
    other = lax.ppermute(own, AXES, mirrored())
    both = jnp.stack([own, other])
    gathered = lax.all_gather(both, ("z", "c"), axis=0, tiled=False)

    qkv_weight, _ = lax.optimization_barrier((qkv_weight, both))
    mine = lax.all_gather(qkv_weight, ("z", "c"), axis=0, tiled=False)
    cells = latent.transpose(1, 2, 0, 3)
    cells_after, mine = lax.optimization_barrier((cells, mine))
    rolled = [
        lax.ppermute(corner(cells_after, 1, 1), AXES, shifted(1, 1)),
        lax.ppermute(corner(cells_after, 1, 0), AXES, shifted(1, 0)),
        lax.ppermute(corner(cells_after, 0, 1), AXES, shifted(0, 1)),
        corner(cells_after, 0, 0),
    ]
    core = lax.axis_index("c")
    sent = lax.dynamic_index_in_dim(mine.reshape(8, 2, 16, 3 * D), core, 1, keepdims=False)
    theirs = lax.all_gather(lax.ppermute(sent, AXES, mirrored()), "c", axis=0, tiled=False)

    spot = jnp.stack([lax.axis_index("xh"), (lax.axis_index(LAT) == 0).astype(jnp.int32)])
    attended = attention(spot, rolled, mine, theirs, position_bias)
    attended, gathered = lax.optimization_barrier((attended, gathered))
    restored = [
        attended[3],
        lax.ppermute(attended[2], AXES, shifted(0, -1)),
        lax.ppermute(attended[1], AXES, shifted(-1, 0)),
        lax.ppermute(attended[0], AXES, shifted(-1, -1)),
    ]
    return tokens(spot, restored, cells, staged(gathered), attn_gain, mlp_gain).transpose(2, 0, 1, 3)


def solution(mesh):
    mesh = Mesh(mesh.devices.reshape(SIZES), AXES)
    placed = (
        P(None, LAT, LON, None),
        P(LON, None),
        P(LON, None),
        P(),
        P(),
        P(LON, None),
        P(LON, None),
        P(),
    )
    return jax.shard_map(
        shards, mesh=mesh, in_specs=placed, out_specs=P(None, LAT, LON, None), check_vma=False
    )
```

```python
import jax
import jax.numpy as jnp
import numpy as np
from jax import lax
from jax.experimental import pallas as pl
from jax.experimental.pallas import tpu as pltpu
from jax.sharding import Mesh, PartitionSpec as P

WLAT = 6
WLON = 12
LEVELS = 4
HALF_LAT = WLAT // 2
HALF_LON = WLON // 2
QUARTER = LEVELS * HALF_LAT * HALF_LON
WN = 4 * QUARTER
D = 512
CORNER = (HALF_LAT, HALF_LON, LEVELS, D)
HEADS = 16
HEAD_DIM = D // HEADS
FF = 2048
LANES = 128
PER_GROUP = LANES // HEAD_DIM
GROUPS = HEADS // PER_GROUP
PADDED = 3 * LANES
PIECES = 4
MASKED = -1e30
EPSILON = 1e-05
F32 = jnp.float32
BF16 = jnp.bfloat16
VMEM_LIMIT = 48 * 1024 * 1024
ATTENTION_LIMIT = 32 * 1024 * 1024
STAGE_LIMIT = 48 * 1024 * 1024
TOKENS_LIMIT = 40 * 1024 * 1024

AXES = ("xl", "y", "xh", "z", "c")
SIZES = (2, 8, 2, 8, 2)
LAT = ("xl", "y")
LON = ("xh", "z", "c")


def place(lat, lon):
    return (lat % 16) * 32 + lon % 32


def shifted(dlat, dlon):
    return [(place(a, o), place(a + dlat, o + dlon)) for a in range(16) for o in range(32)]


def mirrored():
    def at(x, y, z, c):
        return (((x % 2) * 8 + y) * 2 + x // 2) * 16 + z * 2 + c

    return [
        (at(x, y, z, c), at(3 - x, y, z, c))
        for x in range(4)
        for y in range(8)
        for z in range(8)
        for c in range(2)
    ]


def to_quarters():
    hot = np.zeros((WN, LEVELS, WLAT, WLON), np.float32)
    place_of = 0
    for i in range(2):
        for j in range(2):
            for row in range(HALF_LAT):
                for col in range(HALF_LON):
                    for lev in range(LEVELS):
                        hot[place_of, lev, i * HALF_LAT + row, j * HALF_LON + col] = 1
                        place_of += 1
    return hot.reshape(WN, WN)


def tags():
    upper = (np.arange(WN) // WLON % WLAT < HALF_LAT).astype(np.float32)
    columns = np.zeros((2, WN, LANES), np.float32)
    columns[0, :, 0], columns[0, :, 1] = upper, 1 - upper
    columns[1, :, 0], columns[1, :, 1] = MASKED * (1 - upper), MASKED * upper
    return columns


def normed(values, gain):
    average = jnp.mean(values, -1, keepdims=True)
    centered = values - average
    variance = jnp.mean(centered * centered, -1, keepdims=True)
    return centered * lax.rsqrt(variance + EPSILON) * gain


def dot(a, b):
    return jnp.dot(a, b, preferred_element_type=F32)


def dot_t(a, b):
    return lax.dot_general(a, b, (((1,), (1,)), ((), ())), preferred_element_type=F32)


def stacked(quarters):
    return jnp.concatenate([q.astype(F32).reshape(QUARTER, D) for q in quarters], 0)


def corner(cells, i, j):
    return cells[i * HALF_LAT : (i + 1) * HALF_LAT, j * HALF_LON : (j + 1) * HALF_LON]


def copy_all(pairs, sems):
    copies = [
        pltpu.make_async_copy(source, target, sems.at[i]) for i, (source, target) in enumerate(pairs)
    ]
    for copy in copies:
        copy.start()
    for copy in copies:
        copy.wait()


def pack_kernel(up_ref, down_ref, proj_ref, cells_ref, c0, c1, c2, c3, own_ref, both_ref, sems):
    parts = ((up_ref, 0, 64), (down_ref, 64, 128), (proj_ref, 128, 144))
    pairs = [(part, own_ref.at[start:stop]) for part, start, stop in parts]
    pairs += [(part, both_ref.at[0, start:stop]) for part, start, stop in parts]
    for i, target in enumerate((c0, c1, c2, c3)):
        lat, lon = HALF_LAT * (i // 2), HALF_LON * (i % 2)
        pairs.append((cells_ref.at[lat : lat + HALF_LAT, lon : lon + HALF_LON], target))
    copy_all(pairs, sems)


def merge_kernel(both_ref, other_ref, out_ref, sems):
    copy_all([(other_ref, out_ref.at[1])], sems)


def attention_kernel(
    spot_ref, r0, r1, r2, r3, mine_ref, other_ref, hot_ref, tags_ref, bias_hbm,
    o0, o1, o2, o3, bias_ref, sems,
):
    fetches = [
        pltpu.make_async_copy(
            bias_hbm.at[g * PER_GROUP : (g + 1) * PER_GROUP],
            bias_ref.at[g * PER_GROUP : (g + 1) * PER_GROUP],
            sems.at[g],
        )
        for g in range(GROUPS)
    ]
    for fetch in fetches:
        fetch.start()
    hot = hot_ref[...]
    rows = stacked([r[...] for r in (r0, r1, r2, r3)]).astype(BF16)
    rows = lax.dot_general(hot, rows, (((0,), (0,)), ((), ())), preferred_element_type=F32)
    rows = rows.astype(BF16)
    low_half = spot_ref[0] == 0
    low, high = rows[:, : D // 2], rows[:, D // 2 :]
    ours, theirs = jnp.where(low_half, low, high), jnp.where(low_half, high, low)

    def projected(which):
        columns = slice(which * D, (which + 1) * D)
        mine = mine_ref[:, :, columns].reshape(D // 2, D)
        other = jnp.stack([other_ref[0, :, :, columns], other_ref[1, :, :, columns]], 1)
        return (dot(ours, mine) + dot(theirs, other.reshape(D // 2, D))).astype(BF16)

    queries, keys, values = projected(0), projected(1), projected(2)
    lane_head = lax.broadcasted_iota(jnp.int32, (1, LANES), 1) // HEAD_DIM
    zero = jnp.zeros((), BF16)
    gap = jnp.zeros((PADDED - WN, 2 * LANES), BF16)
    beyond = jnp.full((WN, PADDED - WN), MASKED, F32)
    query_tags = jnp.where(spot_ref[1] == 1, tags_ref[0], zero)
    key_tags = tags_ref[1]
    groups = []
    for group in range(GROUPS):
        lanes = slice(group * LANES, (group + 1) * LANES)
        group_q = jnp.concatenate([queries[:, lanes], query_tags], 1)
        group_k, group_v = keys[:, lanes], values[:, lanes]
        key_rows, value_rows = [], []
        for j in range(PER_GROUP):
            mine = lane_head == j
            key_rows += [jnp.concatenate([jnp.where(mine, group_k, zero), key_tags], 1), gap]
            sums = jnp.broadcast_to(jnp.where(mine, 1.0, 0.0).astype(BF16), (WN, LANES))
            value_rows += [jnp.concatenate([jnp.where(mine, group_v, zero), sums], 1), gap]
        scores = dot_t(group_q, jnp.concatenate(key_rows, 0))
        fetches[group].wait()
        weights = []
        for j in range(PER_GROUP):
            bias = bias_ref[group * PER_GROUP + j].astype(F32)
            bias = jnp.concatenate([bias, beyond], 1)
            head = scores[:, j * PADDED : (j + 1) * PADDED] * HEAD_DIM ** (-0.5) + bias
            weights.append(jnp.exp(head - jnp.max(head, -1, keepdims=True)).astype(BF16))
        product = dot(jnp.concatenate(weights, 1), jnp.concatenate(value_rows, 0))
        groups.append((product[:, :LANES] / product[:, LANES:]).astype(BF16))
    attended = dot(hot, jnp.concatenate(groups, 1))
    for i, out in enumerate((o0, o1, o2, o3)):
        out[...] = attended[i * QUARTER : (i + 1) * QUARTER].reshape(CORNER).astype(BF16)


def stage_kernel(gathered_ref, wp_ref, wu_ref, wd_ref, sems):
    parts = ((wp_ref, 128, 144), (wu_ref, 0, 64), (wd_ref, 64, 128))
    copy_all([(gathered_ref.at[:, :, start:stop], target) for target, start, stop in parts], sems)


def token_kernel(
    spot_ref, m0, m1, m2, m3, cells_ref, wp, wu, wd, attn_gain_ref, mlp_gain_ref, out_ref
):
    attended = stacked([m[...] for m in (m0, m1, m2, m3)]).astype(BF16)
    cells = stacked([corner(cells_ref, i, j) for i in range(2) for j in range(2)])
    low_half = spot_ref[0] == 0
    low, high = attended[:, : D // 2], attended[:, D // 2 :]
    ours, theirs = jnp.where(low_half, low, high), jnp.where(low_half, high, low)
    projected = dot(ours, wp[:, 0].reshape(D // 2, D)) + dot(theirs, wp[:, 1].reshape(D // 2, D))
    rows = (cells + normed(projected, attn_gain_ref[...])).astype(BF16)
    lowered = None
    step = 16 // PIECES
    units = FF // PIECES
    for i in range(0, 16, step):
        up = wu[i : i + step].reshape(units, D)
        down = wd[i : i + step].reshape(units, D)
        raised = dot_t(rows, up)
        hidden = 0.5 * raised * (1.0 + lax.erf(raised * (0.5**0.5)))
        part = dot(hidden.astype(BF16), down)
        lowered = part if lowered is None else lowered + part
    updated = rows.astype(F32) + normed(lowered, mlp_gain_ref[...])
    run = HALF_LON * LEVELS
    for i in range(2):
        for j in range(2):
            for row in range(HALF_LAT):
                start = (i * 2 + j) * QUARTER + row * run
                piece = updated[start : start + run].reshape(HALF_LON, LEVELS, D)
                out_ref[i * HALF_LAT + row, j * HALF_LON : (j + 1) * HALF_LON] = piece.astype(BF16)


def whole(shape):
    return pl.BlockSpec(shape, lambda i: (0,) * len(shape))


def scalars():
    return pl.BlockSpec(memory_space=pltpu.SMEM)


def held():
    return pl.BlockSpec(memory_space=pltpu.VMEM)


def fetched():
    return pl.BlockSpec(memory_space=pltpu.HBM)


def off_chip(*arrays):
    return [pltpu.with_memory_space_constraint(a, pltpu.HBM) for a in arrays]


def params():
    return pltpu.CompilerParams(vmem_limit_bytes=VMEM_LIMIT)


def packed(up_weight, down_weight, proj_weight, cells):
    out = pl.pallas_call(
        pack_kernel,
        in_specs=[fetched()] * 4,
        out_specs=[held()] * 5 + [fetched()],
        out_shape=[jax.ShapeDtypeStruct(CORNER, BF16)] * 4
        + [jax.ShapeDtypeStruct(shape, BF16) for shape in ((144, D), (2, 144, D))],
        scratch_shapes=[pltpu.SemaphoreType.DMA((10,))],
        compiler_params=params(),
        name="pack",
    )(*off_chip(up_weight, down_weight, proj_weight, cells))
    return out[:4], out[4], out[5]


def merged(both, other):
    return pl.pallas_call(
        merge_kernel,
        in_specs=[fetched(), fetched()],
        out_specs=fetched(),
        out_shape=jax.ShapeDtypeStruct(both.shape, BF16),
        scratch_shapes=[pltpu.SemaphoreType.DMA((1,))],
        input_output_aliases={0: 0},
        compiler_params=params(),
        name="merge",
    )(both, other)


def attention(spot, quarters, mine, other, bias):
    constants = (jnp.asarray(to_quarters(), BF16), jnp.asarray(tags(), BF16))
    return pl.pallas_call(
        attention_kernel,
        in_specs=[scalars()] + [held()] * (len(quarters) + 4) + [fetched()],
        out_specs=[held()] * 4,
        out_shape=[jax.ShapeDtypeStruct(CORNER, BF16)] * 4,
        scratch_shapes=[pltpu.VMEM(bias.shape, BF16), pltpu.SemaphoreType.DMA((GROUPS,))],
        compiler_params=pltpu.CompilerParams(vmem_limit_bytes=ATTENTION_LIMIT),
        name="attention",
    )(spot, *quarters, mine, other, *constants, *off_chip(bias))


def staged(gathered):
    sizes = [(16, 2, rows, D) for rows in (16, 64, 64)]
    return pl.pallas_call(
        stage_kernel,
        in_specs=[fetched()],
        out_specs=[pl.BlockSpec(memory_space=pltpu.VMEM)] * 3,
        out_shape=[jax.ShapeDtypeStruct(size, BF16) for size in sizes],
        scratch_shapes=[pltpu.SemaphoreType.DMA((3,))],
        compiler_params=pltpu.CompilerParams(vmem_limit_bytes=STAGE_LIMIT),
        cost_estimate=pl.CostEstimate(flops=0, bytes_accessed=2 * 144 * 32 * D * 2, transcendentals=0),
        name="stage",
    )(*off_chip(gathered))


def tokens(spot, quarters, cells, weights, attn_gain, mlp_gain):
    out = (WLAT, WLON, LEVELS, D)
    return pl.pallas_call(
        token_kernel,
        grid=(1,),
        in_specs=[scalars()]
        + [whole(CORNER)] * 4
        + [whole(a.shape) for a in (cells, *weights)]
        + [whole((1, D))] * 2,
        out_specs=whole(out),
        out_shape=jax.ShapeDtypeStruct(out, BF16),
        compiler_params=pltpu.CompilerParams(vmem_limit_bytes=TOKENS_LIMIT),
        name="tokens",
    )(
        spot, *quarters, cells, *weights,
        attn_gain.reshape(1, D), mlp_gain.reshape(1, D),
    )


def shards(
    latent, qkv_weight, proj_weight, position_bias, attn_gain, up_weight, down_weight, mlp_gain
):
    cells = latent.transpose(1, 2, 0, 3)
    corners, own, both = packed(up_weight, down_weight, proj_weight, cells)
    both = merged(both, lax.ppermute(own, AXES, mirrored()))
    gathered = lax.all_gather(both, ("z", "c"), axis=0, tiled=False)
    qkv_weight, _ = lax.optimization_barrier((qkv_weight, both))
    mine = lax.all_gather(qkv_weight, ("z", "c"), axis=0, tiled=False)
    corners, mine = lax.optimization_barrier((corners, mine))
    rolled = [
        lax.ppermute(corners[3], AXES, shifted(1, 1)),
        lax.ppermute(corners[2], AXES, shifted(1, 0)),
        lax.ppermute(corners[1], AXES, shifted(0, 1)),
        corners[0],
    ]
    core = lax.axis_index("c")
    sent = lax.dynamic_index_in_dim(mine.reshape(8, 2, 16, 3 * D), core, 1, keepdims=False)
    theirs = lax.all_gather(lax.ppermute(sent, AXES, mirrored()), "c", axis=0, tiled=False)

    spot = jnp.stack([lax.axis_index("xh"), (lax.axis_index(LAT) == 0).astype(jnp.int32)])
    attended = attention(spot, rolled, mine, theirs, position_bias)
    restored = [
        attended[3],
        lax.ppermute(attended[2], AXES, shifted(0, -1)),
        lax.ppermute(attended[1], AXES, shifted(-1, 0)),
        lax.ppermute(attended[0], AXES, shifted(-1, -1)),
    ]
    return tokens(spot, restored, cells, staged(gathered), attn_gain, mlp_gain).transpose(2, 0, 1, 3)


def solution(mesh):
    mesh = Mesh(mesh.devices.reshape(SIZES), AXES)
    placed = (
        P(None, LAT, LON, None),
        P(LON, None),
        P(LON, None),
        P(),
        P(),
        P(LON, None),
        P(LON, None),
        P(),
    )
    return jax.shard_map(
        shards, mesh=mesh, in_specs=placed, out_specs=P(None, LAT, LON, None), check_vma=False
    )
```

```python
import jax
import jax.numpy as jnp
import numpy as np
from jax import lax
from jax.experimental import pallas as pl
from jax.experimental.pallas import tpu as pltpu
from jax.sharding import Mesh, PartitionSpec as P

WLAT = 6
WLON = 12
LEVELS = 4
HALF_LAT = WLAT // 2
HALF_LON = WLON // 2
QUARTER = LEVELS * HALF_LAT * HALF_LON
WN = 4 * QUARTER
D = 512
CORNER = (HALF_LAT, HALF_LON, LEVELS, D)
HEADS = 16
HEAD_DIM = D // HEADS
FF = 2048
LANES = 128
PER_GROUP = LANES // HEAD_DIM
GROUPS = HEADS // PER_GROUP
PADDED = 3 * LANES
PIECES = 4
MASKED = -1e30
EPSILON = 1e-05
F32 = jnp.float32
BF16 = jnp.bfloat16
VMEM_LIMIT = 48 * 1024 * 1024
ATTENTION_LIMIT = 32 * 1024 * 1024
STAGE_LIMIT = 48 * 1024 * 1024
TOKENS_LIMIT = 40 * 1024 * 1024

AXES = ("xl", "y", "xh", "z", "c")
SIZES = (2, 8, 2, 8, 2)
LAT = ("xl", "y")
LON = ("xh", "z", "c")


def place(lat, lon):
    return (lat % 16) * 32 + lon % 32


def shifted(dlat, dlon):
    return [(place(a, o), place(a + dlat, o + dlon)) for a in range(16) for o in range(32)]


def mirrored_pairs():
    def at(x, y, z, c):
        return (((x % 2) * 8 + y) * 2 + x // 2) * 16 + z * 2 + c

    return [
        [at(x, y, z, c), at(3 - x, y, z, c)]
        for x in range(2)
        for y in range(8)
        for z in range(8)
        for c in range(2)
    ]


def mirrored():
    return [pair for a, b in mirrored_pairs() for pair in ((a, b), (b, a))]


def to_quarters():
    hot = np.zeros((WN, LEVELS, WLAT, WLON), np.float32)
    place_of = 0
    for i in range(2):
        for j in range(2):
            for row in range(HALF_LAT):
                for col in range(HALF_LON):
                    for lev in range(LEVELS):
                        hot[place_of, lev, i * HALF_LAT + row, j * HALF_LON + col] = 1
                        place_of += 1
    return hot.reshape(WN, WN)


def tags():
    upper = (np.arange(WN) // WLON % WLAT < HALF_LAT).astype(np.float32)
    columns = np.zeros((2, WN, LANES), np.float32)
    columns[0, :, 0], columns[0, :, 1] = upper, 1 - upper
    columns[1, :, 0], columns[1, :, 1] = MASKED * (1 - upper), MASKED * upper
    return columns


def normed(values, gain):
    average = jnp.mean(values, -1, keepdims=True)
    centered = values - average
    variance = jnp.mean(centered * centered, -1, keepdims=True)
    return centered * lax.rsqrt(variance + EPSILON) * gain


def dot(a, b):
    return jnp.dot(a, b, preferred_element_type=F32)


def dot_t(a, b):
    return lax.dot_general(a, b, (((1,), (1,)), ((), ())), preferred_element_type=F32)


def stacked(quarters):
    return jnp.concatenate([q.astype(F32).reshape(QUARTER, D) for q in quarters], 0)


def corner(cells, i, j):
    return cells[i * HALF_LAT : (i + 1) * HALF_LAT, j * HALF_LON : (j + 1) * HALF_LON]


def copy_all(pairs, sems):
    copies = [
        pltpu.make_async_copy(source, target, sems.at[i]) for i, (source, target) in enumerate(pairs)
    ]
    for copy in copies:
        copy.start()
    for copy in copies:
        copy.wait()


def pack_kernel(up_ref, down_ref, proj_ref, own_ref, sems):
    parts = ((up_ref, 0, 64), (down_ref, 64, 128), (proj_ref, 128, 144))
    copy_all([(part, own_ref.at[start:stop]) for part, start, stop in parts], sems)


def attention_kernel(
    spot_ref, r0, r1, r2, r3, mine_ref, other_ref, hot_ref, tags_ref, bias_hbm,
    o0, o1, o2, o3, bias_ref, sems,
):
    fetches = [
        pltpu.make_async_copy(
            bias_hbm.at[g * PER_GROUP : (g + 1) * PER_GROUP],
            bias_ref.at[g * PER_GROUP : (g + 1) * PER_GROUP],
            sems.at[g],
        )
        for g in range(GROUPS)
    ]
    for fetch in fetches:
        fetch.start()
    hot = hot_ref[...]
    rows = stacked([r[...] for r in (r0, r1, r2, r3)]).astype(BF16)
    rows = lax.dot_general(hot, rows, (((0,), (0,)), ((), ())), preferred_element_type=F32)
    rows = rows.astype(BF16)
    low_half = spot_ref[0] == 0
    low, high = rows[:, : D // 2], rows[:, D // 2 :]
    ours, theirs = jnp.where(low_half, low, high), jnp.where(low_half, high, low)

    def projected(which):
        columns = slice(which * D, (which + 1) * D)
        mine = mine_ref[:, :, columns].reshape(D // 2, D)
        other = jnp.stack([other_ref[0, :, :, columns], other_ref[1, :, :, columns]], 1)
        return (dot(ours, mine) + dot(theirs, other.reshape(D // 2, D))).astype(BF16)

    queries, keys, values = projected(0), projected(1), projected(2)
    lane_head = lax.broadcasted_iota(jnp.int32, (1, LANES), 1) // HEAD_DIM
    zero = jnp.zeros((), BF16)
    gap = jnp.zeros((PADDED - WN, 2 * LANES), BF16)
    beyond = jnp.full((WN, PADDED - WN), MASKED, F32)
    query_tags = jnp.where(spot_ref[1] == 1, tags_ref[0], zero)
    key_tags = tags_ref[1]
    groups = []
    for group in range(GROUPS):
        lanes = slice(group * LANES, (group + 1) * LANES)
        group_q = jnp.concatenate([queries[:, lanes], query_tags], 1)
        group_k, group_v = keys[:, lanes], values[:, lanes]
        key_rows, value_rows = [], []
        for j in range(PER_GROUP):
            mine = lane_head == j
            key_rows += [jnp.concatenate([jnp.where(mine, group_k, zero), key_tags], 1), gap]
            sums = jnp.broadcast_to(jnp.where(mine, 1.0, 0.0).astype(BF16), (WN, LANES))
            value_rows += [jnp.concatenate([jnp.where(mine, group_v, zero), sums], 1), gap]
        scores = dot_t(group_q, jnp.concatenate(key_rows, 0))
        fetches[group].wait()
        weights = []
        for j in range(PER_GROUP):
            bias = bias_ref[group * PER_GROUP + j].astype(F32)
            bias = jnp.concatenate([bias, beyond], 1)
            head = scores[:, j * PADDED : (j + 1) * PADDED] * HEAD_DIM ** (-0.5) + bias
            weights.append(jnp.exp(head - jnp.max(head, -1, keepdims=True)).astype(BF16))
        product = dot(jnp.concatenate(weights, 1), jnp.concatenate(value_rows, 0))
        groups.append((product[:, :LANES] / product[:, LANES:]).astype(BF16))
    attended = dot(hot, jnp.concatenate(groups, 1))
    for i, out in enumerate((o0, o1, o2, o3)):
        out[...] = attended[i * QUARTER : (i + 1) * QUARTER].reshape(CORNER).astype(BF16)


def stage_kernel(gathered_ref, wp_ref, wu_ref, wd_ref, sems):
    parts = ((wp_ref, 128, 144), (wu_ref, 0, 64), (wd_ref, 64, 128))
    copy_all([(gathered_ref.at[:, :, start:stop], target) for target, start, stop in parts], sems)


def token_kernel(
    m0, m1, m2, m3, cells_ref, wp, wu, wd, attn_gain_ref, mlp_gain_ref, out_ref
):
    attended = stacked([m[...] for m in (m0, m1, m2, m3)]).astype(BF16)
    cells = stacked([corner(cells_ref, i, j) for i in range(2) for j in range(2)])
    low = dot(attended[:, : D // 2], wp[:, 0].reshape(D // 2, D))
    projected = low + dot(attended[:, D // 2 :], wp[:, 1].reshape(D // 2, D))
    rows = (cells + normed(projected, attn_gain_ref[...])).astype(BF16)
    lowered = None
    step = 16 // PIECES
    units = FF // PIECES
    for i in range(0, 16, step):
        up = wu[i : i + step].reshape(units, D)
        down = wd[i : i + step].reshape(units, D)
        raised = dot_t(rows, up)
        hidden = 0.5 * raised * (1.0 + lax.erf(raised * (0.5**0.5)))
        part = dot(hidden.astype(BF16), down)
        lowered = part if lowered is None else lowered + part
    updated = rows.astype(F32) + normed(lowered, mlp_gain_ref[...])
    run = HALF_LON * LEVELS
    for i in range(2):
        for j in range(2):
            for row in range(HALF_LAT):
                start = (i * 2 + j) * QUARTER + row * run
                piece = updated[start : start + run].reshape(HALF_LON, LEVELS, D)
                out_ref[i * HALF_LAT + row, j * HALF_LON : (j + 1) * HALF_LON] = piece.astype(BF16)


def whole(shape):
    return pl.BlockSpec(shape, lambda i: (0,) * len(shape))


def scalars():
    return pl.BlockSpec(memory_space=pltpu.SMEM)


def held():
    return pl.BlockSpec(memory_space=pltpu.VMEM)


def fetched():
    return pl.BlockSpec(memory_space=pltpu.HBM)


def off_chip(*arrays):
    return [pltpu.with_memory_space_constraint(a, pltpu.HBM) for a in arrays]


def params():
    return pltpu.CompilerParams(vmem_limit_bytes=VMEM_LIMIT)


def packed(up_weight, down_weight, proj_weight):
    return pl.pallas_call(
        pack_kernel,
        in_specs=[fetched()] * 3,
        out_specs=held(),
        out_shape=jax.ShapeDtypeStruct((144, D), BF16),
        scratch_shapes=[pltpu.SemaphoreType.DMA((3,))],
        compiler_params=params(),
        name="pack",
    )(*off_chip(up_weight, down_weight, proj_weight))


def attention(spot, quarters, mine, other, bias):
    constants = (jnp.asarray(to_quarters(), BF16), jnp.asarray(tags(), BF16))
    return pl.pallas_call(
        attention_kernel,
        in_specs=[scalars()] + [held()] * (len(quarters) + 4) + [fetched()],
        out_specs=[held()] * 4,
        out_shape=[jax.ShapeDtypeStruct(CORNER, BF16)] * 4,
        scratch_shapes=[pltpu.VMEM(bias.shape, BF16), pltpu.SemaphoreType.DMA((GROUPS,))],
        compiler_params=pltpu.CompilerParams(vmem_limit_bytes=ATTENTION_LIMIT),
        name="attention",
    )(spot, *quarters, mine, other, *constants, *off_chip(bias))


def staged(gathered):
    sizes = [(16, 2, rows, D) for rows in (16, 64, 64)]
    return pl.pallas_call(
        stage_kernel,
        in_specs=[fetched()],
        out_specs=[pl.BlockSpec(memory_space=pltpu.VMEM)] * 3,
        out_shape=[jax.ShapeDtypeStruct(size, BF16) for size in sizes],
        scratch_shapes=[pltpu.SemaphoreType.DMA((3,))],
        compiler_params=pltpu.CompilerParams(vmem_limit_bytes=STAGE_LIMIT),
        cost_estimate=pl.CostEstimate(flops=0, bytes_accessed=2 * 144 * 32 * D * 2, transcendentals=0),
        name="stage",
    )(*off_chip(gathered))


def tokens(quarters, cells, weights, attn_gain, mlp_gain):
    out = (WLAT, WLON, LEVELS, D)
    return pl.pallas_call(
        token_kernel,
        grid=(1,),
        in_specs=[whole(CORNER)] * 4
        + [whole(a.shape) for a in (cells, *weights)]
        + [whole((1, D))] * 2,
        out_specs=whole(out),
        out_shape=jax.ShapeDtypeStruct(out, BF16),
        compiler_params=pltpu.CompilerParams(vmem_limit_bytes=TOKENS_LIMIT),
        name="tokens",
    )(*quarters, cells, *weights, attn_gain.reshape(1, D), mlp_gain.reshape(1, D))


def shards(
    latent, qkv_weight, proj_weight, position_bias, attn_gain, up_weight, down_weight, mlp_gain
):
    own = packed(up_weight, down_weight, proj_weight)
    both = lax.all_gather(own, AXES, axis=0, tiled=False, axis_index_groups=mirrored_pairs())
    gathered = lax.all_gather(both, ("z", "c"), axis=0, tiled=False)
    qkv_weight, _ = lax.optimization_barrier((qkv_weight, both))
    mine = lax.all_gather(qkv_weight, ("z", "c"), axis=0, tiled=False)
    cells = latent.transpose(1, 2, 0, 3)
    cells_after, mine = lax.optimization_barrier((cells, mine))
    rolled = [
        lax.ppermute(corner(cells_after, 1, 1), AXES, shifted(1, 1)),
        lax.ppermute(corner(cells_after, 1, 0), AXES, shifted(1, 0)),
        lax.ppermute(corner(cells_after, 0, 1), AXES, shifted(0, 1)),
        corner(cells_after, 0, 0),
    ]
    core = lax.axis_index("c")
    sent = lax.dynamic_index_in_dim(mine.reshape(8, 2, 16, 3 * D), core, 1, keepdims=False)
    theirs = lax.all_gather(lax.ppermute(sent, AXES, mirrored()), "c", axis=0, tiled=False)

    spot = jnp.stack([lax.axis_index("xh"), (lax.axis_index(LAT) == 0).astype(jnp.int32)])
    attended = attention(spot, rolled, mine, theirs, position_bias)
    restored = [
        attended[3],
        lax.ppermute(attended[2], AXES, shifted(0, -1)),
        lax.ppermute(attended[1], AXES, shifted(-1, 0)),
        lax.ppermute(attended[0], AXES, shifted(-1, -1)),
    ]
    return tokens(restored, cells, staged(gathered), attn_gain, mlp_gain).transpose(2, 0, 1, 3)


def solution(mesh):
    mesh = Mesh(mesh.devices.reshape(SIZES), AXES)
    placed = (
        P(None, LAT, LON, None),
        P(LON, None),
        P(LON, None),
        P(),
        P(),
        P(LON, None),
        P(LON, None),
        P(),
    )
    return jax.shard_map(
        shards, mesh=mesh, in_specs=placed, out_specs=P(None, LAT, LON, None), check_vma=False
    )
```

```python
import jax
import jax.numpy as jnp
import numpy as np
from jax import lax
from jax.experimental import pallas as pl
from jax.experimental.pallas import tpu as pltpu
from jax.sharding import Mesh, PartitionSpec as P

WLAT = 6
WLON = 12
LEVELS = 4
HALF_LAT = WLAT // 2
HALF_LON = WLON // 2
QUARTER = LEVELS * HALF_LAT * HALF_LON
WN = 4 * QUARTER
D = 512
CORNER = (HALF_LAT, HALF_LON, LEVELS, D)
HEADS = 16
HEAD_DIM = D // HEADS
FF = 2048
LANES = 128
PER_GROUP = LANES // HEAD_DIM
GROUPS = HEADS // PER_GROUP
PADDED = 3 * LANES
PIECES = 4
MASKED = -1e30
EPSILON = 1e-05
F32 = jnp.float32
BF16 = jnp.bfloat16
VMEM_LIMIT = 8 * 1024 * 1024
ATTENTION_LIMIT = 32 * 1024 * 1024
STAGE_LIMIT = 48 * 1024 * 1024
TOKENS_LIMIT = 40 * 1024 * 1024

AXES = ("xl", "y", "xh", "z", "c")
SIZES = (2, 8, 2, 8, 2)
LAT = ("xl", "y")
LON = ("xh", "z", "c")


def place(lat, lon):
    return (lat % 16) * 32 + lon % 32


def shifted(dlat, dlon):
    return [(place(a, o), place(a + dlat, o + dlon)) for a in range(16) for o in range(32)]


def mirrored_pairs():
    def at(x, y, z, c):
        return (((x % 2) * 8 + y) * 2 + x // 2) * 16 + z * 2 + c

    return [
        [at(x, y, z, c), at(3 - x, y, z, c)]
        for x in range(2)
        for y in range(8)
        for z in range(8)
        for c in range(2)
    ]


def mirrored():
    return [pair for a, b in mirrored_pairs() for pair in ((a, b), (b, a))]


def to_quarters():
    hot = np.zeros((WN, LEVELS, WLAT, WLON), np.float32)
    place_of = 0
    for i in range(2):
        for j in range(2):
            for row in range(HALF_LAT):
                for col in range(HALF_LON):
                    for lev in range(LEVELS):
                        hot[place_of, lev, i * HALF_LAT + row, j * HALF_LON + col] = 1
                        place_of += 1
    return hot.reshape(WN, WN)


def tags():
    upper = (np.arange(WN) // WLON % WLAT < HALF_LAT).astype(np.float32)
    columns = np.zeros((2, WN, LANES), np.float32)
    columns[0, :, 0], columns[0, :, 1] = upper, 1 - upper
    columns[1, :, 0], columns[1, :, 1] = MASKED * (1 - upper), MASKED * upper
    return columns


def normed(values, gain):
    average = jnp.mean(values, -1, keepdims=True)
    centered = values - average
    variance = jnp.mean(centered * centered, -1, keepdims=True)
    return centered * lax.rsqrt(variance + EPSILON) * gain


def dot(a, b):
    return jnp.dot(a, b, preferred_element_type=F32)


def dot_t(a, b):
    return lax.dot_general(a, b, (((1,), (1,)), ((), ())), preferred_element_type=F32)


def stacked(quarters):
    return jnp.concatenate([q.astype(F32).reshape(QUARTER, D) for q in quarters], 0)


def corner(cells, i, j):
    return cells[i * HALF_LAT : (i + 1) * HALF_LAT, j * HALF_LON : (j + 1) * HALF_LON]


def copy_all(pairs, sems):
    copies = [
        pltpu.make_async_copy(source, target, sems.at[i]) for i, (source, target) in enumerate(pairs)
    ]
    for copy in copies:
        copy.start()
    for copy in copies:
        copy.wait()


def pack_kernel(up_ref, down_ref, proj_ref, own_ref, sems):
    parts = ((up_ref, 0, 64), (down_ref, 64, 128), (proj_ref, 128, 144))
    copy_all([(part, own_ref.at[start:stop]) for part, start, stop in parts], sems)


def bias_kernel(bias_hbm, bias_ref, sems):
    copy_all([(bias_hbm, bias_ref)], sems)


def attention_kernel(
    spot_ref, r0, r1, r2, r3, mine_ref, other_ref, hot_ref, tags_ref, bias_ref, o0, o1, o2, o3
):
    hot = hot_ref[...]
    rows = stacked([r[...] for r in (r0, r1, r2, r3)]).astype(BF16)
    rows = lax.dot_general(hot, rows, (((0,), (0,)), ((), ())), preferred_element_type=F32)
    rows = rows.astype(BF16)
    low_half = spot_ref[0] == 0
    low, high = rows[:, : D // 2], rows[:, D // 2 :]
    ours, theirs = jnp.where(low_half, low, high), jnp.where(low_half, high, low)

    def projected(which):
        columns = slice(which * D, (which + 1) * D)
        mine = mine_ref[:, :, columns].reshape(D // 2, D)
        other = jnp.stack([other_ref[0, :, :, columns], other_ref[1, :, :, columns]], 1)
        return (dot(ours, mine) + dot(theirs, other.reshape(D // 2, D))).astype(BF16)

    queries, keys, values = projected(0), projected(1), projected(2)
    lane_head = lax.broadcasted_iota(jnp.int32, (1, LANES), 1) // HEAD_DIM
    zero = jnp.zeros((), BF16)
    gap = jnp.zeros((PADDED - WN, 2 * LANES), BF16)
    beyond = jnp.full((WN, PADDED - WN), MASKED, F32)
    query_tags = jnp.where(spot_ref[1] == 1, tags_ref[0], zero)
    key_tags = tags_ref[1]
    groups = []
    for group in range(GROUPS):
        lanes = slice(group * LANES, (group + 1) * LANES)
        group_q = jnp.concatenate([queries[:, lanes], query_tags], 1)
        group_k, group_v = keys[:, lanes], values[:, lanes]
        key_rows, value_rows = [], []
        for j in range(PER_GROUP):
            mine = lane_head == j
            key_rows += [jnp.concatenate([jnp.where(mine, group_k, zero), key_tags], 1), gap]
            sums = jnp.broadcast_to(jnp.where(mine, 1.0, 0.0).astype(BF16), (WN, LANES))
            value_rows += [jnp.concatenate([jnp.where(mine, group_v, zero), sums], 1), gap]
        scores = dot_t(group_q, jnp.concatenate(key_rows, 0))
        weights = []
        for j in range(PER_GROUP):
            bias = bias_ref[group * PER_GROUP + j].astype(F32)
            bias = jnp.concatenate([bias, beyond], 1)
            head = scores[:, j * PADDED : (j + 1) * PADDED] * HEAD_DIM ** (-0.5) + bias
            weights.append(jnp.exp(head - jnp.max(head, -1, keepdims=True)).astype(BF16))
        product = dot(jnp.concatenate(weights, 1), jnp.concatenate(value_rows, 0))
        groups.append((product[:, :LANES] / product[:, LANES:]).astype(BF16))
    attended = dot(hot, jnp.concatenate(groups, 1))
    for i, out in enumerate((o0, o1, o2, o3)):
        out[...] = attended[i * QUARTER : (i + 1) * QUARTER].reshape(CORNER).astype(BF16)


def stage_kernel(gathered_ref, wp_ref, wu_ref, wd_ref, sems):
    parts = ((wp_ref, 128, 144), (wu_ref, 0, 64), (wd_ref, 64, 128))
    copy_all([(gathered_ref.at[:, :, start:stop], target) for target, start, stop in parts], sems)


def token_kernel(
    m0, m1, m2, m3, cells_ref, wp, wu, wd, attn_gain_ref, mlp_gain_ref, out_ref
):
    attended = stacked([m[...] for m in (m0, m1, m2, m3)]).astype(BF16)
    cells = stacked([corner(cells_ref, i, j) for i in range(2) for j in range(2)])
    low = dot(attended[:, : D // 2], wp[:, 0].reshape(D // 2, D))
    projected = low + dot(attended[:, D // 2 :], wp[:, 1].reshape(D // 2, D))
    rows = (cells + normed(projected, attn_gain_ref[...])).astype(BF16)
    lowered = None
    step = 16 // PIECES
    units = FF // PIECES
    for i in range(0, 16, step):
        up = wu[i : i + step].reshape(units, D)
        down = wd[i : i + step].reshape(units, D)
        raised = dot_t(rows, up)
        hidden = 0.5 * raised * (1.0 + lax.erf(raised * (0.5**0.5)))
        part = dot(hidden.astype(BF16), down)
        lowered = part if lowered is None else lowered + part
    updated = rows.astype(F32) + normed(lowered, mlp_gain_ref[...])
    run = HALF_LON * LEVELS
    for i in range(2):
        for j in range(2):
            for row in range(HALF_LAT):
                start = (i * 2 + j) * QUARTER + row * run
                piece = updated[start : start + run].reshape(HALF_LON, LEVELS, D)
                out_ref[i * HALF_LAT + row, j * HALF_LON : (j + 1) * HALF_LON] = piece.astype(BF16)


def whole(shape):
    return pl.BlockSpec(shape, lambda i: (0,) * len(shape))


def scalars():
    return pl.BlockSpec(memory_space=pltpu.SMEM)


def held():
    return pl.BlockSpec(memory_space=pltpu.VMEM)


def fetched():
    return pl.BlockSpec(memory_space=pltpu.HBM)


def off_chip(*arrays):
    return [pltpu.with_memory_space_constraint(a, pltpu.HBM) for a in arrays]


def params():
    return pltpu.CompilerParams(vmem_limit_bytes=VMEM_LIMIT)


def packed(up_weight, down_weight, proj_weight):
    return pl.pallas_call(
        pack_kernel,
        in_specs=[fetched()] * 3,
        out_specs=held(),
        out_shape=jax.ShapeDtypeStruct((144, D), BF16),
        scratch_shapes=[pltpu.SemaphoreType.DMA((3,))],
        compiler_params=params(),
        name="pack",
    )(*off_chip(up_weight, down_weight, proj_weight))


def held_bias(bias):
    return pl.pallas_call(
        bias_kernel,
        in_specs=[fetched()],
        out_specs=held(),
        out_shape=jax.ShapeDtypeStruct(bias.shape, BF16),
        scratch_shapes=[pltpu.SemaphoreType.DMA((1,))],
        compiler_params=params(),
        cost_estimate=pl.CostEstimate(flops=0, bytes_accessed=2 * bias.size * 2, transcendentals=0),
        name="bias",
    )(*off_chip(bias))


def attention(spot, quarters, mine, other, bias):
    constants = (jnp.asarray(to_quarters(), BF16), jnp.asarray(tags(), BF16))
    return pl.pallas_call(
        attention_kernel,
        in_specs=[scalars()] + [held()] * (len(quarters) + 5),
        out_specs=[held()] * 4,
        out_shape=[jax.ShapeDtypeStruct(CORNER, BF16)] * 4,
        compiler_params=pltpu.CompilerParams(vmem_limit_bytes=ATTENTION_LIMIT),
        name="attention",
    )(spot, *quarters, mine, other, *constants, bias)


def staged(gathered):
    sizes = [(16, 2, rows, D) for rows in (16, 64, 64)]
    return pl.pallas_call(
        stage_kernel,
        in_specs=[fetched()],
        out_specs=[pl.BlockSpec(memory_space=pltpu.VMEM)] * 3,
        out_shape=[jax.ShapeDtypeStruct(size, BF16) for size in sizes],
        scratch_shapes=[pltpu.SemaphoreType.DMA((3,))],
        compiler_params=pltpu.CompilerParams(vmem_limit_bytes=STAGE_LIMIT),
        cost_estimate=pl.CostEstimate(flops=0, bytes_accessed=2 * 144 * 32 * D * 2, transcendentals=0),
        name="stage",
    )(*off_chip(gathered))


def tokens(quarters, cells, weights, attn_gain, mlp_gain):
    out = (WLAT, WLON, LEVELS, D)
    return pl.pallas_call(
        token_kernel,
        grid=(1,),
        in_specs=[whole(CORNER)] * 4
        + [whole(a.shape) for a in (cells, *weights)]
        + [whole((1, D))] * 2,
        out_specs=whole(out),
        out_shape=jax.ShapeDtypeStruct(out, BF16),
        compiler_params=pltpu.CompilerParams(vmem_limit_bytes=TOKENS_LIMIT),
        name="tokens",
    )(*quarters, cells, *weights, attn_gain.reshape(1, D), mlp_gain.reshape(1, D))


def shards(
    latent, qkv_weight, proj_weight, position_bias, attn_gain, up_weight, down_weight, mlp_gain
):
    own = packed(up_weight, down_weight, proj_weight)
    both = lax.all_gather(own, AXES, axis=0, tiled=False, axis_index_groups=mirrored_pairs())
    gathered = lax.all_gather(both, ("z", "c"), axis=0, tiled=False)
    qkv_weight, _ = lax.optimization_barrier((qkv_weight, both))
    mine = lax.all_gather(qkv_weight, ("z", "c"), axis=0, tiled=False)
    cells = latent.transpose(1, 2, 0, 3)
    cells_after, bias, mine = lax.optimization_barrier((cells, position_bias, mine))
    rolled = [
        lax.ppermute(corner(cells_after, 1, 1), AXES, shifted(1, 1)),
        lax.ppermute(corner(cells_after, 1, 0), AXES, shifted(1, 0)),
        lax.ppermute(corner(cells_after, 0, 1), AXES, shifted(0, 1)),
        corner(cells_after, 0, 0),
    ]
    core = lax.axis_index("c")
    sent = lax.dynamic_index_in_dim(mine.reshape(8, 2, 16, 3 * D), core, 1, keepdims=False)
    theirs = lax.all_gather(lax.ppermute(sent, AXES, mirrored()), "c", axis=0, tiled=False)

    spot = jnp.stack([lax.axis_index("xh"), (lax.axis_index(LAT) == 0).astype(jnp.int32)])
    attended = attention(spot, rolled, mine, theirs, held_bias(bias))
    restored = [
        attended[3],
        lax.ppermute(attended[2], AXES, shifted(0, -1)),
        lax.ppermute(attended[1], AXES, shifted(-1, 0)),
        lax.ppermute(attended[0], AXES, shifted(-1, -1)),
    ]
    return tokens(restored, cells, staged(gathered), attn_gain, mlp_gain).transpose(2, 0, 1, 3)


def solution(mesh):
    mesh = Mesh(mesh.devices.reshape(SIZES), AXES)
    placed = (
        P(None, LAT, LON, None),
        P(LON, None),
        P(LON, None),
        P(),
        P(),
        P(LON, None),
        P(LON, None),
        P(),
    )
    return jax.shard_map(
        shards, mesh=mesh, in_specs=placed, out_specs=P(None, LAT, LON, None), check_vma=False
    )
```

```python
import jax
import jax.numpy as jnp
import numpy as np
from jax import lax
from jax.experimental import pallas as pl
from jax.experimental.pallas import tpu as pltpu
from jax.sharding import Mesh, PartitionSpec as P

WLAT = 6
WLON = 12
LEVELS = 4
HALF_LAT = WLAT // 2
HALF_LON = WLON // 2
QUARTER = LEVELS * HALF_LAT * HALF_LON
WN = 4 * QUARTER
D = 512
CORNER = (HALF_LAT, HALF_LON, LEVELS, D)
HEADS = 16
HEAD_DIM = D // HEADS
FF = 2048
LANES = 128
PER_GROUP = LANES // HEAD_DIM
GROUPS = HEADS // PER_GROUP
PADDED = 3 * LANES
PIECES = 4
MASKED = -1e30
EPSILON = 1e-05
F32 = jnp.float32
BF16 = jnp.bfloat16
VMEM_LIMIT = 8 * 1024 * 1024
ATTENTION_LIMIT = 32 * 1024 * 1024
STAGE_LIMIT = 48 * 1024 * 1024
TOKENS_LIMIT = 40 * 1024 * 1024

AXES = ("xl", "y", "xh", "z", "c")
SIZES = (2, 8, 2, 8, 2)
LAT = ("xl", "y")
LON = ("xh", "z", "c")


def place(lat, lon):
    return (lat % 16) * 32 + lon % 32


def shifted(dlat, dlon):
    return [(place(a, o), place(a + dlat, o + dlon)) for a in range(16) for o in range(32)]


def mirrored_pairs():
    def at(x, y, z, c):
        return (((x % 2) * 8 + y) * 2 + x // 2) * 16 + z * 2 + c

    return [
        [at(x, y, z, c), at(3 - x, y, z, c)]
        for x in range(2)
        for y in range(8)
        for z in range(8)
        for c in range(2)
    ]


def mirrored():
    return [pair for a, b in mirrored_pairs() for pair in ((a, b), (b, a))]


def to_quarters():
    hot = np.zeros((WN, LEVELS, WLAT, WLON), np.float32)
    place_of = 0
    for i in range(2):
        for j in range(2):
            for row in range(HALF_LAT):
                for col in range(HALF_LON):
                    for lev in range(LEVELS):
                        hot[place_of, lev, i * HALF_LAT + row, j * HALF_LON + col] = 1
                        place_of += 1
    return hot.reshape(WN, WN)


def tags():
    upper = (np.arange(WN) // WLON % WLAT < HALF_LAT).astype(np.float32)
    columns = np.zeros((2, WN, LANES), np.float32)
    columns[0, :, 0], columns[0, :, 1] = upper, 1 - upper
    columns[1, :, 0], columns[1, :, 1] = MASKED * (1 - upper), MASKED * upper
    return columns


def normed(values, gain):
    average = jnp.mean(values, -1, keepdims=True)
    centered = values - average
    variance = jnp.mean(centered * centered, -1, keepdims=True)
    return centered * lax.rsqrt(variance + EPSILON) * gain


def dot(a, b):
    return jnp.dot(a, b, preferred_element_type=F32)


def dot_t(a, b):
    return lax.dot_general(a, b, (((1,), (1,)), ((), ())), preferred_element_type=F32)


def stacked(quarters):
    return jnp.concatenate([q.astype(F32).reshape(QUARTER, D) for q in quarters], 0)


def corner(cells, i, j):
    return cells[i * HALF_LAT : (i + 1) * HALF_LAT, j * HALF_LON : (j + 1) * HALF_LON]


def copy_all(pairs, sems):
    copies = [
        pltpu.make_async_copy(source, target, sems.at[i]) for i, (source, target) in enumerate(pairs)
    ]
    for copy in copies:
        copy.start()
    for copy in copies:
        copy.wait()


def pack_kernel(up_ref, down_ref, proj_ref, own_ref, sems):
    parts = ((up_ref, 0, 64), (down_ref, 64, 128), (proj_ref, 128, 144))
    copy_all([(part, own_ref.at[start:stop]) for part, start, stop in parts], sems)


def bias_kernel(bias_hbm, bias_ref, sems):
    copy_all([(bias_hbm, bias_ref)], sems)


def attention_kernel(
    spot_ref, r0, r1, r2, r3, mine_ref, other_ref, hot_ref, tags_ref, bias_ref, o0, o1, o2, o3
):
    hot = hot_ref[...]
    rows = stacked([r[...] for r in (r0, r1, r2, r3)]).astype(BF16)
    rows = lax.dot_general(hot, rows, (((0,), (0,)), ((), ())), preferred_element_type=F32)
    rows = rows.astype(BF16)
    low_half = spot_ref[0] == 0
    low, high = rows[:, : D // 2], rows[:, D // 2 :]
    ours, theirs = jnp.where(low_half, low, high), jnp.where(low_half, high, low)

    def projected(which):
        columns = slice(which * D, (which + 1) * D)
        mine = mine_ref[:, :, columns].reshape(D // 2, D)
        other = jnp.stack([other_ref[0, :, :, columns], other_ref[1, :, :, columns]], 1)
        return (dot(ours, mine) + dot(theirs, other.reshape(D // 2, D))).astype(BF16)

    queries, keys, values = projected(0), projected(1), projected(2)
    lane_head = lax.broadcasted_iota(jnp.int32, (1, LANES), 1) // HEAD_DIM
    zero = jnp.zeros((), BF16)
    gap = jnp.zeros((PADDED - WN, 2 * LANES), BF16)
    beyond = jnp.full((WN, PADDED - WN), MASKED, F32)
    query_tags = jnp.where(spot_ref[1] == 1, tags_ref[0], zero)
    key_tags = tags_ref[1]
    groups = []
    for group in range(GROUPS):
        lanes = slice(group * LANES, (group + 1) * LANES)
        group_q = jnp.concatenate([queries[:, lanes], query_tags], 1)
        group_k, group_v = keys[:, lanes], values[:, lanes]
        key_rows, value_rows = [], []
        for j in range(PER_GROUP):
            mine = lane_head == j
            key_rows += [jnp.concatenate([jnp.where(mine, group_k, zero), key_tags], 1), gap]
            sums = jnp.broadcast_to(jnp.where(mine, 1.0, 0.0).astype(BF16), (WN, LANES))
            value_rows += [jnp.concatenate([jnp.where(mine, group_v, zero), sums], 1), gap]
        scores = dot_t(group_q, jnp.concatenate(key_rows, 0))
        weights = []
        for j in range(PER_GROUP):
            bias = bias_ref[group * PER_GROUP + j].astype(F32)
            bias = jnp.concatenate([bias, beyond], 1)
            head = scores[:, j * PADDED : (j + 1) * PADDED] * HEAD_DIM ** (-0.5) + bias
            weights.append(jnp.exp(head - jnp.max(head, -1, keepdims=True)).astype(BF16))
        product = dot(jnp.concatenate(weights, 1), jnp.concatenate(value_rows, 0))
        groups.append((product[:, :LANES] / product[:, LANES:]).astype(BF16))
    attended = dot(hot, jnp.concatenate(groups, 1))
    for i, out in enumerate((o0, o1, o2, o3)):
        out[...] = attended[i * QUARTER : (i + 1) * QUARTER].reshape(CORNER).astype(BF16)


def stage_kernel(gathered_ref, wp_ref, wu_ref, wd_ref, sems):
    parts = ((wp_ref, 128, 144), (wu_ref, 0, 64), (wd_ref, 64, 128))
    copy_all([(gathered_ref.at[:, :, start:stop], target) for target, start, stop in parts], sems)


def token_kernel(
    m3, m2, m1, m0, cells_ref, wp, wu, wd, attn_gain_ref, mlp_gain_ref, out_ref
):
    attended = stacked([m[...] for m in (m0, m1, m2, m3)]).astype(BF16)
    cells = stacked([corner(cells_ref, i, j) for i in range(2) for j in range(2)])
    low = dot(attended[:, : D // 2], wp[:, 0].reshape(D // 2, D))
    projected = low + dot(attended[:, D // 2 :], wp[:, 1].reshape(D // 2, D))
    rows = (cells + normed(projected, attn_gain_ref[...])).astype(BF16)
    lowered = None
    step = 16 // PIECES
    units = FF // PIECES
    for i in range(0, 16, step):
        up = wu[i : i + step].reshape(units, D)
        down = wd[i : i + step].reshape(units, D)
        raised = dot_t(rows, up)
        hidden = 0.5 * raised * (1.0 + lax.erf(raised * (0.5**0.5)))
        part = dot(hidden.astype(BF16), down)
        lowered = part if lowered is None else lowered + part
    updated = rows.astype(F32) + normed(lowered, mlp_gain_ref[...])
    run = HALF_LON * LEVELS
    for i in range(2):
        for j in range(2):
            for row in range(HALF_LAT):
                start = (i * 2 + j) * QUARTER + row * run
                piece = updated[start : start + run].reshape(HALF_LON, LEVELS, D)
                out_ref[i * HALF_LAT + row, j * HALF_LON : (j + 1) * HALF_LON] = piece.astype(BF16)


def whole(shape):
    return pl.BlockSpec(shape, lambda i: (0,) * len(shape))


def scalars():
    return pl.BlockSpec(memory_space=pltpu.SMEM)


def held():
    return pl.BlockSpec(memory_space=pltpu.VMEM)


def fetched():
    return pl.BlockSpec(memory_space=pltpu.HBM)


def off_chip(*arrays):
    return [pltpu.with_memory_space_constraint(a, pltpu.HBM) for a in arrays]


def params():
    return pltpu.CompilerParams(vmem_limit_bytes=VMEM_LIMIT)


def packed(up_weight, down_weight, proj_weight):
    return pl.pallas_call(
        pack_kernel,
        in_specs=[fetched()] * 3,
        out_specs=held(),
        out_shape=jax.ShapeDtypeStruct((144, D), BF16),
        scratch_shapes=[pltpu.SemaphoreType.DMA((3,))],
        compiler_params=params(),
        name="pack",
    )(*off_chip(up_weight, down_weight, proj_weight))


def held_bias(bias):
    return pl.pallas_call(
        bias_kernel,
        in_specs=[fetched()],
        out_specs=held(),
        out_shape=jax.ShapeDtypeStruct(bias.shape, BF16),
        scratch_shapes=[pltpu.SemaphoreType.DMA((1,))],
        compiler_params=params(),
        cost_estimate=pl.CostEstimate(flops=0, bytes_accessed=2 * bias.size * 2, transcendentals=0),
        name="bias",
    )(*off_chip(bias))


def attention(spot, quarters, mine, other, bias):
    constants = (jnp.asarray(to_quarters(), BF16), jnp.asarray(tags(), BF16))
    return pl.pallas_call(
        attention_kernel,
        in_specs=[scalars()] + [held()] * (len(quarters) + 5),
        out_specs=[held()] * 4,
        out_shape=[jax.ShapeDtypeStruct(CORNER, BF16)] * 4,
        compiler_params=pltpu.CompilerParams(vmem_limit_bytes=ATTENTION_LIMIT),
        name="attention",
    )(spot, *quarters, mine, other, *constants, bias)


def staged(gathered):
    sizes = [(16, 2, rows, D) for rows in (16, 64, 64)]
    return pl.pallas_call(
        stage_kernel,
        in_specs=[fetched()],
        out_specs=[pl.BlockSpec(memory_space=pltpu.VMEM)] * 3,
        out_shape=[jax.ShapeDtypeStruct(size, BF16) for size in sizes],
        scratch_shapes=[pltpu.SemaphoreType.DMA((3,))],
        compiler_params=pltpu.CompilerParams(vmem_limit_bytes=STAGE_LIMIT),
        cost_estimate=pl.CostEstimate(flops=0, bytes_accessed=2 * 144 * 32 * D * 2, transcendentals=0),
        name="stage",
    )(*off_chip(gathered))


def tokens(quarters, cells, weights, attn_gain, mlp_gain):
    out = (WLAT, WLON, LEVELS, D)
    return pl.pallas_call(
        token_kernel,
        grid=(1,),
        in_specs=[whole(CORNER)] * 4
        + [whole(a.shape) for a in (cells, *weights)]
        + [whole((1, D))] * 2,
        out_specs=whole(out),
        out_shape=jax.ShapeDtypeStruct(out, BF16),
        compiler_params=pltpu.CompilerParams(vmem_limit_bytes=TOKENS_LIMIT),
        name="tokens",
    )(*quarters, cells, *weights, attn_gain.reshape(1, D), mlp_gain.reshape(1, D))


def shards(
    latent, qkv_weight, proj_weight, position_bias, attn_gain, up_weight, down_weight, mlp_gain
):
    own = packed(up_weight, down_weight, proj_weight)
    both = lax.all_gather(own, AXES, axis=0, tiled=False, axis_index_groups=mirrored_pairs())
    gathered = lax.all_gather(both, ("z", "c"), axis=0, tiled=False)
    qkv_weight, _ = lax.optimization_barrier((qkv_weight, both))
    mine = lax.all_gather(qkv_weight, ("z", "c"), axis=0, tiled=False)
    cells = latent.transpose(1, 2, 0, 3)
    cells_after, bias, mine = lax.optimization_barrier((cells, position_bias, mine))
    rolled = [
        lax.ppermute(corner(cells_after, 1, 1), AXES, shifted(1, 1)),
        lax.ppermute(corner(cells_after, 1, 0), AXES, shifted(1, 0)),
        lax.ppermute(corner(cells_after, 0, 1), AXES, shifted(0, 1)),
        corner(cells_after, 0, 0),
    ]
    core = lax.axis_index("c")
    sent = lax.dynamic_index_in_dim(mine.reshape(8, 2, 16, 3 * D), core, 1, keepdims=False)
    theirs = lax.all_gather(lax.ppermute(sent, AXES, mirrored()), "c", axis=0, tiled=False)

    spot = jnp.stack([lax.axis_index("xh"), (lax.axis_index(LAT) == 0).astype(jnp.int32)])
    attended = attention(spot, rolled, mine, theirs, held_bias(bias))
    restored = [
        lax.ppermute(attended[0], AXES, shifted(-1, -1)),
        lax.ppermute(attended[1], AXES, shifted(-1, 0)),
        lax.ppermute(attended[2], AXES, shifted(0, -1)),
        attended[3],
    ]
    return tokens(restored, cells, staged(gathered), attn_gain, mlp_gain).transpose(2, 0, 1, 3)


def solution(mesh):
    mesh = Mesh(mesh.devices.reshape(SIZES), AXES)
    placed = (
        P(None, LAT, LON, None),
        P(LON, None),
        P(LON, None),
        P(),
        P(),
        P(LON, None),
        P(LON, None),
        P(),
    )
    return jax.shard_map(
        shards, mesh=mesh, in_specs=placed, out_specs=P(None, LAT, LON, None), check_vma=False
    )
```

```python
import jax
import jax.numpy as jnp
import numpy as np
from jax import lax
from jax.experimental import pallas as pl
from jax.experimental.pallas import tpu as pltpu
from jax.sharding import Mesh, PartitionSpec as P

WLAT = 6
WLON = 12
LEVELS = 4
HALF_LAT = WLAT // 2
HALF_LON = WLON // 2
QUARTER = LEVELS * HALF_LAT * HALF_LON
WN = 4 * QUARTER
D = 512
CORNER = (HALF_LAT, HALF_LON, LEVELS, D)
HEADS = 16
HEAD_DIM = D // HEADS
FF = 2048
LANES = 128
PER_GROUP = LANES // HEAD_DIM
GROUPS = HEADS // PER_GROUP
PADDED = 3 * LANES
PIECES = 4
MASKED = -1e30
EPSILON = 1e-05
F32 = jnp.float32
BF16 = jnp.bfloat16
VMEM_LIMIT = 8 * 1024 * 1024
ATTENTION_LIMIT = 32 * 1024 * 1024
STAGE_LIMIT = 48 * 1024 * 1024
TOKENS_LIMIT = 40 * 1024 * 1024

AXES = ("xl", "y", "xh", "z", "c")
SIZES = (2, 8, 2, 8, 2)
LAT = ("xl", "y")
LON = ("xh", "z", "c")


def place(lat, lon):
    return (lat % 16) * 32 + lon % 32


def shifted(dlat, dlon):
    return [(place(a, o), place(a + dlat, o + dlon)) for a in range(16) for o in range(32)]


def mirrored_pairs():
    def at(x, y, z, c):
        return (((x % 2) * 8 + y) * 2 + x // 2) * 16 + z * 2 + c

    return [
        [at(x, y, z, c), at(3 - x, y, z, c)]
        for x in range(2)
        for y in range(8)
        for z in range(8)
        for c in range(2)
    ]


def mirrored():
    return [pair for a, b in mirrored_pairs() for pair in ((a, b), (b, a))]


def to_quarters():
    hot = np.zeros((WN, LEVELS, WLAT, WLON), np.float32)
    place_of = 0
    for i in range(2):
        for j in range(2):
            for row in range(HALF_LAT):
                for col in range(HALF_LON):
                    for lev in range(LEVELS):
                        hot[place_of, lev, i * HALF_LAT + row, j * HALF_LON + col] = 1
                        place_of += 1
    return hot.reshape(WN, WN)


def tags():
    upper = (np.arange(WN) // WLON % WLAT < HALF_LAT).astype(np.float32)
    columns = np.zeros((2, WN, LANES), np.float32)
    columns[0, :, 0], columns[0, :, 1] = upper, 1 - upper
    columns[1, :, 0], columns[1, :, 1] = MASKED * (1 - upper), MASKED * upper
    return columns


def normed(values, gain):
    average = jnp.mean(values, -1, keepdims=True)
    centered = values - average
    variance = jnp.mean(centered * centered, -1, keepdims=True)
    return centered * lax.rsqrt(variance + EPSILON) * gain


def dot(a, b):
    return jnp.dot(a, b, preferred_element_type=F32)


def dot_t(a, b):
    return lax.dot_general(a, b, (((1,), (1,)), ((), ())), preferred_element_type=F32)


def stacked(quarters):
    return jnp.concatenate([q.astype(F32).reshape(QUARTER, D) for q in quarters], 0)


def corner(cells, i, j):
    return cells[i * HALF_LAT : (i + 1) * HALF_LAT, j * HALF_LON : (j + 1) * HALF_LON]


def copy_all(pairs, sems):
    copies = [
        pltpu.make_async_copy(source, target, sems.at[i]) for i, (source, target) in enumerate(pairs)
    ]
    for copy in copies:
        copy.start()
    for copy in copies:
        copy.wait()


def pack_kernel(up_ref, down_ref, proj_ref, own_ref, sems):
    parts = ((up_ref, 0, 64), (down_ref, 64, 128), (proj_ref, 128, 144))
    copy_all([(part, own_ref.at[start:stop]) for part, start, stop in parts], sems)


def bias_kernel(bias_hbm, bias_ref, sems):
    copy_all([(bias_hbm, bias_ref)], sems)


def attention_kernel(
    spot_ref, r1, r2, r0, r3, mine_ref, other_ref, hot_ref, tags_ref, bias_ref, o0, o1, o2, o3
):
    hot = hot_ref[...]
    rows = stacked([r[...] for r in (r0, r1, r2, r3)]).astype(BF16)
    rows = lax.dot_general(hot, rows, (((0,), (0,)), ((), ())), preferred_element_type=F32)
    rows = rows.astype(BF16)
    low_half = spot_ref[0] == 0
    low, high = rows[:, : D // 2], rows[:, D // 2 :]
    ours, theirs = jnp.where(low_half, low, high), jnp.where(low_half, high, low)

    def projected(which):
        columns = slice(which * D, (which + 1) * D)
        mine = mine_ref[:, :, columns].reshape(D // 2, D)
        other = jnp.stack([other_ref[0, :, :, columns], other_ref[1, :, :, columns]], 1)
        return (dot(ours, mine) + dot(theirs, other.reshape(D // 2, D))).astype(BF16)

    queries, keys, values = projected(0), projected(1), projected(2)
    lane_head = lax.broadcasted_iota(jnp.int32, (1, LANES), 1) // HEAD_DIM
    zero = jnp.zeros((), BF16)
    gap = jnp.zeros((PADDED - WN, 2 * LANES), BF16)
    beyond = jnp.full((WN, PADDED - WN), MASKED, F32)
    query_tags = jnp.where(spot_ref[1] == 1, tags_ref[0], zero)
    key_tags = tags_ref[1]
    groups = []
    for group in range(GROUPS):
        lanes = slice(group * LANES, (group + 1) * LANES)
        group_q = jnp.concatenate([queries[:, lanes], query_tags], 1)
        group_k, group_v = keys[:, lanes], values[:, lanes]
        key_rows, value_rows = [], []
        for j in range(PER_GROUP):
            mine = lane_head == j
            key_rows += [jnp.concatenate([jnp.where(mine, group_k, zero), key_tags], 1), gap]
            sums = jnp.broadcast_to(jnp.where(mine, 1.0, 0.0).astype(BF16), (WN, LANES))
            value_rows += [jnp.concatenate([jnp.where(mine, group_v, zero), sums], 1), gap]
        scores = dot_t(group_q, jnp.concatenate(key_rows, 0))
        weights = []
        for j in range(PER_GROUP):
            bias = bias_ref[group * PER_GROUP + j].astype(F32)
            bias = jnp.concatenate([bias, beyond], 1)
            head = scores[:, j * PADDED : (j + 1) * PADDED] * HEAD_DIM ** (-0.5) + bias
            weights.append(jnp.exp(head - jnp.max(head, -1, keepdims=True)).astype(BF16))
        product = dot(jnp.concatenate(weights, 1), jnp.concatenate(value_rows, 0))
        groups.append((product[:, :LANES] / product[:, LANES:]).astype(BF16))
    attended = dot(hot, jnp.concatenate(groups, 1))
    for i, out in enumerate((o0, o1, o2, o3)):
        out[...] = attended[i * QUARTER : (i + 1) * QUARTER].reshape(CORNER).astype(BF16)


def stage_kernel(gathered_ref, wp_ref, wu_ref, wd_ref, sems):
    parts = ((wp_ref, 128, 144), (wu_ref, 0, 64), (wd_ref, 64, 128))
    copy_all([(gathered_ref.at[:, :, start:stop], target) for target, start, stop in parts], sems)


def token_kernel(
    m2, m3, m1, m0, cells_ref, wp, wu, wd, attn_gain_ref, mlp_gain_ref, out_ref
):
    attended = stacked([m[...] for m in (m0, m1, m2, m3)]).astype(BF16)
    cells = stacked([corner(cells_ref, i, j) for i in range(2) for j in range(2)])
    low = dot(attended[:, : D // 2], wp[:, 0].reshape(D // 2, D))
    projected = low + dot(attended[:, D // 2 :], wp[:, 1].reshape(D // 2, D))
    rows = (cells + normed(projected, attn_gain_ref[...])).astype(BF16)
    lowered = None
    step = 16 // PIECES
    units = FF // PIECES
    for i in range(0, 16, step):
        up = wu[i : i + step].reshape(units, D)
        down = wd[i : i + step].reshape(units, D)
        raised = dot_t(rows, up)
        hidden = 0.5 * raised * (1.0 + lax.erf(raised * (0.5**0.5)))
        part = dot(hidden.astype(BF16), down)
        lowered = part if lowered is None else lowered + part
    updated = rows.astype(F32) + normed(lowered, mlp_gain_ref[...])
    run = HALF_LON * LEVELS
    for i in range(2):
        for j in range(2):
            for row in range(HALF_LAT):
                start = (i * 2 + j) * QUARTER + row * run
                piece = updated[start : start + run].reshape(HALF_LON, LEVELS, D)
                out_ref[i * HALF_LAT + row, j * HALF_LON : (j + 1) * HALF_LON] = piece.astype(BF16)


def whole(shape):
    return pl.BlockSpec(shape, lambda i: (0,) * len(shape))


def scalars():
    return pl.BlockSpec(memory_space=pltpu.SMEM)


def held():
    return pl.BlockSpec(memory_space=pltpu.VMEM)


def fetched():
    return pl.BlockSpec(memory_space=pltpu.HBM)


def off_chip(*arrays):
    return [pltpu.with_memory_space_constraint(a, pltpu.HBM) for a in arrays]


def params():
    return pltpu.CompilerParams(vmem_limit_bytes=VMEM_LIMIT)


def packed(up_weight, down_weight, proj_weight):
    return pl.pallas_call(
        pack_kernel,
        in_specs=[fetched()] * 3,
        out_specs=held(),
        out_shape=jax.ShapeDtypeStruct((144, D), BF16),
        scratch_shapes=[pltpu.SemaphoreType.DMA((3,))],
        compiler_params=params(),
        name="pack",
    )(*off_chip(up_weight, down_weight, proj_weight))


def held_bias(bias):
    return pl.pallas_call(
        bias_kernel,
        in_specs=[fetched()],
        out_specs=held(),
        out_shape=jax.ShapeDtypeStruct(bias.shape, BF16),
        scratch_shapes=[pltpu.SemaphoreType.DMA((1,))],
        compiler_params=params(),
        cost_estimate=pl.CostEstimate(flops=0, bytes_accessed=2 * bias.size * 2, transcendentals=0),
        name="bias",
    )(*off_chip(bias))


def attention(spot, quarters, mine, other, bias):
    constants = (jnp.asarray(to_quarters(), BF16), jnp.asarray(tags(), BF16))
    return pl.pallas_call(
        attention_kernel,
        in_specs=[scalars()] + [held()] * (len(quarters) + 5),
        out_specs=[held()] * 4,
        out_shape=[jax.ShapeDtypeStruct(CORNER, BF16)] * 4,
        compiler_params=pltpu.CompilerParams(vmem_limit_bytes=ATTENTION_LIMIT),
        name="attention",
    )(spot, *quarters, mine, other, *constants, bias)


def staged(gathered):
    sizes = [(16, 2, rows, D) for rows in (16, 64, 64)]
    return pl.pallas_call(
        stage_kernel,
        in_specs=[fetched()],
        out_specs=[pl.BlockSpec(memory_space=pltpu.VMEM)] * 3,
        out_shape=[jax.ShapeDtypeStruct(size, BF16) for size in sizes],
        scratch_shapes=[pltpu.SemaphoreType.DMA((3,))],
        compiler_params=pltpu.CompilerParams(vmem_limit_bytes=STAGE_LIMIT),
        cost_estimate=pl.CostEstimate(flops=0, bytes_accessed=2 * 144 * 32 * D * 2, transcendentals=0),
        name="stage",
    )(*off_chip(gathered))


def tokens(quarters, cells, weights, attn_gain, mlp_gain):
    out = (WLAT, WLON, LEVELS, D)
    return pl.pallas_call(
        token_kernel,
        grid=(1,),
        in_specs=[whole(CORNER)] * 4
        + [whole(a.shape) for a in (cells, *weights)]
        + [whole((1, D))] * 2,
        out_specs=whole(out),
        out_shape=jax.ShapeDtypeStruct(out, BF16),
        compiler_params=pltpu.CompilerParams(vmem_limit_bytes=TOKENS_LIMIT),
        name="tokens",
    )(*quarters, cells, *weights, attn_gain.reshape(1, D), mlp_gain.reshape(1, D))


def shards(
    latent, qkv_weight, proj_weight, position_bias, attn_gain, up_weight, down_weight, mlp_gain
):
    own = packed(up_weight, down_weight, proj_weight)
    both = lax.all_gather(own, AXES, axis=0, tiled=False, axis_index_groups=mirrored_pairs())
    gathered = lax.all_gather(both, ("z", "c"), axis=0, tiled=False)
    qkv_weight, _ = lax.optimization_barrier((qkv_weight, both))
    mine = lax.all_gather(qkv_weight, ("z", "c"), axis=0, tiled=False)
    cells = latent.transpose(1, 2, 0, 3)
    cells_after, bias, mine = lax.optimization_barrier((cells, position_bias, mine))
    rolled = [
        lax.ppermute(corner(cells_after, 1, 0), AXES, shifted(1, 0)),
        lax.ppermute(corner(cells_after, 0, 1), AXES, shifted(0, 1)),
        lax.ppermute(corner(cells_after, 1, 1), AXES, shifted(1, 1)),
        corner(cells_after, 0, 0),
    ]
    core = lax.axis_index("c")
    sent = lax.dynamic_index_in_dim(mine.reshape(8, 2, 16, 3 * D), core, 1, keepdims=False)
    theirs = lax.all_gather(lax.ppermute(sent, AXES, mirrored()), "c", axis=0, tiled=False)

    spot = jnp.stack([lax.axis_index("xh"), (lax.axis_index(LAT) == 0).astype(jnp.int32)])
    attended = attention(spot, rolled, mine, theirs, held_bias(bias))
    restored = [
        lax.ppermute(attended[1], AXES, shifted(-1, 0)),
        lax.ppermute(attended[0], AXES, shifted(-1, -1)),
        lax.ppermute(attended[2], AXES, shifted(0, -1)),
        attended[3],
    ]
    return tokens(restored, cells, staged(gathered), attn_gain, mlp_gain).transpose(2, 0, 1, 3)


def solution(mesh):
    mesh = Mesh(mesh.devices.reshape(SIZES), AXES)
    placed = (
        P(None, LAT, LON, None),
        P(LON, None),
        P(LON, None),
        P(),
        P(),
        P(LON, None),
        P(LON, None),
        P(),
    )
    return jax.shard_map(
        shards, mesh=mesh, in_specs=placed, out_specs=P(None, LAT, LON, None), check_vma=False
    )
```

```python
import jax
import jax.numpy as jnp
import numpy as np
from jax import lax
from jax.experimental import pallas as pl
from jax.experimental.pallas import tpu as pltpu
from jax.sharding import Mesh, PartitionSpec as P

WLAT = 6
WLON = 12
LEVELS = 4
HALF_LAT = WLAT // 2
HALF_LON = WLON // 2
QUARTER = LEVELS * HALF_LAT * HALF_LON
WN = 4 * QUARTER
D = 512
CORNER = (HALF_LAT, HALF_LON, LEVELS, D)
HEADS = 16
HEAD_DIM = D // HEADS
FF = 2048
LANES = 128
PER_GROUP = LANES // HEAD_DIM
GROUPS = HEADS // PER_GROUP
PADDED = 3 * LANES
PIECES = 2
MASKED = -1e30
EPSILON = 1e-05
F32 = jnp.float32
BF16 = jnp.bfloat16
VMEM_LIMIT = 8 * 1024 * 1024
ATTENTION_LIMIT = 32 * 1024 * 1024
STAGE_LIMIT = 48 * 1024 * 1024
TOKENS_LIMIT = 40 * 1024 * 1024

AXES = ("xl", "y", "xh", "z", "c")
SIZES = (2, 8, 2, 8, 2)
LAT = ("xl", "y")
LON = ("xh", "z", "c")


def place(lat, lon):
    return (lat % 16) * 32 + lon % 32


def shifted(dlat, dlon):
    return [(place(a, o), place(a + dlat, o + dlon)) for a in range(16) for o in range(32)]


def mirrored_pairs():
    def at(x, y, z, c):
        return (((x % 2) * 8 + y) * 2 + x // 2) * 16 + z * 2 + c

    return [
        [at(x, y, z, c), at(3 - x, y, z, c)]
        for x in range(2)
        for y in range(8)
        for z in range(8)
        for c in range(2)
    ]


def mirrored():
    return [pair for a, b in mirrored_pairs() for pair in ((a, b), (b, a))]


def to_quarters():
    hot = np.zeros((WN, LEVELS, WLAT, WLON), np.float32)
    place_of = 0
    for i in range(2):
        for j in range(2):
            for row in range(HALF_LAT):
                for col in range(HALF_LON):
                    for lev in range(LEVELS):
                        hot[place_of, lev, i * HALF_LAT + row, j * HALF_LON + col] = 1
                        place_of += 1
    return hot.reshape(WN, WN)


def tags():
    upper = (np.arange(WN) // WLON % WLAT < HALF_LAT).astype(np.float32)
    columns = np.zeros((2, WN, LANES), np.float32)
    columns[0, :, 0], columns[0, :, 1] = upper, 1 - upper
    columns[1, :, 0], columns[1, :, 1] = MASKED * (1 - upper), MASKED * upper
    return columns


def normed(values, gain):
    average = jnp.mean(values, -1, keepdims=True)
    centered = values - average
    variance = jnp.mean(centered * centered, -1, keepdims=True)
    return centered * lax.rsqrt(variance + EPSILON) * gain


def dot(a, b):
    return jnp.dot(a, b, preferred_element_type=F32)


def dot_t(a, b):
    return lax.dot_general(a, b, (((1,), (1,)), ((), ())), preferred_element_type=F32)


def stacked(quarters):
    return jnp.concatenate([q.astype(F32).reshape(QUARTER, D) for q in quarters], 0)


def corner(cells, i, j):
    return cells[i * HALF_LAT : (i + 1) * HALF_LAT, j * HALF_LON : (j + 1) * HALF_LON]


def copy_all(pairs, sems):
    copies = [
        pltpu.make_async_copy(source, target, sems.at[i]) for i, (source, target) in enumerate(pairs)
    ]
    for copy in copies:
        copy.start()
    for copy in copies:
        copy.wait()


def pack_kernel(up_ref, down_ref, proj_ref, own_ref, sems):
    parts = ((up_ref, 0, 64), (down_ref, 64, 128), (proj_ref, 128, 144))
    copy_all([(part, own_ref.at[start:stop]) for part, start, stop in parts], sems)


def bias_kernel(bias_hbm, bias_ref, sems):
    copy_all([(bias_hbm, bias_ref)], sems)


def attention_kernel(
    spot_ref, r1, r2, r0, r3, mine_ref, other_ref, hot_ref, tags_ref, bias_ref, o0, o1, o2, o3
):
    hot = hot_ref[...]
    rows = stacked([r[...] for r in (r0, r1, r2, r3)]).astype(BF16)
    rows = lax.dot_general(hot, rows, (((0,), (0,)), ((), ())), preferred_element_type=F32)
    rows = rows.astype(BF16)
    low_half = spot_ref[0] == 0
    low, high = rows[:, : D // 2], rows[:, D // 2 :]
    ours, theirs = jnp.where(low_half, low, high), jnp.where(low_half, high, low)

    def projected(which):
        columns = slice(which * D, (which + 1) * D)
        mine = mine_ref[:, :, columns].reshape(D // 2, D)
        other = jnp.stack([other_ref[0, :, :, columns], other_ref[1, :, :, columns]], 1)
        return (dot(ours, mine) + dot(theirs, other.reshape(D // 2, D))).astype(BF16)

    queries, keys, values = projected(0), projected(1), projected(2)
    lane_head = lax.broadcasted_iota(jnp.int32, (1, LANES), 1) // HEAD_DIM
    zero = jnp.zeros((), BF16)
    gap = jnp.zeros((PADDED - WN, 2 * LANES), BF16)
    beyond = jnp.full((WN, PADDED - WN), MASKED, F32)
    query_tags = jnp.where(spot_ref[1] == 1, tags_ref[0], zero)
    key_tags = tags_ref[1]
    groups = []
    for group in range(GROUPS):
        lanes = slice(group * LANES, (group + 1) * LANES)
        group_q = jnp.concatenate([queries[:, lanes], query_tags], 1)
        group_k, group_v = keys[:, lanes], values[:, lanes]
        key_rows, value_rows = [], []
        for j in range(PER_GROUP):
            mine = lane_head == j
            key_rows += [jnp.concatenate([jnp.where(mine, group_k, zero), key_tags], 1), gap]
            sums = jnp.broadcast_to(jnp.where(mine, 1.0, 0.0).astype(BF16), (WN, LANES))
            value_rows += [jnp.concatenate([jnp.where(mine, group_v, zero), sums], 1), gap]
        scores = dot_t(group_q, jnp.concatenate(key_rows, 0))
        weights = []
        for j in range(PER_GROUP):
            bias = bias_ref[group * PER_GROUP + j].astype(F32)
            bias = jnp.concatenate([bias, beyond], 1)
            head = scores[:, j * PADDED : (j + 1) * PADDED] * HEAD_DIM ** (-0.5) + bias
            weights.append(jnp.exp(head - jnp.max(head, -1, keepdims=True)).astype(BF16))
        product = dot(jnp.concatenate(weights, 1), jnp.concatenate(value_rows, 0))
        groups.append((product[:, :LANES] / product[:, LANES:]).astype(BF16))
    attended = dot(hot, jnp.concatenate(groups, 1))
    for i, out in enumerate((o0, o1, o2, o3)):
        out[...] = attended[i * QUARTER : (i + 1) * QUARTER].reshape(CORNER).astype(BF16)


def stage_kernel(gathered_ref, wp_ref, wu_ref, wd_ref, sems):
    parts = ((wp_ref, 128, 144), (wu_ref, 0, 64), (wd_ref, 64, 128))
    copy_all([(gathered_ref.at[:, :, start:stop], target) for target, start, stop in parts], sems)


def token_kernel(
    m2, m3, m1, m0, cells_ref, wp, wu, wd, attn_gain_ref, mlp_gain_ref, out_hbm,
    out_ref, sems,
):
    attended = stacked([m[...] for m in (m0, m1, m2, m3)]).astype(BF16)
    cells = stacked([corner(cells_ref, i, j) for i in range(2) for j in range(2)])
    low = dot(attended[:, : D // 2], wp[:, 0].reshape(D // 2, D))
    projected = low + dot(attended[:, D // 2 :], wp[:, 1].reshape(D // 2, D))
    rows = (cells + normed(projected, attn_gain_ref[...])).astype(BF16)
    lowered = None
    step = 16 // PIECES
    units = FF // PIECES
    for i in range(0, 16, step):
        up = wu[i : i + step].reshape(units, D)
        down = wd[i : i + step].reshape(units, D)
        raised = dot_t(rows, up)
        hidden = 0.5 * raised * (1.0 + lax.erf(raised * (0.5**0.5)))
        part = dot(hidden.astype(BF16), down)
        lowered = part if lowered is None else lowered + part
    updated = rows.astype(F32) + normed(lowered, mlp_gain_ref[...])
    run = HALF_LON * LEVELS
    copies = []
    for i in range(2):
        for j in range(2):
            for row in range(HALF_LAT):
                start = (i * 2 + j) * QUARTER + row * run
                piece = updated[start : start + run].reshape(HALF_LON, LEVELS, D)
                out_ref[i * HALF_LAT + row, j * HALF_LON : (j + 1) * HALF_LON] = piece.astype(BF16)
        half = slice(i * HALF_LAT, (i + 1) * HALF_LAT)
        copies.append(pltpu.make_async_copy(out_ref.at[half], out_hbm.at[half], sems.at[i]))
        copies[-1].start()
    for copy in copies:
        copy.wait()


def whole(shape):
    return pl.BlockSpec(shape, lambda i: (0,) * len(shape))


def scalars():
    return pl.BlockSpec(memory_space=pltpu.SMEM)


def held():
    return pl.BlockSpec(memory_space=pltpu.VMEM)


def fetched():
    return pl.BlockSpec(memory_space=pltpu.HBM)


def off_chip(*arrays):
    return [pltpu.with_memory_space_constraint(a, pltpu.HBM) for a in arrays]


def params():
    return pltpu.CompilerParams(vmem_limit_bytes=VMEM_LIMIT)


def packed(up_weight, down_weight, proj_weight):
    return pl.pallas_call(
        pack_kernel,
        in_specs=[fetched()] * 3,
        out_specs=held(),
        out_shape=jax.ShapeDtypeStruct((144, D), BF16),
        scratch_shapes=[pltpu.SemaphoreType.DMA((3,))],
        compiler_params=params(),
        name="pack",
    )(*off_chip(up_weight, down_weight, proj_weight))


def held_bias(bias):
    return pl.pallas_call(
        bias_kernel,
        in_specs=[fetched()],
        out_specs=held(),
        out_shape=jax.ShapeDtypeStruct(bias.shape, BF16),
        scratch_shapes=[pltpu.SemaphoreType.DMA((1,))],
        compiler_params=params(),
        cost_estimate=pl.CostEstimate(flops=0, bytes_accessed=2 * bias.size * 2, transcendentals=0),
        name="bias",
    )(*off_chip(bias))


def attention(spot, quarters, mine, other, bias):
    constants = (jnp.asarray(to_quarters(), BF16), jnp.asarray(tags(), BF16))
    return pl.pallas_call(
        attention_kernel,
        in_specs=[scalars()] + [held()] * (len(quarters) + 5),
        out_specs=[held()] * 4,
        out_shape=[jax.ShapeDtypeStruct(CORNER, BF16)] * 4,
        compiler_params=pltpu.CompilerParams(vmem_limit_bytes=ATTENTION_LIMIT),
        name="attention",
    )(spot, *quarters, mine, other, *constants, bias)


def staged(gathered):
    sizes = [(16, 2, rows, D) for rows in (16, 64, 64)]
    return pl.pallas_call(
        stage_kernel,
        in_specs=[fetched()],
        out_specs=[pl.BlockSpec(memory_space=pltpu.VMEM)] * 3,
        out_shape=[jax.ShapeDtypeStruct(size, BF16) for size in sizes],
        scratch_shapes=[pltpu.SemaphoreType.DMA((3,))],
        compiler_params=pltpu.CompilerParams(vmem_limit_bytes=STAGE_LIMIT),
        cost_estimate=pl.CostEstimate(flops=0, bytes_accessed=2 * 144 * 32 * D * 2, transcendentals=0),
        name="stage",
    )(*off_chip(gathered))


def tokens(quarters, cells, weights, attn_gain, mlp_gain):
    out = (WLAT, WLON, LEVELS, D)
    operands = (*quarters, cells, *weights, attn_gain.reshape(1, D), mlp_gain.reshape(1, D))
    return pl.pallas_call(
        token_kernel,
        in_specs=[held()] * len(operands),
        out_specs=fetched(),
        out_shape=jax.ShapeDtypeStruct(out, BF16),
        scratch_shapes=[pltpu.VMEM(out, BF16), pltpu.SemaphoreType.DMA((2,))],
        compiler_params=pltpu.CompilerParams(vmem_limit_bytes=TOKENS_LIMIT),
        name="tokens",
    )(*operands)


def shards(
    latent, qkv_weight, proj_weight, position_bias, attn_gain, up_weight, down_weight, mlp_gain
):
    own = packed(up_weight, down_weight, proj_weight)
    both = lax.all_gather(own, AXES, axis=0, tiled=False, axis_index_groups=mirrored_pairs())
    gathered = lax.all_gather(both, ("z", "c"), axis=0, tiled=False)
    qkv_weight, _ = lax.optimization_barrier((qkv_weight, both))
    mine = lax.all_gather(qkv_weight, ("z", "c"), axis=0, tiled=False)
    cells = latent.transpose(1, 2, 0, 3)
    cells_after, bias, mine = lax.optimization_barrier((cells, position_bias, mine))
    rolled = [
        lax.ppermute(corner(cells_after, 1, 0), AXES, shifted(1, 0)),
        lax.ppermute(corner(cells_after, 0, 1), AXES, shifted(0, 1)),
        lax.ppermute(corner(cells_after, 1, 1), AXES, shifted(1, 1)),
        corner(cells_after, 0, 0),
    ]
    core = lax.axis_index("c")
    sent = lax.dynamic_index_in_dim(mine.reshape(8, 2, 16, 3 * D), core, 1, keepdims=False)
    theirs = lax.all_gather(lax.ppermute(sent, AXES, mirrored()), "c", axis=0, tiled=False)

    spot = jnp.stack([lax.axis_index("xh"), (lax.axis_index(LAT) == 0).astype(jnp.int32)])
    attended = attention(spot, rolled, mine, theirs, held_bias(bias))
    restored = [
        lax.ppermute(attended[1], AXES, shifted(-1, 0)),
        lax.ppermute(attended[0], AXES, shifted(-1, -1)),
        lax.ppermute(attended[2], AXES, shifted(0, -1)),
        attended[3],
    ]
    return tokens(restored, cells, staged(gathered), attn_gain, mlp_gain).transpose(2, 0, 1, 3)


def solution(mesh):
    mesh = Mesh(mesh.devices.reshape(SIZES), AXES)
    placed = (
        P(None, LAT, LON, None),
        P(LON, None),
        P(LON, None),
        P(),
        P(),
        P(LON, None),
        P(LON, None),
        P(),
    )
    return jax.shard_map(
        shards, mesh=mesh, in_specs=placed, out_specs=P(None, LAT, LON, None), check_vma=False
    )
```

```python
import jax
import jax.numpy as jnp
import numpy as np
from jax import lax
from jax.experimental import pallas as pl
from jax.experimental.pallas import tpu as pltpu
from jax.sharding import Mesh, PartitionSpec as P

WLAT = 6
WLON = 12
LEVELS = 4
HALF_LAT = WLAT // 2
HALF_LON = WLON // 2
QUARTER = LEVELS * HALF_LAT * HALF_LON
WN = 4 * QUARTER
D = 512
CORNER = (HALF_LAT, HALF_LON, LEVELS, D)
HEADS = 16
HEAD_DIM = D // HEADS
FF = 2048
LANES = 128
PER_GROUP = LANES // HEAD_DIM
GROUPS = HEADS // PER_GROUP
PADDED = 3 * LANES
PIECES = 2
MASKED = -1e30
EPSILON = 1e-05
F32 = jnp.float32
BF16 = jnp.bfloat16
VMEM_LIMIT = 8 * 1024 * 1024
ATTENTION_LIMIT = 32 * 1024 * 1024
STAGE_LIMIT = 48 * 1024 * 1024
TOKENS_LIMIT = 40 * 1024 * 1024

AXES = ("xl", "y", "xh", "z", "c")
SIZES = (2, 8, 2, 8, 2)
LAT = ("xl", "y")
LON = ("xh", "z", "c")


def place(lat, lon):
    return (lat % 16) * 32 + lon % 32


def shifted(dlat, dlon):
    return [(place(a, o), place(a + dlat, o + dlon)) for a in range(16) for o in range(32)]


def mirrored_pairs():
    def at(x, y, z, c):
        return (((x % 2) * 8 + y) * 2 + x // 2) * 16 + z * 2 + c

    return [
        [at(x, y, z, c), at(3 - x, y, z, c)]
        for x in range(2)
        for y in range(8)
        for z in range(8)
        for c in range(2)
    ]


def mirrored():
    return [pair for a, b in mirrored_pairs() for pair in ((a, b), (b, a))]


def to_quarters():
    hot = np.zeros((WN, LEVELS, WLAT, WLON), np.float32)
    place_of = 0
    for i in range(2):
        for j in range(2):
            for row in range(HALF_LAT):
                for col in range(HALF_LON):
                    for lev in range(LEVELS):
                        hot[place_of, lev, i * HALF_LAT + row, j * HALF_LON + col] = 1
                        place_of += 1
    return hot.reshape(WN, WN)


def tags():
    upper = (np.arange(WN) // WLON % WLAT < HALF_LAT).astype(np.float32)
    columns = np.zeros((2, WN, LANES), np.float32)
    columns[0, :, 0], columns[0, :, 1] = upper, 1 - upper
    columns[1, :, 0], columns[1, :, 1] = MASKED * (1 - upper), MASKED * upper
    return columns


def normed(values, gain):
    average = jnp.mean(values, -1, keepdims=True)
    centered = values - average
    variance = jnp.mean(centered * centered, -1, keepdims=True)
    return centered * lax.rsqrt(variance + EPSILON) * gain


def dot(a, b):
    return jnp.dot(a, b, preferred_element_type=F32)


def dot_t(a, b):
    return lax.dot_general(a, b, (((1,), (1,)), ((), ())), preferred_element_type=F32)


def stacked(quarters):
    return jnp.concatenate([q.astype(F32).reshape(QUARTER, D) for q in quarters], 0)


def corner(cells, i, j):
    return cells[i * HALF_LAT : (i + 1) * HALF_LAT, j * HALF_LON : (j + 1) * HALF_LON]


def copy_all(pairs, sems):
    copies = [
        pltpu.make_async_copy(source, target, sems.at[i]) for i, (source, target) in enumerate(pairs)
    ]
    for copy in copies:
        copy.start()
    for copy in copies:
        copy.wait()


def pack_kernel(up_ref, down_ref, proj_ref, own_ref, sems):
    parts = ((up_ref, 0, 64), (down_ref, 64, 128), (proj_ref, 128, 144))
    copy_all([(part, own_ref.at[start:stop]) for part, start, stop in parts], sems)


def bias_kernel(bias_hbm, bias_ref, sems):
    copy_all([(bias_hbm, bias_ref)], sems)


def attention_kernel(
    spot_ref, r0, r2, r1, r3, mine_ref, other_ref, hot_ref, tags_ref, bias_ref, o0, o1, o2, o3
):
    hot = hot_ref[...]
    rows = stacked([r[...] for r in (r0, r1, r2, r3)]).astype(BF16)
    rows = lax.dot_general(hot, rows, (((0,), (0,)), ((), ())), preferred_element_type=F32)
    rows = rows.astype(BF16)
    low_half = spot_ref[0] == 0
    low, high = rows[:, : D // 2], rows[:, D // 2 :]
    ours, theirs = jnp.where(low_half, low, high), jnp.where(low_half, high, low)

    def projected(which):
        columns = slice(which * D, (which + 1) * D)
        mine = mine_ref[:, :, columns].reshape(D // 2, D)
        other = jnp.stack([other_ref[0, :, :, columns], other_ref[1, :, :, columns]], 1)
        return (dot(ours, mine) + dot(theirs, other.reshape(D // 2, D))).astype(BF16)

    queries, keys, values = projected(0), projected(1), projected(2)
    lane_head = lax.broadcasted_iota(jnp.int32, (1, LANES), 1) // HEAD_DIM
    zero = jnp.zeros((), BF16)
    gap = jnp.zeros((PADDED - WN, 2 * LANES), BF16)
    beyond = jnp.full((WN, PADDED - WN), MASKED, F32)
    query_tags = jnp.where(spot_ref[1] == 1, tags_ref[0], zero)
    key_tags = tags_ref[1]
    groups = []
    for group in range(GROUPS):
        lanes = slice(group * LANES, (group + 1) * LANES)
        group_q = jnp.concatenate([queries[:, lanes], query_tags], 1)
        group_k, group_v = keys[:, lanes], values[:, lanes]
        key_rows, value_rows = [], []
        for j in range(PER_GROUP):
            mine = lane_head == j
            key_rows += [jnp.concatenate([jnp.where(mine, group_k, zero), key_tags], 1), gap]
            sums = jnp.broadcast_to(jnp.where(mine, 1.0, 0.0).astype(BF16), (WN, LANES))
            value_rows += [jnp.concatenate([jnp.where(mine, group_v, zero), sums], 1), gap]
        scores = dot_t(group_q, jnp.concatenate(key_rows, 0))
        weights = []
        for j in range(PER_GROUP):
            bias = bias_ref[group * PER_GROUP + j].astype(F32)
            bias = jnp.concatenate([bias, beyond], 1)
            head = scores[:, j * PADDED : (j + 1) * PADDED] * HEAD_DIM ** (-0.5) + bias
            weights.append(jnp.exp(head - jnp.max(head, -1, keepdims=True)).astype(BF16))
        product = dot(jnp.concatenate(weights, 1), jnp.concatenate(value_rows, 0))
        groups.append((product[:, :LANES] / product[:, LANES:]).astype(BF16))
    attended = dot(hot, jnp.concatenate(groups, 1))
    for i, out in enumerate((o0, o1, o2, o3)):
        out[...] = attended[i * QUARTER : (i + 1) * QUARTER].reshape(CORNER).astype(BF16)


def stage_kernel(gathered_ref, wp_ref, wu_ref, wd_ref, sems):
    parts = ((wp_ref, 128, 144), (wu_ref, 0, 64), (wd_ref, 64, 128))
    copy_all([(gathered_ref.at[:, :, start:stop], target) for target, start, stop in parts], sems)


def token_kernel(
    m2, m3, m1, m0, cells_ref, wp, wu, wd, attn_gain_ref, mlp_gain_ref, out_hbm,
    out_ref, sems,
):
    attended = stacked([m[...] for m in (m0, m1, m2, m3)]).astype(BF16)
    cells = stacked([corner(cells_ref, i, j) for i in range(2) for j in range(2)])
    low = dot(attended[:, : D // 2], wp[:, 0].reshape(D // 2, D))
    projected = low + dot(attended[:, D // 2 :], wp[:, 1].reshape(D // 2, D))
    rows = (cells + normed(projected, attn_gain_ref[...])).astype(BF16)
    lowered = None
    step = 16 // PIECES
    units = FF // PIECES
    for i in range(0, 16, step):
        up = wu[i : i + step].reshape(units, D)
        down = wd[i : i + step].reshape(units, D)
        raised = dot_t(rows, up)
        hidden = 0.5 * raised * (1.0 + lax.erf(raised * (0.5**0.5)))
        part = dot(hidden.astype(BF16), down)
        lowered = part if lowered is None else lowered + part
    updated = rows.astype(F32) + normed(lowered, mlp_gain_ref[...])
    run = HALF_LON * LEVELS
    copies = []
    for i in range(2):
        for j in range(2):
            for row in range(HALF_LAT):
                start = (i * 2 + j) * QUARTER + row * run
                piece = updated[start : start + run].reshape(HALF_LON, LEVELS, D)
                out_ref[i * HALF_LAT + row, j * HALF_LON : (j + 1) * HALF_LON] = piece.astype(BF16)
        half = slice(i * HALF_LAT, (i + 1) * HALF_LAT)
        copies.append(pltpu.make_async_copy(out_ref.at[half], out_hbm.at[half], sems.at[i]))
        copies[-1].start()
    for copy in copies:
        copy.wait()


def whole(shape):
    return pl.BlockSpec(shape, lambda i: (0,) * len(shape))


def scalars():
    return pl.BlockSpec(memory_space=pltpu.SMEM)


def held():
    return pl.BlockSpec(memory_space=pltpu.VMEM)


def fetched():
    return pl.BlockSpec(memory_space=pltpu.HBM)


def off_chip(*arrays):
    return [pltpu.with_memory_space_constraint(a, pltpu.HBM) for a in arrays]


def params():
    return pltpu.CompilerParams(vmem_limit_bytes=VMEM_LIMIT)


def packed(up_weight, down_weight, proj_weight):
    return pl.pallas_call(
        pack_kernel,
        in_specs=[fetched()] * 3,
        out_specs=held(),
        out_shape=jax.ShapeDtypeStruct((144, D), BF16),
        scratch_shapes=[pltpu.SemaphoreType.DMA((3,))],
        compiler_params=params(),
        name="pack",
    )(*off_chip(up_weight, down_weight, proj_weight))


def held_bias(bias):
    return pl.pallas_call(
        bias_kernel,
        in_specs=[fetched()],
        out_specs=held(),
        out_shape=jax.ShapeDtypeStruct(bias.shape, BF16),
        scratch_shapes=[pltpu.SemaphoreType.DMA((1,))],
        compiler_params=params(),
        cost_estimate=pl.CostEstimate(flops=0, bytes_accessed=2 * bias.size * 2, transcendentals=0),
        name="bias",
    )(*off_chip(bias))


def attention(spot, quarters, mine, other, bias):
    constants = (jnp.asarray(to_quarters(), BF16), jnp.asarray(tags(), BF16))
    return pl.pallas_call(
        attention_kernel,
        in_specs=[scalars()] + [held()] * (len(quarters) + 5),
        out_specs=[held()] * 4,
        out_shape=[jax.ShapeDtypeStruct(CORNER, BF16)] * 4,
        compiler_params=pltpu.CompilerParams(vmem_limit_bytes=ATTENTION_LIMIT),
        name="attention",
    )(spot, *quarters, mine, other, *constants, bias)


def staged(gathered):
    sizes = [(16, 2, rows, D) for rows in (16, 64, 64)]
    return pl.pallas_call(
        stage_kernel,
        in_specs=[fetched()],
        out_specs=[pl.BlockSpec(memory_space=pltpu.VMEM)] * 3,
        out_shape=[jax.ShapeDtypeStruct(size, BF16) for size in sizes],
        scratch_shapes=[pltpu.SemaphoreType.DMA((3,))],
        compiler_params=pltpu.CompilerParams(vmem_limit_bytes=STAGE_LIMIT),
        cost_estimate=pl.CostEstimate(flops=0, bytes_accessed=2 * 144 * 32 * D * 2, transcendentals=0),
        name="stage",
    )(*off_chip(gathered))


def tokens(quarters, cells, weights, attn_gain, mlp_gain):
    out = (WLAT, WLON, LEVELS, D)
    operands = (*quarters, cells, *weights, attn_gain.reshape(1, D), mlp_gain.reshape(1, D))
    return pl.pallas_call(
        token_kernel,
        in_specs=[held()] * len(operands),
        out_specs=fetched(),
        out_shape=jax.ShapeDtypeStruct(out, BF16),
        scratch_shapes=[pltpu.VMEM(out, BF16), pltpu.SemaphoreType.DMA((2,))],
        compiler_params=pltpu.CompilerParams(vmem_limit_bytes=TOKENS_LIMIT),
        name="tokens",
    )(*operands)


def shards(
    latent, qkv_weight, proj_weight, position_bias, attn_gain, up_weight, down_weight, mlp_gain
):
    own = packed(up_weight, down_weight, proj_weight)
    both = lax.all_gather(own, AXES, axis=0, tiled=False, axis_index_groups=mirrored_pairs())
    gathered = lax.all_gather(both, ("z", "c"), axis=0, tiled=False)
    qkv_weight, _ = lax.optimization_barrier((qkv_weight, both))
    mine = lax.all_gather(qkv_weight, ("z", "c"), axis=0, tiled=False)
    cells = latent.transpose(1, 2, 0, 3)
    cells_after, bias, mine = lax.optimization_barrier((cells, position_bias, mine))
    rolled = [
        lax.ppermute(corner(cells_after, 1, 1), AXES, shifted(1, 1)),
        lax.ppermute(corner(cells_after, 0, 1), AXES, shifted(0, 1)),
        lax.ppermute(corner(cells_after, 1, 0), AXES, shifted(1, 0)),
        corner(cells_after, 0, 0),
    ]
    core = lax.axis_index("c")
    sent = lax.dynamic_index_in_dim(mine.reshape(8, 2, 16, 3 * D), core, 1, keepdims=False)
    theirs = lax.all_gather(lax.ppermute(sent, AXES, mirrored()), "c", axis=0, tiled=False)

    spot = jnp.stack([lax.axis_index("xh"), (lax.axis_index(LAT) == 0).astype(jnp.int32)])
    attended = attention(spot, rolled, mine, theirs, held_bias(bias))
    restored = [
        lax.ppermute(attended[1], AXES, shifted(-1, 0)),
        lax.ppermute(attended[0], AXES, shifted(-1, -1)),
        lax.ppermute(attended[2], AXES, shifted(0, -1)),
        attended[3],
    ]
    return tokens(restored, cells, staged(gathered), attn_gain, mlp_gain).transpose(2, 0, 1, 3)


def solution(mesh):
    mesh = Mesh(mesh.devices.reshape(SIZES), AXES)
    placed = (
        P(None, LAT, LON, None),
        P(LON, None),
        P(LON, None),
        P(),
        P(),
        P(LON, None),
        P(LON, None),
        P(),
    )
    return jax.shard_map(
        shards, mesh=mesh, in_specs=placed, out_specs=P(None, LAT, LON, None), check_vma=False
    )
```

```python
import jax
import jax.numpy as jnp
import numpy as np
from jax import lax
from jax.experimental import pallas as pl
from jax.experimental.pallas import tpu as pltpu
from jax.sharding import Mesh, PartitionSpec as P

WLAT = 6
WLON = 12
LEVELS = 4
HALF_LAT = WLAT // 2
HALF_LON = WLON // 2
QUARTER = LEVELS * HALF_LAT * HALF_LON
WN = 4 * QUARTER
D = 512
CORNER = (HALF_LAT, HALF_LON, LEVELS, D)
HEADS = 16
HEAD_DIM = D // HEADS
FF = 2048
LANES = 128
PER_GROUP = LANES // HEAD_DIM
GROUPS = HEADS // PER_GROUP
PADDED = 3 * LANES
PIECES = 2
MASKED = -1e30
EPSILON = 1e-05
F32 = jnp.float32
BF16 = jnp.bfloat16
VMEM_LIMIT = 8 * 1024 * 1024
ATTENTION_LIMIT = 32 * 1024 * 1024
STAGE_LIMIT = 48 * 1024 * 1024
TOKENS_LIMIT = 40 * 1024 * 1024

AXES = ("xl", "y", "xh", "z", "c")
SIZES = (2, 8, 2, 8, 2)
LAT = ("xl", "y")
LON = ("xh", "z", "c")


def place(lat, lon):
    return (lat % 16) * 32 + lon % 32


def shifted(dlat, dlon):
    return [(place(a, o), place(a + dlat, o + dlon)) for a in range(16) for o in range(32)]


def mirrored_pairs():
    def at(x, y, z, c):
        return (((x % 2) * 8 + y) * 2 + x // 2) * 16 + z * 2 + c

    return [
        [at(x, y, z, c), at(3 - x, y, z, c)]
        for x in range(2)
        for y in range(8)
        for z in range(8)
        for c in range(2)
    ]


def mirrored():
    return [pair for a, b in mirrored_pairs() for pair in ((a, b), (b, a))]


def to_quarters():
    hot = np.zeros((WN, LEVELS, WLAT, WLON), np.float32)
    place_of = 0
    for i in range(2):
        for j in range(2):
            for row in range(HALF_LAT):
                for col in range(HALF_LON):
                    for lev in range(LEVELS):
                        hot[place_of, lev, i * HALF_LAT + row, j * HALF_LON + col] = 1
                        place_of += 1
    return hot.reshape(WN, WN)


def tags():
    upper = (np.arange(WN) // WLON % WLAT < HALF_LAT).astype(np.float32)
    columns = np.zeros((2, WN, LANES), np.float32)
    columns[0, :, 0], columns[0, :, 1] = upper, 1 - upper
    columns[1, :, 0], columns[1, :, 1] = MASKED * (1 - upper), MASKED * upper
    return columns


def normed(values, gain):
    average = jnp.mean(values, -1, keepdims=True)
    centered = values - average
    variance = jnp.mean(centered * centered, -1, keepdims=True)
    return centered * lax.rsqrt(variance + EPSILON) * gain


def dot(a, b):
    return jnp.dot(a, b, preferred_element_type=F32)


def dot_t(a, b):
    return lax.dot_general(a, b, (((1,), (1,)), ((), ())), preferred_element_type=F32)


def stacked(quarters):
    return jnp.concatenate([q.astype(F32).reshape(QUARTER, D) for q in quarters], 0)


def corner(cells, i, j):
    return cells[i * HALF_LAT : (i + 1) * HALF_LAT, j * HALF_LON : (j + 1) * HALF_LON]


def copy_all(pairs, sems):
    copies = [
        pltpu.make_async_copy(source, target, sems.at[i]) for i, (source, target) in enumerate(pairs)
    ]
    for copy in copies:
        copy.start()
    for copy in copies:
        copy.wait()


def pack_kernel(up_ref, down_ref, proj_ref, own_ref, sems):
    parts = ((up_ref, 0, 64), (down_ref, 64, 128), (proj_ref, 128, 144))
    copy_all([(part, own_ref.at[start:stop]) for part, start, stop in parts], sems)


def bias_kernel(bias_hbm, bias_ref, sems):
    copy_all([(bias_hbm, bias_ref)], sems)


def attention_kernel(
    spot_ref, r0, r2, r1, r3, mine_ref, other_ref, hot_ref, tags_ref, bias_ref, o0, o1, o2, o3
):
    hot = hot_ref[...]
    rows = stacked([r[...] for r in (r0, r1, r2, r3)]).astype(BF16)
    rows = lax.dot_general(hot, rows, (((0,), (0,)), ((), ())), preferred_element_type=F32)
    rows = rows.astype(BF16)
    low_half = spot_ref[0] == 0
    low, high = rows[:, : D // 2], rows[:, D // 2 :]
    ours, theirs = jnp.where(low_half, low, high), jnp.where(low_half, high, low)

    def projected(which):
        columns = slice(which * D, (which + 1) * D)
        mine = mine_ref[:, :, columns].reshape(D // 2, D)
        other = jnp.stack([other_ref[0, :, :, columns], other_ref[1, :, :, columns]], 1)
        return (dot(ours, mine) + dot(theirs, other.reshape(D // 2, D))).astype(BF16)

    queries, keys, values = projected(0), projected(1), projected(2)
    lane_head = lax.broadcasted_iota(jnp.int32, (1, LANES), 1) // HEAD_DIM
    zero = jnp.zeros((), BF16)
    gap = jnp.zeros((PADDED - WN, 2 * LANES), BF16)
    beyond = jnp.full((WN, PADDED - WN), MASKED, F32)
    query_tags = jnp.where(spot_ref[1] == 1, tags_ref[0], zero)
    key_tags = tags_ref[1]
    groups = []
    for group in range(GROUPS):
        lanes = slice(group * LANES, (group + 1) * LANES)
        group_q = jnp.concatenate([queries[:, lanes], query_tags], 1)
        group_k, group_v = keys[:, lanes], values[:, lanes]
        key_rows, value_rows = [], []
        for j in range(PER_GROUP):
            mine = lane_head == j
            key_rows += [jnp.concatenate([jnp.where(mine, group_k, zero), key_tags], 1), gap]
            sums = jnp.broadcast_to(jnp.where(mine, 1.0, 0.0).astype(BF16), (WN, LANES))
            value_rows += [jnp.concatenate([jnp.where(mine, group_v, zero), sums], 1), gap]
        scores = dot_t(group_q, jnp.concatenate(key_rows, 0))
        weights = []
        for j in range(PER_GROUP):
            bias = bias_ref[group * PER_GROUP + j].astype(F32)
            bias = jnp.concatenate([bias, beyond], 1)
            head = scores[:, j * PADDED : (j + 1) * PADDED] * HEAD_DIM ** (-0.5) + bias
            weights.append(jnp.exp(head - jnp.max(head, -1, keepdims=True)).astype(BF16))
        product = dot(jnp.concatenate(weights, 1), jnp.concatenate(value_rows, 0))
        groups.append((product[:, :LANES] / product[:, LANES:]).astype(BF16))
    attended = dot(hot, jnp.concatenate(groups, 1))
    for i, out in enumerate((o0, o1, o2, o3)):
        out[...] = attended[i * QUARTER : (i + 1) * QUARTER].reshape(CORNER).astype(BF16)


def stage_kernel(gathered_ref, wp_ref, wu_ref, wd_ref, sems):
    parts = ((wp_ref, 128, 144), (wu_ref, 0, 64), (wd_ref, 64, 128))
    copy_all([(gathered_ref.at[:, :, start:stop], target) for target, start, stop in parts], sems)


def token_kernel(
    m3, m1, m2, m0, cells_ref, wp, wu, wd, attn_gain_ref, mlp_gain_ref, out_hbm,
    out_ref, sems,
):
    attended = stacked([m[...] for m in (m0, m1, m2, m3)]).astype(BF16)
    cells = stacked([corner(cells_ref, i, j) for i in range(2) for j in range(2)])
    low = dot(attended[:, : D // 2], wp[:, 0].reshape(D // 2, D))
    projected = low + dot(attended[:, D // 2 :], wp[:, 1].reshape(D // 2, D))
    rows = (cells + normed(projected, attn_gain_ref[...])).astype(BF16)
    lowered = None
    step = 16 // PIECES
    units = FF // PIECES
    for i in range(0, 16, step):
        up = wu[i : i + step].reshape(units, D)
        down = wd[i : i + step].reshape(units, D)
        raised = dot_t(rows, up)
        hidden = 0.5 * raised * (1.0 + lax.erf(raised * (0.5**0.5)))
        part = dot(hidden.astype(BF16), down)
        lowered = part if lowered is None else lowered + part
    updated = rows.astype(F32) + normed(lowered, mlp_gain_ref[...])
    run = HALF_LON * LEVELS
    copies = []
    for i in range(2):
        for j in range(2):
            for row in range(HALF_LAT):
                start = (i * 2 + j) * QUARTER + row * run
                piece = updated[start : start + run].reshape(HALF_LON, LEVELS, D)
                out_ref[i * HALF_LAT + row, j * HALF_LON : (j + 1) * HALF_LON] = piece.astype(BF16)
        half = slice(i * HALF_LAT, (i + 1) * HALF_LAT)
        copies.append(pltpu.make_async_copy(out_ref.at[half], out_hbm.at[half], sems.at[i]))
        copies[-1].start()
    for copy in copies:
        copy.wait()


def whole(shape):
    return pl.BlockSpec(shape, lambda i: (0,) * len(shape))


def scalars():
    return pl.BlockSpec(memory_space=pltpu.SMEM)


def held():
    return pl.BlockSpec(memory_space=pltpu.VMEM)


def fetched():
    return pl.BlockSpec(memory_space=pltpu.HBM)


def off_chip(*arrays):
    return [pltpu.with_memory_space_constraint(a, pltpu.HBM) for a in arrays]


def params():
    return pltpu.CompilerParams(vmem_limit_bytes=VMEM_LIMIT)


def packed(up_weight, down_weight, proj_weight):
    return pl.pallas_call(
        pack_kernel,
        in_specs=[fetched()] * 3,
        out_specs=held(),
        out_shape=jax.ShapeDtypeStruct((144, D), BF16),
        scratch_shapes=[pltpu.SemaphoreType.DMA((3,))],
        compiler_params=params(),
        name="pack",
    )(*off_chip(up_weight, down_weight, proj_weight))


def held_bias(bias):
    return pl.pallas_call(
        bias_kernel,
        in_specs=[fetched()],
        out_specs=held(),
        out_shape=jax.ShapeDtypeStruct(bias.shape, BF16),
        scratch_shapes=[pltpu.SemaphoreType.DMA((1,))],
        compiler_params=params(),
        cost_estimate=pl.CostEstimate(flops=0, bytes_accessed=2 * bias.size * 2, transcendentals=0),
        name="bias",
    )(*off_chip(bias))


def attention(spot, quarters, mine, other, bias):
    constants = (jnp.asarray(to_quarters(), BF16), jnp.asarray(tags(), BF16))
    return pl.pallas_call(
        attention_kernel,
        in_specs=[scalars()] + [held()] * (len(quarters) + 5),
        out_specs=[held()] * 4,
        out_shape=[jax.ShapeDtypeStruct(CORNER, BF16)] * 4,
        compiler_params=pltpu.CompilerParams(vmem_limit_bytes=ATTENTION_LIMIT),
        name="attention",
    )(spot, *quarters, mine, other, *constants, bias)


def staged(gathered):
    sizes = [(16, 2, rows, D) for rows in (16, 64, 64)]
    return pl.pallas_call(
        stage_kernel,
        in_specs=[fetched()],
        out_specs=[pl.BlockSpec(memory_space=pltpu.VMEM)] * 3,
        out_shape=[jax.ShapeDtypeStruct(size, BF16) for size in sizes],
        scratch_shapes=[pltpu.SemaphoreType.DMA((3,))],
        compiler_params=pltpu.CompilerParams(vmem_limit_bytes=STAGE_LIMIT),
        cost_estimate=pl.CostEstimate(flops=0, bytes_accessed=2 * 144 * 32 * D * 2, transcendentals=0),
        name="stage",
    )(*off_chip(gathered))


def tokens(quarters, cells, weights, attn_gain, mlp_gain):
    out = (WLAT, WLON, LEVELS, D)
    operands = (*quarters, cells, *weights, attn_gain.reshape(1, D), mlp_gain.reshape(1, D))
    return pl.pallas_call(
        token_kernel,
        in_specs=[held()] * len(operands),
        out_specs=fetched(),
        out_shape=jax.ShapeDtypeStruct(out, BF16),
        scratch_shapes=[pltpu.VMEM(out, BF16), pltpu.SemaphoreType.DMA((2,))],
        compiler_params=pltpu.CompilerParams(vmem_limit_bytes=TOKENS_LIMIT),
        name="tokens",
    )(*operands)


def shards(
    latent, qkv_weight, proj_weight, position_bias, attn_gain, up_weight, down_weight, mlp_gain
):
    own = packed(up_weight, down_weight, proj_weight)
    both = lax.all_gather(own, AXES, axis=0, tiled=False, axis_index_groups=mirrored_pairs())
    gathered = lax.all_gather(both, ("z", "c"), axis=0, tiled=False)
    qkv_weight, _ = lax.optimization_barrier((qkv_weight, both))
    mine = lax.all_gather(qkv_weight, ("z", "c"), axis=0, tiled=False)
    cells = latent.transpose(1, 2, 0, 3)
    cells_after, bias, mine = lax.optimization_barrier((cells, position_bias, mine))
    rolled = [
        lax.ppermute(corner(cells_after, 1, 1), AXES, shifted(1, 1)),
        lax.ppermute(corner(cells_after, 0, 1), AXES, shifted(0, 1)),
        lax.ppermute(corner(cells_after, 1, 0), AXES, shifted(1, 0)),
        corner(cells_after, 0, 0),
    ]
    core = lax.axis_index("c")
    sent = lax.dynamic_index_in_dim(mine.reshape(8, 2, 16, 3 * D), core, 1, keepdims=False)
    theirs = lax.all_gather(lax.ppermute(sent, AXES, mirrored()), "c", axis=0, tiled=False)

    spot = jnp.stack([lax.axis_index("xh"), (lax.axis_index(LAT) == 0).astype(jnp.int32)])
    attended = attention(spot, rolled, mine, theirs, held_bias(bias))
    restored = [
        lax.ppermute(attended[0], AXES, shifted(-1, -1)),
        lax.ppermute(attended[2], AXES, shifted(0, -1)),
        lax.ppermute(attended[1], AXES, shifted(-1, 0)),
        attended[3],
    ]
    return tokens(restored, cells, staged(gathered), attn_gain, mlp_gain).transpose(2, 0, 1, 3)


def solution(mesh):
    mesh = Mesh(mesh.devices.reshape(SIZES), AXES)
    placed = (
        P(None, LAT, LON, None),
        P(LON, None),
        P(LON, None),
        P(),
        P(),
        P(LON, None),
        P(LON, None),
        P(),
    )
    return jax.shard_map(
        shards, mesh=mesh, in_specs=placed, out_specs=P(None, LAT, LON, None), check_vma=False
    )
```

```python
import jax
import jax.numpy as jnp
import numpy as np
from jax import lax
from jax.experimental import pallas as pl
from jax.experimental.pallas import tpu as pltpu
from jax.sharding import Mesh, PartitionSpec as P

WLAT = 6
WLON = 12
LEVELS = 4
HALF_LAT = WLAT // 2
HALF_LON = WLON // 2
QUARTER = LEVELS * HALF_LAT * HALF_LON
WN = 4 * QUARTER
D = 512
CORNER = (HALF_LAT, HALF_LON, LEVELS, D)
HEADS = 16
HEAD_DIM = D // HEADS
FF = 2048
LANES = 128
PER_GROUP = LANES // HEAD_DIM
GROUPS = HEADS // PER_GROUP
PADDED = 3 * LANES
PIECES = 2
MASKED = -1e30
EPSILON = 1e-05
F32 = jnp.float32
BF16 = jnp.bfloat16
VMEM_LIMIT = 8 * 1024 * 1024
ATTENTION_LIMIT = 32 * 1024 * 1024
STAGE_LIMIT = 48 * 1024 * 1024
TOKENS_LIMIT = 40 * 1024 * 1024

AXES = ("xl", "y", "xh", "z", "c")
SIZES = (2, 8, 2, 8, 2)
LAT = ("xl", "y")
LON = ("xh", "z", "c")


def place(lat, lon):
    return (lat % 16) * 32 + lon % 32


def shifted(dlat, dlon):
    return [(place(a, o), place(a + dlat, o + dlon)) for a in range(16) for o in range(32)]


def mirrored_pairs():
    def at(x, y, z, c):
        return (((x % 2) * 8 + y) * 2 + x // 2) * 16 + z * 2 + c

    return [
        [at(x, y, z, c), at(3 - x, y, z, c)]
        for x in range(2)
        for y in range(8)
        for z in range(8)
        for c in range(2)
    ]


def mirrored():
    return [pair for a, b in mirrored_pairs() for pair in ((a, b), (b, a))]


def to_quarters():
    hot = np.zeros((WN, LEVELS, WLAT, WLON), np.float32)
    place_of = 0
    for i in range(2):
        for j in range(2):
            for row in range(HALF_LAT):
                for col in range(HALF_LON):
                    for lev in range(LEVELS):
                        hot[place_of, lev, i * HALF_LAT + row, j * HALF_LON + col] = 1
                        place_of += 1
    return hot.reshape(WN, WN)


def tags():
    upper = (np.arange(WN) // WLON % WLAT < HALF_LAT).astype(np.float32)
    columns = np.zeros((2, WN, LANES), np.float32)
    columns[0, :, 0], columns[0, :, 1] = upper, 1 - upper
    columns[1, :, 0], columns[1, :, 1] = MASKED * (1 - upper), MASKED * upper
    return columns


def normed(values, gain):
    average = jnp.mean(values, -1, keepdims=True)
    centered = values - average
    variance = jnp.mean(centered * centered, -1, keepdims=True)
    return centered * lax.rsqrt(variance + EPSILON) * gain


def dot(a, b):
    return jnp.dot(a, b, preferred_element_type=F32)


def dot_t(a, b):
    return lax.dot_general(a, b, (((1,), (1,)), ((), ())), preferred_element_type=F32)


def stacked(quarters):
    return jnp.concatenate([q.astype(F32).reshape(QUARTER, D) for q in quarters], 0)


def corner(cells, i, j):
    return cells[i * HALF_LAT : (i + 1) * HALF_LAT, j * HALF_LON : (j + 1) * HALF_LON]


def copy_all(pairs, sems):
    copies = [
        pltpu.make_async_copy(source, target, sems.at[i]) for i, (source, target) in enumerate(pairs)
    ]
    for copy in copies:
        copy.start()
    for copy in copies:
        copy.wait()


def pack_kernel(up_ref, down_ref, proj_ref, own_ref, sems):
    parts = ((up_ref, 0, 64), (down_ref, 64, 128), (proj_ref, 128, 144))
    copy_all([(part, own_ref.at[start:stop]) for part, start, stop in parts], sems)


def bias_kernel(bias_hbm, bias_ref, sems):
    copy_all([(bias_hbm, bias_ref)], sems)


def attention_kernel(
    spot_ref, r0, r2, r1, r3, mine_ref, other_ref, hot_ref, tags_ref, bias_ref, o0, o1, o2, o3
):
    hot = hot_ref[...]
    rows = stacked([r[...] for r in (r0, r1, r2, r3)]).astype(BF16)
    rows = lax.dot_general(hot, rows, (((0,), (0,)), ((), ())), preferred_element_type=F32)
    rows = rows.astype(BF16)
    low_half = spot_ref[0] == 0
    low, high = rows[:, : D // 2], rows[:, D // 2 :]
    ours, theirs = jnp.where(low_half, low, high), jnp.where(low_half, high, low)

    def projected(which):
        columns = slice(which * D, (which + 1) * D)
        mine = mine_ref[:, :, columns].reshape(D // 2, D)
        other = jnp.stack([other_ref[0, :, :, columns], other_ref[1, :, :, columns]], 1)
        return (dot(ours, mine) + dot(theirs, other.reshape(D // 2, D))).astype(BF16)

    queries, keys, values = projected(0), projected(1), projected(2)
    lane_head = lax.broadcasted_iota(jnp.int32, (1, LANES), 1) // HEAD_DIM
    zero = jnp.zeros((), BF16)
    gap = jnp.zeros((PADDED - WN, 2 * LANES), BF16)
    beyond = jnp.full((WN, PADDED - WN), MASKED, F32)
    query_tags = jnp.where(spot_ref[1] == 1, tags_ref[0], zero)
    key_tags = tags_ref[1]
    groups = []
    for group in range(GROUPS):
        lanes = slice(group * LANES, (group + 1) * LANES)
        group_q = jnp.concatenate([queries[:, lanes], query_tags], 1)
        group_k, group_v = keys[:, lanes], values[:, lanes]
        key_rows, value_rows = [], []
        for j in range(PER_GROUP):
            mine = lane_head == j
            key_rows += [jnp.concatenate([jnp.where(mine, group_k, zero), key_tags], 1), gap]
            sums = jnp.broadcast_to(jnp.where(mine, 1.0, 0.0).astype(BF16), (WN, LANES))
            value_rows += [jnp.concatenate([jnp.where(mine, group_v, zero), sums], 1), gap]
        scores = dot_t(group_q, jnp.concatenate(key_rows, 0))
        weights = []
        for j in range(PER_GROUP):
            bias = bias_ref[group * PER_GROUP + j].astype(F32)
            bias = jnp.concatenate([bias, beyond], 1)
            head = scores[:, j * PADDED : (j + 1) * PADDED] * HEAD_DIM ** (-0.5) + bias
            weights.append(jnp.exp(head - jnp.max(head, -1, keepdims=True)).astype(BF16))
        product = dot(jnp.concatenate(weights, 1), jnp.concatenate(value_rows, 0))
        groups.append((product[:, :LANES] / product[:, LANES:]).astype(BF16))
    attended = dot(hot, jnp.concatenate(groups, 1))
    for i, out in enumerate((o0, o1, o2, o3)):
        out[...] = attended[i * QUARTER : (i + 1) * QUARTER].reshape(CORNER).astype(BF16)


def stage_kernel(gathered_ref, wp_ref, wu_ref, wd_ref, sems):
    parts = ((wp_ref, 128, 144), (wu_ref, 0, 64), (wd_ref, 64, 128))
    copy_all([(gathered_ref.at[:, :, start:stop], target) for target, start, stop in parts], sems)


def token_kernel(
    m2, m1, m3, m0, cells_ref, wp, wu, wd, attn_gain_ref, mlp_gain_ref, out_hbm,
    out_ref, sems,
):
    attended = stacked([m[...] for m in (m0, m1, m2, m3)]).astype(BF16)
    cells = stacked([corner(cells_ref, i, j) for i in range(2) for j in range(2)])
    low = dot(attended[:, : D // 2], wp[:, 0].reshape(D // 2, D))
    projected = low + dot(attended[:, D // 2 :], wp[:, 1].reshape(D // 2, D))
    rows = (cells + normed(projected, attn_gain_ref[...])).astype(BF16)
    lowered = None
    step = 16 // PIECES
    units = FF // PIECES
    for i in range(0, 16, step):
        up = wu[i : i + step].reshape(units, D)
        down = wd[i : i + step].reshape(units, D)
        raised = dot_t(rows, up)
        hidden = 0.5 * raised * (1.0 + lax.erf(raised * (0.5**0.5)))
        part = dot(hidden.astype(BF16), down)
        lowered = part if lowered is None else lowered + part
    updated = rows.astype(F32) + normed(lowered, mlp_gain_ref[...])
    run = HALF_LON * LEVELS
    copies = []
    for i in range(2):
        for j in range(2):
            for row in range(HALF_LAT):
                start = (i * 2 + j) * QUARTER + row * run
                piece = updated[start : start + run].reshape(HALF_LON, LEVELS, D)
                out_ref[i * HALF_LAT + row, j * HALF_LON : (j + 1) * HALF_LON] = piece.astype(BF16)
        half = slice(i * HALF_LAT, (i + 1) * HALF_LAT)
        copies.append(pltpu.make_async_copy(out_ref.at[half], out_hbm.at[half], sems.at[i]))
        copies[-1].start()
    for copy in copies:
        copy.wait()


def whole(shape):
    return pl.BlockSpec(shape, lambda i: (0,) * len(shape))


def scalars():
    return pl.BlockSpec(memory_space=pltpu.SMEM)


def held():
    return pl.BlockSpec(memory_space=pltpu.VMEM)


def fetched():
    return pl.BlockSpec(memory_space=pltpu.HBM)


def off_chip(*arrays):
    return [pltpu.with_memory_space_constraint(a, pltpu.HBM) for a in arrays]


def params():
    return pltpu.CompilerParams(vmem_limit_bytes=VMEM_LIMIT)


def packed(up_weight, down_weight, proj_weight):
    return pl.pallas_call(
        pack_kernel,
        in_specs=[fetched()] * 3,
        out_specs=held(),
        out_shape=jax.ShapeDtypeStruct((144, D), BF16),
        scratch_shapes=[pltpu.SemaphoreType.DMA((3,))],
        compiler_params=params(),
        name="pack",
    )(*off_chip(up_weight, down_weight, proj_weight))


def held_bias(bias):
    return pl.pallas_call(
        bias_kernel,
        in_specs=[fetched()],
        out_specs=held(),
        out_shape=jax.ShapeDtypeStruct(bias.shape, BF16),
        scratch_shapes=[pltpu.SemaphoreType.DMA((1,))],
        compiler_params=params(),
        cost_estimate=pl.CostEstimate(flops=0, bytes_accessed=2 * bias.size * 2, transcendentals=0),
        name="bias",
    )(*off_chip(bias))


def attention(spot, quarters, mine, other, bias):
    constants = (jnp.asarray(to_quarters(), BF16), jnp.asarray(tags(), BF16))
    return pl.pallas_call(
        attention_kernel,
        in_specs=[scalars()] + [held()] * (len(quarters) + 5),
        out_specs=[held()] * 4,
        out_shape=[jax.ShapeDtypeStruct(CORNER, BF16)] * 4,
        compiler_params=pltpu.CompilerParams(vmem_limit_bytes=ATTENTION_LIMIT),
        name="attention",
    )(spot, *quarters, mine, other, *constants, bias)


def staged(gathered):
    sizes = [(16, 2, rows, D) for rows in (16, 64, 64)]
    return pl.pallas_call(
        stage_kernel,
        in_specs=[fetched()],
        out_specs=[pl.BlockSpec(memory_space=pltpu.VMEM)] * 3,
        out_shape=[jax.ShapeDtypeStruct(size, BF16) for size in sizes],
        scratch_shapes=[pltpu.SemaphoreType.DMA((3,))],
        compiler_params=pltpu.CompilerParams(vmem_limit_bytes=STAGE_LIMIT),
        cost_estimate=pl.CostEstimate(flops=0, bytes_accessed=2 * 144 * 32 * D * 2, transcendentals=0),
        name="stage",
    )(*off_chip(gathered))


def tokens(quarters, cells, weights, attn_gain, mlp_gain):
    out = (WLAT, WLON, LEVELS, D)
    operands = (*quarters, cells, *weights, attn_gain.reshape(1, D), mlp_gain.reshape(1, D))
    return pl.pallas_call(
        token_kernel,
        in_specs=[held()] * len(operands),
        out_specs=fetched(),
        out_shape=jax.ShapeDtypeStruct(out, BF16),
        scratch_shapes=[pltpu.VMEM(out, BF16), pltpu.SemaphoreType.DMA((2,))],
        compiler_params=pltpu.CompilerParams(vmem_limit_bytes=TOKENS_LIMIT),
        name="tokens",
    )(*operands)


def shards(
    latent, qkv_weight, proj_weight, position_bias, attn_gain, up_weight, down_weight, mlp_gain
):
    own = packed(up_weight, down_weight, proj_weight)
    both = lax.all_gather(own, AXES, axis=0, tiled=False, axis_index_groups=mirrored_pairs())
    gathered = lax.all_gather(both, ("z", "c"), axis=0, tiled=False)
    qkv_weight, _ = lax.optimization_barrier((qkv_weight, both))
    mine = lax.all_gather(qkv_weight, ("z", "c"), axis=0, tiled=False)
    cells = latent.transpose(1, 2, 0, 3)
    cells_after, bias, mine = lax.optimization_barrier((cells, position_bias, mine))
    rolled = [
        lax.ppermute(corner(cells_after, 1, 1), AXES, shifted(1, 1)),
        lax.ppermute(corner(cells_after, 0, 1), AXES, shifted(0, 1)),
        lax.ppermute(corner(cells_after, 1, 0), AXES, shifted(1, 0)),
        corner(cells_after, 0, 0),
    ]
    core = lax.axis_index("c")
    sent = lax.dynamic_index_in_dim(mine.reshape(8, 2, 16, 3 * D), core, 1, keepdims=False)
    theirs = lax.all_gather(lax.ppermute(sent, AXES, mirrored()), "c", axis=0, tiled=False)

    spot = jnp.stack([lax.axis_index("xh"), (lax.axis_index(LAT) == 0).astype(jnp.int32)])
    attended = attention(spot, rolled, mine, theirs, held_bias(bias))
    restored = [
        lax.ppermute(attended[1], AXES, shifted(-1, 0)),
        lax.ppermute(attended[2], AXES, shifted(0, -1)),
        lax.ppermute(attended[0], AXES, shifted(-1, -1)),
        attended[3],
    ]
    return tokens(restored, cells, staged(gathered), attn_gain, mlp_gain).transpose(2, 0, 1, 3)


def solution(mesh):
    mesh = Mesh(mesh.devices.reshape(SIZES), AXES)
    placed = (
        P(None, LAT, LON, None),
        P(LON, None),
        P(LON, None),
        P(),
        P(),
        P(LON, None),
        P(LON, None),
        P(),
    )
    return jax.shard_map(
        shards, mesh=mesh, in_specs=placed, out_specs=P(None, LAT, LON, None), check_vma=False
    )
```

```python
import jax
import jax.numpy as jnp
import numpy as np
from jax import lax
from jax.experimental import pallas as pl
from jax.experimental.pallas import tpu as pltpu
from jax.sharding import Mesh, PartitionSpec as P

WLAT = 6
WLON = 12
LEVELS = 4
HALF_LAT = WLAT // 2
HALF_LON = WLON // 2
QUARTER = LEVELS * HALF_LAT * HALF_LON
WN = 4 * QUARTER
D = 512
CORNER = (HALF_LAT, HALF_LON, LEVELS, D)
HEADS = 16
HEAD_DIM = D // HEADS
FF = 2048
LANES = 128
PER_GROUP = LANES // HEAD_DIM
GROUPS = HEADS // PER_GROUP
PADDED = 3 * LANES
PIECES = 2
MASKED = -1e30
EPSILON = 1e-05
F32 = jnp.float32
BF16 = jnp.bfloat16
VMEM_LIMIT = 8 * 1024 * 1024
ATTENTION_LIMIT = 32 * 1024 * 1024
STAGE_LIMIT = 48 * 1024 * 1024
TOKENS_LIMIT = 40 * 1024 * 1024

AXES = ("xl", "y", "xh", "z", "c")
SIZES = (2, 8, 2, 8, 2)
LAT = ("xl", "y")
LON = ("xh", "z", "c")


def place(lat, lon):
    return (lat % 16) * 32 + lon % 32


def shifted(dlat, dlon):
    return [(place(a, o), place(a + dlat, o + dlon)) for a in range(16) for o in range(32)]


def mirrored_pairs():
    def at(x, y, z, c):
        return (((x % 2) * 8 + y) * 2 + x // 2) * 16 + z * 2 + c

    return [
        [at(x, y, z, c), at(3 - x, y, z, c)]
        for x in range(2)
        for y in range(8)
        for z in range(8)
        for c in range(2)
    ]


def mirrored():
    return [pair for a, b in mirrored_pairs() for pair in ((a, b), (b, a))]


def to_quarters():
    hot = np.zeros((WN, LEVELS, WLAT, WLON), np.float32)
    place_of = 0
    for i in range(2):
        for j in range(2):
            for row in range(HALF_LAT):
                for col in range(HALF_LON):
                    for lev in range(LEVELS):
                        hot[place_of, lev, i * HALF_LAT + row, j * HALF_LON + col] = 1
                        place_of += 1
    return hot.reshape(WN, WN)


def tags():
    upper = (np.arange(WN) // WLON % WLAT < HALF_LAT).astype(np.float32)
    columns = np.zeros((2, WN, LANES), np.float32)
    columns[0, :, 0], columns[0, :, 1] = upper, 1 - upper
    columns[1, :, 0], columns[1, :, 1] = MASKED * (1 - upper), MASKED * upper
    return columns


def normed(values, gain):
    average = jnp.mean(values, -1, keepdims=True)
    centered = values - average
    variance = jnp.mean(centered * centered, -1, keepdims=True)
    return centered * lax.rsqrt(variance + EPSILON) * gain


def dot(a, b):
    return jnp.dot(a, b, preferred_element_type=F32)


def dot_t(a, b):
    return lax.dot_general(a, b, (((1,), (1,)), ((), ())), preferred_element_type=F32)


def stacked(quarters):
    return jnp.concatenate([q.astype(F32).reshape(QUARTER, D) for q in quarters], 0)


def corner(cells, i, j):
    return cells[i * HALF_LAT : (i + 1) * HALF_LAT, j * HALF_LON : (j + 1) * HALF_LON]


def copy_all(pairs, sems):
    copies = [
        pltpu.make_async_copy(source, target, sems.at[i]) for i, (source, target) in enumerate(pairs)
    ]
    for copy in copies:
        copy.start()
    for copy in copies:
        copy.wait()


def pack_kernel(up_ref, down_ref, proj_ref, own_ref, sems):
    parts = ((up_ref, 0, 64), (down_ref, 64, 128), (proj_ref, 128, 144))
    copy_all([(part, own_ref.at[start:stop]) for part, start, stop in parts], sems)


def bias_kernel(bias_hbm, bias_ref, sems):
    copy_all([(bias_hbm.at[: HEADS // 2], bias_ref)], sems)


def attention_kernel(
    spot_ref, r0, r2, r1, r3, mine_ref, other_ref, hot_ref, tags_ref, bias_ref, bias_hbm,
    o0, o1, o2, o3, late_ref, sem,
):
    fetch = pltpu.make_async_copy(bias_hbm.at[HEADS // 2 :], late_ref, sem)
    fetch.start()
    hot = hot_ref[...]
    rows = stacked([r[...] for r in (r0, r1, r2, r3)]).astype(BF16)
    rows = lax.dot_general(hot, rows, (((0,), (0,)), ((), ())), preferred_element_type=F32)
    rows = rows.astype(BF16)
    low_half = spot_ref[0] == 0
    low, high = rows[:, : D // 2], rows[:, D // 2 :]
    ours, theirs = jnp.where(low_half, low, high), jnp.where(low_half, high, low)

    def projected(which):
        columns = slice(which * D, (which + 1) * D)
        mine = mine_ref[:, :, columns].reshape(D // 2, D)
        other = jnp.stack([other_ref[0, :, :, columns], other_ref[1, :, :, columns]], 1)
        return (dot(ours, mine) + dot(theirs, other.reshape(D // 2, D))).astype(BF16)

    queries, keys, values = projected(0), projected(1), projected(2)
    lane_head = lax.broadcasted_iota(jnp.int32, (1, LANES), 1) // HEAD_DIM
    zero = jnp.zeros((), BF16)
    gap = jnp.zeros((PADDED - WN, 2 * LANES), BF16)
    beyond = jnp.full((WN, PADDED - WN), MASKED, F32)
    query_tags = jnp.where(spot_ref[1] == 1, tags_ref[0], zero)
    key_tags = tags_ref[1]
    groups = []
    for group in range(GROUPS):
        if group == GROUPS // 2:
            fetch.wait()
        lanes = slice(group * LANES, (group + 1) * LANES)
        group_q = jnp.concatenate([queries[:, lanes], query_tags], 1)
        group_k, group_v = keys[:, lanes], values[:, lanes]
        key_rows, value_rows = [], []
        for j in range(PER_GROUP):
            mine = lane_head == j
            key_rows += [jnp.concatenate([jnp.where(mine, group_k, zero), key_tags], 1), gap]
            sums = jnp.broadcast_to(jnp.where(mine, 1.0, 0.0).astype(BF16), (WN, LANES))
            value_rows += [jnp.concatenate([jnp.where(mine, group_v, zero), sums], 1), gap]
        scores = dot_t(group_q, jnp.concatenate(key_rows, 0))
        weights = []
        for j in range(PER_GROUP):
            head = group * PER_GROUP + j
            early = head < HEADS // 2
            bias = (bias_ref[head] if early else late_ref[head - HEADS // 2]).astype(F32)
            bias = jnp.concatenate([bias, beyond], 1)
            head = scores[:, j * PADDED : (j + 1) * PADDED] * HEAD_DIM ** (-0.5) + bias
            weights.append(jnp.exp(head - jnp.max(head, -1, keepdims=True)).astype(BF16))
        product = dot(jnp.concatenate(weights, 1), jnp.concatenate(value_rows, 0))
        groups.append((product[:, :LANES] / product[:, LANES:]).astype(BF16))
    attended = dot(hot, jnp.concatenate(groups, 1))
    for i, out in enumerate((o0, o1, o2, o3)):
        out[...] = attended[i * QUARTER : (i + 1) * QUARTER].reshape(CORNER).astype(BF16)


def stage_kernel(gathered_ref, wp_ref, wu_ref, wd_ref, sems):
    parts = ((wp_ref, 128, 144), (wu_ref, 0, 64), (wd_ref, 64, 128))
    copy_all([(gathered_ref.at[:, :, start:stop], target) for target, start, stop in parts], sems)


def token_kernel(
    m2, m3, m1, m0, cells_ref, wp, wu, wd, attn_gain_ref, mlp_gain_ref, out_hbm,
    out_ref, sems,
):
    attended = stacked([m[...] for m in (m0, m1, m2, m3)]).astype(BF16)
    cells = stacked([corner(cells_ref, i, j) for i in range(2) for j in range(2)])
    low = dot(attended[:, : D // 2], wp[:, 0].reshape(D // 2, D))
    projected = low + dot(attended[:, D // 2 :], wp[:, 1].reshape(D // 2, D))
    rows = (cells + normed(projected, attn_gain_ref[...])).astype(BF16)
    lowered = None
    step = 16 // PIECES
    units = FF // PIECES
    for i in range(0, 16, step):
        up = wu[i : i + step].reshape(units, D)
        down = wd[i : i + step].reshape(units, D)
        raised = dot_t(rows, up)
        hidden = 0.5 * raised * (1.0 + lax.erf(raised * (0.5**0.5)))
        part = dot(hidden.astype(BF16), down)
        lowered = part if lowered is None else lowered + part
    updated = rows.astype(F32) + normed(lowered, mlp_gain_ref[...])
    run = HALF_LON * LEVELS
    copies = []
    for i in range(2):
        for j in range(2):
            for row in range(HALF_LAT):
                start = (i * 2 + j) * QUARTER + row * run
                piece = updated[start : start + run].reshape(HALF_LON, LEVELS, D)
                out_ref[i * HALF_LAT + row, j * HALF_LON : (j + 1) * HALF_LON] = piece.astype(BF16)
        half = slice(i * HALF_LAT, (i + 1) * HALF_LAT)
        copies.append(pltpu.make_async_copy(out_ref.at[half], out_hbm.at[half], sems.at[i]))
        copies[-1].start()
    for copy in copies:
        copy.wait()


def whole(shape):
    return pl.BlockSpec(shape, lambda i: (0,) * len(shape))


def scalars():
    return pl.BlockSpec(memory_space=pltpu.SMEM)


def held():
    return pl.BlockSpec(memory_space=pltpu.VMEM)


def fetched():
    return pl.BlockSpec(memory_space=pltpu.HBM)


def off_chip(*arrays):
    return [pltpu.with_memory_space_constraint(a, pltpu.HBM) for a in arrays]


def params():
    return pltpu.CompilerParams(vmem_limit_bytes=VMEM_LIMIT)


def packed(up_weight, down_weight, proj_weight):
    return pl.pallas_call(
        pack_kernel,
        in_specs=[fetched()] * 3,
        out_specs=held(),
        out_shape=jax.ShapeDtypeStruct((144, D), BF16),
        scratch_shapes=[pltpu.SemaphoreType.DMA((3,))],
        compiler_params=params(),
        name="pack",
    )(*off_chip(up_weight, down_weight, proj_weight))


def held_bias(bias):
    return pl.pallas_call(
        bias_kernel,
        in_specs=[fetched()],
        out_specs=held(),
        out_shape=jax.ShapeDtypeStruct((HEADS // 2, WN, WN), BF16),
        scratch_shapes=[pltpu.SemaphoreType.DMA((1,))],
        compiler_params=params(),
        cost_estimate=pl.CostEstimate(flops=0, bytes_accessed=bias.size * 2, transcendentals=0),
        name="bias",
    )(*off_chip(bias))


def attention(spot, quarters, mine, other, early_bias, bias):
    constants = (jnp.asarray(to_quarters(), BF16), jnp.asarray(tags(), BF16))
    return pl.pallas_call(
        attention_kernel,
        in_specs=[scalars()] + [held()] * (len(quarters) + 5) + [fetched()],
        out_specs=[held()] * 4,
        out_shape=[jax.ShapeDtypeStruct(CORNER, BF16)] * 4,
        scratch_shapes=[pltpu.VMEM((HEADS // 2, WN, WN), BF16), pltpu.SemaphoreType.DMA(())],
        compiler_params=pltpu.CompilerParams(vmem_limit_bytes=ATTENTION_LIMIT),
        name="attention",
    )(spot, *quarters, mine, other, *constants, early_bias, *off_chip(bias))


def staged(gathered):
    sizes = [(16, 2, rows, D) for rows in (16, 64, 64)]
    return pl.pallas_call(
        stage_kernel,
        in_specs=[fetched()],
        out_specs=[pl.BlockSpec(memory_space=pltpu.VMEM)] * 3,
        out_shape=[jax.ShapeDtypeStruct(size, BF16) for size in sizes],
        scratch_shapes=[pltpu.SemaphoreType.DMA((3,))],
        compiler_params=pltpu.CompilerParams(vmem_limit_bytes=STAGE_LIMIT),
        cost_estimate=pl.CostEstimate(flops=0, bytes_accessed=2 * 144 * 32 * D * 2, transcendentals=0),
        name="stage",
    )(*off_chip(gathered))


def tokens(quarters, cells, weights, attn_gain, mlp_gain):
    out = (WLAT, WLON, LEVELS, D)
    operands = (*quarters, cells, *weights, attn_gain.reshape(1, D), mlp_gain.reshape(1, D))
    return pl.pallas_call(
        token_kernel,
        in_specs=[held()] * len(operands),
        out_specs=fetched(),
        out_shape=jax.ShapeDtypeStruct(out, BF16),
        scratch_shapes=[pltpu.VMEM(out, BF16), pltpu.SemaphoreType.DMA((2,))],
        compiler_params=pltpu.CompilerParams(vmem_limit_bytes=TOKENS_LIMIT),
        name="tokens",
    )(*operands)


def shards(
    latent, qkv_weight, proj_weight, position_bias, attn_gain, up_weight, down_weight, mlp_gain
):
    own = packed(up_weight, down_weight, proj_weight)
    both = lax.all_gather(own, AXES, axis=0, tiled=False, axis_index_groups=mirrored_pairs())
    gathered = lax.all_gather(both, ("z", "c"), axis=0, tiled=False)
    qkv_weight, _ = lax.optimization_barrier((qkv_weight, both))
    mine = lax.all_gather(qkv_weight, ("z", "c"), axis=0, tiled=False)
    cells = latent.transpose(1, 2, 0, 3)
    cells_after, bias, mine = lax.optimization_barrier((cells, position_bias, mine))
    rolled = [
        lax.ppermute(corner(cells_after, 1, 1), AXES, shifted(1, 1)),
        lax.ppermute(corner(cells_after, 0, 1), AXES, shifted(0, 1)),
        lax.ppermute(corner(cells_after, 1, 0), AXES, shifted(1, 0)),
        corner(cells_after, 0, 0),
    ]
    core = lax.axis_index("c")
    sent = lax.dynamic_index_in_dim(mine.reshape(8, 2, 16, 3 * D), core, 1, keepdims=False)
    theirs = lax.all_gather(lax.ppermute(sent, AXES, mirrored()), "c", axis=0, tiled=False)

    spot = jnp.stack([lax.axis_index("xh"), (lax.axis_index(LAT) == 0).astype(jnp.int32)])
    attended = attention(spot, rolled, mine, theirs, held_bias(bias), bias)
    restored = [
        lax.ppermute(attended[1], AXES, shifted(-1, 0)),
        lax.ppermute(attended[0], AXES, shifted(-1, -1)),
        lax.ppermute(attended[2], AXES, shifted(0, -1)),
        attended[3],
    ]
    return tokens(restored, cells, staged(gathered), attn_gain, mlp_gain).transpose(2, 0, 1, 3)


def solution(mesh):
    mesh = Mesh(mesh.devices.reshape(SIZES), AXES)
    placed = (
        P(None, LAT, LON, None),
        P(LON, None),
        P(LON, None),
        P(),
        P(),
        P(LON, None),
        P(LON, None),
        P(),
    )
    return jax.shard_map(
        shards, mesh=mesh, in_specs=placed, out_specs=P(None, LAT, LON, None), check_vma=False
    )
```
